128 devices in a mesh: scan: 16 (over y, z_hi, core), tx: 4 (over x), ty: 2 (over z_lo).
Axes of the slice: x: 4, y: 4, z: 4 (z_hi: 2, z_lo: 2; z = z_hi * 2 + z_lo), core: 2. Of those that a mesh axis runs over, the one named last changes fastest.
Arguments:
- object_slices: float32 [2, 2, 1024, 512], P(None, None, 'tx', 'ty'), may hold values from -0.9 to 0.9
- probe_modes: float32 [2, 8, 256, 256], replicated, may hold values from -1.2 to 1.2
- corners: int32 [4, 2, 16, 2], P('tx', 'ty', 'scan'), may hold values from 0 to 127, as said below
- measured: float32 [4, 2, 16, 256, 256], P('tx', 'ty', 'scan'), may hold values from 0.2 to 2.5
Outputs:
- updated_object: float32 [2, 2, 1024, 512], P(None, None, 'tx', 'ty')
The draws below stay inside these ranges and needn't reach their ends.
Inputs may be any that keep to these rules, and one draw needn't show every extreme that they name: corners place every window inside its own tile and the 128 pixels below and to the right of it.
All inputs are finite; a program needn't handle non-finite values.
Results may differ from the reference program's by a relative error of at most 0.0001.
Values sent between devices are 32-bit elements; how exact they have to be, the bound alone decides.
No kernel may reach another device: no remote copies, remote signals or barrier semaphores. Data moves between devices by JAX's collectives and lax.ppermute only.
A program may use at most 64 MiB of HBM per device.

```python
import jax
import jax.numpy as jnp
from jax import lax

P_SIZE = 256
MODES = 8
SLICES = 2
ITERS = 1
TILE = 256
SCANS = 16
NY = 1024
NX = 512
N_TX = 4
N_TY = 2


def draw_corners(key, part):
    corner_span = TILE - P_SIZE + P_SIZE // 2
    drawn = jax.random.randint(key, (N_TX, N_TY, SCANS, 2), 0, corner_span, dtype=jnp.int32)
    drawn = drawn.at[0, 0, 0, :].set(0)
    return drawn.at[N_TX - 1, N_TY - 1, SCANS - 1, :].set(corner_span - 1)


def steps_of(own_key, extent, cuts, smallest, high):
    gain = 1.0
    for dim, parts in cuts:
        heights = jax.random.uniform(jax.random.fold_in(jax.random.fold_in(own_key, 6), dim), (parts,), jnp.float32, smallest / len(cuts), high / len(cuts))
        gain = gain * jnp.repeat(jnp.exp(heights), extent[dim] // parts).reshape((-1,) + (1,) * (len(extent) - 1 - dim))
    return gain


def scatter_about(rng, dims, width, limit, cuts=(), kind=jnp.bfloat16):
    gain = steps_of(rng, dims, cuts, -0.22, 0.18) if cuts else 1.0
    array = jax.random.normal(rng, dims, jnp.float32) * width * gain
    return jnp.minimum(jnp.maximum(array, -limit), limit).astype(kind)


def setup_inputs(seed: int = 0) -> dict:
    streams_of = jax.random.split(jax.random.key(seed), 5)
    return {
        "object_slices": scatter_about(streams_of[0], (SLICES, 2, NY, NX), 0.15, 0.9, ((2, 4), (3, 2)), jnp.float32),
        "probe_modes": scatter_about(streams_of[1], (2, MODES, P_SIZE, P_SIZE), 0.2, 1.2, (), jnp.float32),
        "corners": draw_corners(jax.random.fold_in(streams_of[4], 71), 0),
        "measured": jnp.clip(0.2 + 2.3 * jax.random.uniform(streams_of[3], (N_TX, N_TY, SCANS, P_SIZE, P_SIZE), jnp.float32) ** steps_of(streams_of[3], (N_TX, N_TY, SCANS, P_SIZE, P_SIZE), ((0, 4), (1, 2), (2, 16)), -0.2, 0.2), 0.2, 2.5),
    }


fresnel_coef = 0.1
step_size = 4.0


def laplacian(field):
    padded = jnp.pad(field, ((0, 0), (1, 1), (1, 1)))
    return padded[:, :-2, 1:-1] + padded[:, 2:, 1:-1] + padded[:, 1:-1, :-2] + padded[:, 1:-1, 2:] - 4.0 * field


def propagate(field, sign_value):
    lap_once = laplacian(field)
    lap_twice = laplacian(lap_once)
    return field + (sign_value * fresnel_coef * 1j) * lap_once - (0.5 * fresnel_coef ** 2) * lap_twice


def position_terms(padded_obj, probe_complex, row_start, col_start, measured_one):
    zero_index = jnp.zeros((), jnp.int32)
    window = lax.dynamic_slice(padded_obj, (zero_index, row_start, col_start), (SLICES, P_SIZE, P_SIZE))
    transmit = 1.0 + window
    stored = []
    field_now = probe_complex
    exit_wave = field_now
    for layer_index in range(SLICES):
        stored.append(field_now)
        exit_wave = field_now * transmit[layer_index]
        if layer_index + 1 < SLICES:
            field_now = propagate(exit_wave, 1.0)
    far_field = jnp.fft.fft2(exit_wave, norm="ortho")
    misfit = jnp.sum(jnp.real(far_field) ** 2 + jnp.imag(far_field) ** 2, axis=0) - measured_one
    backward = jnp.fft.ifft2(2.0 * misfit * far_field, norm="ortho")
    gradients = [None] * SLICES
    for layer_index in reversed(range(SLICES)):
        field_now = stored[layer_index]
        grad_term = jnp.sum(jnp.conj(field_now) * backward, axis=0)
        lighting = jnp.sum(jnp.real(field_now) ** 2 + jnp.imag(field_now) ** 2, axis=0)
        gradients[layer_index] = jnp.stack([jnp.real(grad_term), jnp.imag(grad_term), lighting])
        if layer_index > 0:
            backward = propagate(jnp.conj(transmit[layer_index]) * backward, -1.0)
    return jnp.stack(gradients)


def reference(object_slices, probe_modes, corners, measured):
    rim_width = P_SIZE // 2
    probe_complex = lax.complex(probe_modes[0], probe_modes[1])
    row_base = (jnp.arange(N_TX, dtype=jnp.int32) * TILE)[:, None, None]
    col_base = (jnp.arange(N_TY, dtype=jnp.int32) * TILE)[None, :, None]
    row_starts = (row_base + corners[..., 0]).reshape(-1).astype(jnp.int32)
    col_starts = (col_base + corners[..., 1]).reshape(-1).astype(jnp.int32)
    measured_flat = measured.reshape(-1, P_SIZE, P_SIZE)
    current = object_slices
    for iteration in range(ITERS):
        padded_obj = jnp.pad(lax.complex(current[:, 0], current[:, 1]), ((0, 0), (0, rim_width), (0, rim_width)))

        def visit(accumulated, item):
            row_start, col_start, measured_one = item
            grad_terms = position_terms(padded_obj, probe_complex, row_start, col_start, measured_one)
            zero_index = jnp.zeros((), jnp.int32)
            starts = (zero_index, zero_index, row_start, col_start)
            updated = lax.dynamic_slice(accumulated, starts, grad_terms.shape) + grad_terms
            return lax.dynamic_update_slice(accumulated, updated, starts), None

        initial = jnp.zeros((SLICES, 3, NY + rim_width, NX + rim_width), jnp.float32)
        accumulated = lax.scan(visit, initial, (row_starts, col_starts, measured_flat))[0]
        summed = accumulated[:, :, :NY, :NX]
        current = current - step_size * summed[:, :2] / (summed[:, 2:3] + 1.0)
    return current
```

```python
import functools
import math

import jax
import jax.numpy as jnp
import numpy as np
from jax import lax
from jax.experimental import pallas as pl
from jax.experimental.pallas import tpu as pltpu
from jax.sharding import PartitionSpec as P

fresnel_coef = 0.1
step_size = 4.0
SIDE = 256
HALF = 128
LAYERS = 2
SCANS = 16
STEPS = 32
f32 = jnp.float32
bf16 = jnp.bfloat16


def real_right(table):
    return np.block([[table.real, table.imag], [-table.imag, table.real]])


def real_left(table):
    return np.block([[table.real, -table.imag], [table.imag, table.real]])


def two_parts(table):
    high = table.astype(np.float32).astype(bf16)
    low = (table - high.astype(np.float64)).astype(np.float32).astype(bf16)
    return np.stack([high, low])


def make_tables():
    half = np.arange(HALF)
    col_even = np.exp(-2j * np.pi * np.outer(half, half) / HALF) / 16
    col_odd = np.exp(-2j * np.pi * np.outer(half, 2 * half + 1) / SIDE) / 16
    place = 16 * (half % 8) + half // 8
    row_even = np.exp(-2j * np.pi * np.outer(half, place) / HALF) / 16
    row_odd = np.exp(-2j * np.pi * np.outer(half, 2 * place + 1) / SIDE) / 16
    right = [col_even, col_odd, col_even.conj().T, col_odd.conj().T]
    left = [row_even, row_odd, row_even.conj().T, row_odd.conj().T]
    right = np.stack([two_parts(real_right(t)) for t in right])
    left = np.stack([two_parts(real_left(t)) for t in left])
    order = np.zeros((SIDE, SIDE), np.float32)
    order[2 * half, half] = 1.0
    order[2 * half + 1, half + HALF] = 1.0
    return right, left, order.astype(bf16)


def split(value):
    high = value.astype(bf16)
    return high, (value - high.astype(f32)).astype(bf16)


def mul(first, second):
    return jnp.dot(first, second, preferred_element_type=f32)


def right_dot(value, table, which):
    high, low = split(value)
    return (
        mul(high, table[which, 0]) + mul(low, table[which, 0]) + mul(high, table[which, 1])
    )


def left_dot(table, which, value):
    high, low = split(value)
    return (
        mul(table[which, 0], high) + mul(table[which, 0], low) + mul(table[which, 1], high)
    )


def neighbours(v):
    column = lax.broadcasted_iota(jnp.int32, v.shape, 2)
    sub = lax.broadcasted_iota(jnp.int32, (1, 8, SIDE), 1)
    left = jnp.where(column == 0, 0.0, pltpu.roll(v, 1, 2))
    right = jnp.where(column == SIDE - 1, 0.0, pltpu.roll(v, SIDE - 1, 2))
    first = jnp.where(sub == 0, 0.0, pltpu.roll(v[-1:], 1, 1))
    last = jnp.where(sub == 7, 0.0, pltpu.roll(v[:1], 7, 1))
    up = jnp.concatenate([first, v[:-1]], axis=0)
    down = jnp.concatenate([v[1:], last], axis=0)
    return (left + right) + (up + down)


def propagate(re, im, sign):
    damping = 0.5 * fresnel_coef**2
    turn = sign * fresnel_coef
    q_re = 4.0 * damping * re - turn * im - damping * neighbours(re)
    q_im = 4.0 * damping * im + turn * re - damping * neighbours(im)
    return (re - 4.0 * q_re) + neighbours(q_re), (im - 4.0 * q_im) + neighbours(q_im)


def load_rows(ref, lead):
    pick = lambda h, t: ref[lead + (h, pl.ds(t, 8, stride=STEPS), slice(None))]
    return jnp.stack(
        [jnp.concatenate([pick(0, t), pick(1, t)], axis=1) for t in range(STEPS)], axis=0
    )


def store_rows(ref, value):
    for h in range(2):
        for t in range(STEPS):
            ref[h, pl.ds(t, 8, stride=STEPS), :] = value[t, :, h * HALF : (h + 1) * HALF]


def probe_copies(probe_ref, probe, sems, m):
    return [
        pltpu.make_async_copy(
            probe_ref.at[p, m, :, pl.ds(h * HALF, HALF)], probe.at[p, m, h], sems.at[p, m, h]
        )
        for p in range(2)
        for h in range(2)
    ]


def wave_kernel(
    corner_ref,
    own_ref,
    below_ref,
    right_ref,
    diag_ref,
    probe_ref,
    measured_ref,
    col_tab,
    row_tab,
    order_ref,
    out_ref,
    light_ref,
    hold,
    trans,
    wave,
    far,
    misfit,
    total,
    probe_light,
    probe,
    sems,
):
    r, c = corner_ref[0], corner_ref[1]
    modes = probe_ref.shape[1]
    for m in range(modes):
        for copy in probe_copies(probe_ref, probe, sems, m):
            copy.start()
    rows = lax.broadcasted_iota(jnp.int32, (SIDE, SIDE), 0)
    cols = lax.broadcasted_iota(jnp.int32, (SIDE, SIDE), 1)
    top = rows[:HALF] < r
    near = cols[:, :HALF] < c
    back_r = lax.rem(SIDE - r, SIDE)
    back_c = lax.rem(SIDE - c, SIDE)
    for s in range(LAYERS):
        for p in range(2):
            left = jnp.where(near, right_ref[s, p], own_ref[s, p, :, :HALF])
            whole = jnp.concatenate([left, own_ref[s, p, :, HALF:]], axis=1)
            lower = jnp.concatenate(
                [
                    jnp.where(near[:HALF], diag_ref[s, p], below_ref[s, p, :, :HALF]),
                    below_ref[s, p, :, HALF:],
                ],
                axis=1,
            )
            whole = jnp.concatenate([jnp.where(top, lower, whole[:HALF]), whole[HALF:]], axis=0)
            whole = pltpu.roll(pltpu.roll(whole, back_c, 1), back_r, 0)
            hold[0] = whole[:, :HALF]
            hold[1] = whole[:, HALF:]
            view = load_rows(hold, ())
            trans[s, p] = view + 1.0 if p == 0 else view

    inten = measured_ref[...]
    high, low = split(inten)
    rest = (inten - high.astype(f32) - low.astype(f32)).astype(bf16)
    order = order_ref[...]
    misfit[...] = -(mul(high, order) + mul(low, order) + mul(rest, order))
    total[...] = jnp.zeros_like(total)
    probe_light[...] = jnp.zeros_like(probe_light)

    def forward(m, carry):
        for copy in probe_copies(probe_ref, probe, sems, m):
            copy.wait()
        p_re, p_im = load_rows(probe, (0, m)), load_rows(probe, (1, m))
        probe_light[...] += p_re * p_re + p_im * p_im
        t_re, t_im = trans[0, 0], trans[0, 1]
        w_re, w_im = propagate(p_re * t_re - p_im * t_im, p_re * t_im + p_im * t_re, 1.0)
        wave[0, m] = w_re
        wave[1, m] = w_im
        total[2] += w_re * w_re + w_im * w_im
        t_re, t_im = trans[1, 0], trans[1, 1]
        x_re = (w_re * t_re - w_im * t_im).reshape(SIDE, SIDE)
        x_im = (w_re * t_im + w_im * t_re).reshape(SIDE, SIDE)
        even = jnp.concatenate(
            [x_re[:, :HALF] + x_re[:, HALF:], x_im[:, :HALF] + x_im[:, HALF:]], axis=1
        )
        odd = jnp.concatenate(
            [x_re[:, :HALF] - x_re[:, HALF:], x_im[:, :HALF] - x_im[:, HALF:]], axis=1
        )
        even = right_dot(even, col_tab, 0)
        odd = right_dot(odd, col_tab, 1)
        y_re = jnp.concatenate([even[:, :HALF], odd[:, :HALF]], axis=1).reshape(16, 2, 8, SIDE)
        y_im = jnp.concatenate([even[:, HALF:], odd[:, HALF:]], axis=1).reshape(16, 2, 8, SIDE)
        pick = lambda e: jnp.concatenate([y_re[:, e], y_im[:, e]], axis=0).reshape(SIDE, SIDE)
        first = left_dot(row_tab, 0, pick(0))
        second = left_dot(row_tab, 1, pick(1))
        upper, lower = first + second, first - second
        far[m, 0] = upper
        far[m, 1] = lower
        misfit[:HALF] += upper[:HALF] * upper[:HALF] + upper[HALF:] * upper[HALF:]
        misfit[HALF:] += lower[:HALF] * lower[:HALF] + lower[HALF:] * lower[HALF:]
        return carry

    lax.fori_loop(0, modes, forward, 0)
    misfit[...] = 2.0 * misfit[...]

    def backward(m, carry):
        twice = lambda a: jnp.concatenate([a, a], axis=0)
        upper = twice(misfit[:HALF]) * far[m, 0]
        lower = twice(misfit[HALF:]) * far[m, 1]
        even = left_dot(row_tab, 2, upper + lower)
        odd = left_dot(row_tab, 3, upper - lower)
        join = lambda lanes: jnp.concatenate(
            [
                jnp.concatenate([even[:HALF, lanes], even[HALF:, lanes]], axis=1),
                jnp.concatenate([odd[:HALF, lanes], odd[HALF:, lanes]], axis=1),
            ],
            axis=0,
        )
        first = right_dot(join(slice(0, HALF)), col_tab, 2)
        second = right_dot(join(slice(HALF, SIDE)), col_tab, 3)
        plus, minus = first + second, first - second

        def weave(a):
            a = a.reshape(2, 16, 8, SIDE)
            return jnp.stack([a[0], a[1]], axis=1).reshape(STEPS, 8, SIDE)

        b_re = weave(jnp.concatenate([plus[:, :HALF], minus[:, :HALF]], axis=1))
        b_im = weave(jnp.concatenate([plus[:, HALF:], minus[:, HALF:]], axis=1))
        w_re, w_im = wave[0, m], wave[1, m]
        total[0] += w_re * b_re + w_im * b_im
        total[1] += w_re * b_im - w_im * b_re
        t_re, t_im = trans[1, 0], trans[1, 1]
        d_re, d_im = propagate(t_re * b_re + t_im * b_im, t_re * b_im - t_im * b_re, -1.0)
        p_re, p_im = load_rows(probe, (0, m)), load_rows(probe, (1, m))
        total[3] += p_re * d_re + p_im * d_im
        total[4] += p_re * d_im - p_im * d_re
        return carry

    lax.fori_loop(0, modes, backward, 0)

    for k in range(5):
        store_rows(hold, total[k])
        whole = jnp.concatenate([hold[0], hold[1]], axis=1)
        moved = pltpu.roll(pltpu.roll(whole, c, 1), r, 0).reshape(2, 16, 8, SIDE)
        out_ref[:, k, 0] = moved[0]
        out_ref[:, k, 1] = moved[1]
    store_rows(hold, probe_light[...])
    for h in range(2):
        for half in range(2):
            light_ref[half * SIDE : (half + 1) * SIDE, h * HALF : (h + 1) * HALF] = hold[h]


def run_wave(corner, own, below, right, diag, probe, measured):
    right_table, left_table, order = make_tables()
    modes = probe.shape[1]
    vmem = pl.BlockSpec(memory_space=pltpu.VMEM)
    field = (STEPS, 8, SIDE)
    return pl.pallas_call(
        wave_kernel,
        out_shape=(
            jax.ShapeDtypeStruct((SCANS, 5, 2, 8, SIDE), f32),
            jax.ShapeDtypeStruct((2 * SIDE, SIDE), f32),
        ),
        in_specs=[pl.BlockSpec(memory_space=pltpu.SMEM)]
        + [vmem] * 4
        + [pl.BlockSpec(memory_space=pl.ANY)]
        + [vmem] * 4,
        out_specs=(vmem, vmem),
        scratch_shapes=[
            pltpu.VMEM((2, SIDE, HALF), f32),
            pltpu.VMEM((LAYERS, 2) + field, f32),
            pltpu.VMEM((2, modes) + field, f32),
            pltpu.VMEM((modes, 2, SIDE, SIDE), f32),
            pltpu.VMEM((SIDE, SIDE), f32),
            pltpu.VMEM((5,) + field, f32),
            pltpu.VMEM(field, f32),
            pltpu.VMEM((2, modes, 2, SIDE, HALF), f32),
            pltpu.SemaphoreType.DMA((2, modes, 2)),
        ],
        compiler_params=pltpu.CompilerParams(vmem_limit_bytes=48 * 1024 * 1024),
        name="wave",
    )(
        corner,
        own,
        below,
        right,
        diag,
        probe,
        measured,
        jnp.asarray(right_table),
        jnp.asarray(left_table),
        jnp.asarray(order),
    )


def sum_kernel(me_ref, corners_ref, parts_ref, light_ref, own_ref, right_ref, below_ref, diag_ref):
    me = me_ref[0]
    own_ref[...] = jnp.zeros_like(own_ref)
    right_ref[...] = jnp.zeros_like(right_ref)
    below_ref[...] = jnp.zeros_like(below_ref)
    diag_ref[...] = jnp.zeros_like(diag_ref)
    sub = lax.broadcasted_iota(jnp.int32, (2, 8, SIDE), 1)
    side = lax.broadcasted_iota(jnp.int32, (2, 8, SIDE), 0)
    cols = lax.broadcasted_iota(jnp.int32, (2, 8, SIDE), 2)
    rows = HALF * side + 8 * me + sub
    for j in range(SCANS):
        r, c = corners_ref[j, 0], corners_ref[j, 1]
        lights = []
        for h in range(2):
            start = lax.rem(HALF * h + 8 * me + SIDE - r, SIDE)
            base = pl.multiple_of((start // 8) * 8, 8)
            block = light_ref[pl.ds(base, 16), :]
            block = pltpu.roll(block, lax.rem(16 - (start - base), 16), 0)[:8]
            lights.append(pltpu.roll(block, c, 1)[None])
        light = jnp.concatenate(lights, axis=0)
        inside_row, inside_col = rows >= r, cols >= c
        for k in range(6):
            value = parts_ref[j, k] if k < 5 else light
            here = jnp.where(inside_row, value, 0.0)
            there = (value - here)[0]
            own_ref[k] += jnp.where(inside_col, here, 0.0)
            right_ref[k] += jnp.where(inside_col, 0.0, here)[:, :, :HALF]
            below_ref[k] += jnp.where(inside_col[0], there, 0.0)
            diag_ref[k] += jnp.where(inside_col[0], 0.0, there)[:, :HALF]


def run_sum(me, corners, parts, light):
    smem = pl.BlockSpec(memory_space=pltpu.SMEM)
    vmem = pl.BlockSpec(memory_space=pltpu.VMEM)
    return pl.pallas_call(
        sum_kernel,
        out_shape=(
            jax.ShapeDtypeStruct((6, 2, 8, SIDE), f32),
            jax.ShapeDtypeStruct((6, 2, 8, HALF), f32),
            jax.ShapeDtypeStruct((6, 8, SIDE), f32),
            jax.ShapeDtypeStruct((6, 8, HALF), f32),
        ),
        in_specs=[smem, smem, vmem, vmem],
        out_specs=(vmem,) * 4,
        name="sum",
    )(me, corners, parts, light)


def update_kernel(me_ref, object_ref, own_ref, right_ref, below_ref, diag_ref, out_ref):
    me = me_ref[0]
    sums = []
    for k in range(6):
        near = own_ref[k, :, :, :HALF] + right_ref[k]
        whole = jnp.concatenate([near, own_ref[k, :, :, HALF:]], axis=2)
        low = jnp.concatenate(
            [below_ref[k, :, :HALF] + diag_ref[k], below_ref[k, :, HALF:]], axis=1
        )
        sums.append([whole[0] + low, whole[1]])
    for s in range(LAYERS):
        base = 3 * (1 - s)
        for h in range(2):
            scale = step_size / (sums[base + 2][h] + 1.0)
            start = pl.multiple_of(HALF * h + 8 * me, 8)
            for p in range(2):
                out_ref[s, p, h] = (
                    object_ref[s, p, pl.ds(start, 8), :] - scale * sums[base + p][h]
                )


def run_update(me, current, own, right, below, diag):
    smem = pl.BlockSpec(memory_space=pltpu.SMEM)
    vmem = pl.BlockSpec(memory_space=pltpu.VMEM)
    return pl.pallas_call(
        update_kernel,
        out_shape=jax.ShapeDtypeStruct((LAYERS, 2, 2, 8, SIDE), f32),
        in_specs=[smem] + [vmem] * 5,
        out_specs=vmem,
        name="update",
    )(me, current, own, right, below, diag)


def place_kernel(me_ref, *refs):
    blocks, out_ref = refs[:-1], refs[-1]
    me = me_ref[0]
    y, z, core = me // 4, lax.rem(me // 2, 2), lax.rem(me, 2)
    count = 0
    for ref in blocks:
        for b in range(ref.shape[0]):
            dc, dy, dz = count // 8, (count // 2) % 4, count % 2
            i = lax.rem(y + 4 - dy, 4) * 4 + lax.rem(z + dz, 2) * 2 + lax.rem(core + dc, 2)
            for h in range(2):
                start = pl.multiple_of(HALF * h + 8 * i, 8)
                out_ref[:, :, pl.ds(start, 8), :] = ref[b, :, :, h]
            count += 1


def run_place(me, blocks):
    vmem = pl.BlockSpec(memory_space=pltpu.VMEM)
    return pl.pallas_call(
        place_kernel,
        out_shape=jax.ShapeDtypeStruct((LAYERS, 2, SIDE, SIDE), f32),
        in_specs=[pl.BlockSpec(memory_space=pltpu.SMEM)] + [vmem] * len(blocks),
        out_specs=vmem,
        name="place",
    )(me, *blocks)


def shift(array, axis, by):
    count = lax.axis_size(axis)
    pairs = [(i, i + by) for i in range(count) if 0 <= i + by < count]
    return lax.ppermute(array, axis, pairs)


def shift_both(array, by):
    n_x, n_y = lax.axis_size("tx"), lax.axis_size("ty")
    pairs = [
        (a * n_y + b, (a + by) * n_y + b + by)
        for a in range(n_x)
        for b in range(n_y)
        if 0 <= a + by < n_x and 0 <= b + by < n_y
    ]
    return lax.ppermute(array, ("tx", "ty"), pairs)


def along_scan(array, dy, dz, dc):
    pairs = []
    for i in range(SCANS):
        y, z, core = i // 4, (i // 2) % 2, i % 2
        pairs.append((i, ((y + dy) % 4) * 4 + ((z + dz) % 2) * 2 + (core + dc) % 2))
    return lax.ppermute(array, "scan", pairs)


def on_device(object_slices, probe_modes, corners, measured):
    me = lax.axis_index("scan").astype(jnp.int32).reshape(1)
    corner = corners.reshape(2)
    below = shift(object_slices[:, :, :HALF, :], "tx", -1)
    right = shift(object_slices[:, :, :, :HALF], "ty", -1)
    diag = shift_both(object_slices[:, :, :HALF, :HALF], -1)
    told = jnp.broadcast_to(jnp.pad(corner, (0, 126))[None, None], (SCANS, 1, 128))
    all_corners = lax.all_to_all(told, "scan", 0, 0)[:, 0, :2]

    parts, light = run_wave(
        corner, object_slices, below, right, diag, probe_modes, measured.reshape(SIDE, SIDE)
    )
    parts = lax.all_to_all(parts, "scan", 0, 0)
    own, to_right, to_below, to_diag = run_sum(me, all_corners, parts, light)
    to_right = shift(to_right, "ty", 1)
    to_below = shift(to_below, "tx", 1)
    to_diag = shift_both(to_diag, 1)
    mine = run_update(me, object_slices, own, to_right, to_below, to_diag)[None]
    pair = jnp.concatenate([mine, along_scan(mine, 0, 1, 0)], axis=0)
    ring = [pair] + [along_scan(pair, dy, 0, 0) for dy in (1, 2, 3)]
    ring = jnp.concatenate(ring, axis=0)
    other = along_scan(ring, 0, 0, 1)
    return run_place(me, [ring, other])


def solution(mesh):
    placed = (
        P(None, None, "tx", "ty"),
        P(),
        P("tx", "ty", "scan", None),
        P("tx", "ty", "scan", None, None),
    )
    return jax.shard_map(
        on_device, mesh=mesh, in_specs=placed, out_specs=P(None, None, "tx", "ty"), check_vma=False
    )
```

```python
import functools
import math

import jax
import jax.numpy as jnp
import numpy as np
from jax import lax
from jax.experimental import pallas as pl
from jax.experimental.pallas import tpu as pltpu
from jax.sharding import PartitionSpec as P

fresnel_coef = 0.1
step_size = 4.0
SIDE = 256
HALF = 128
LAYERS = 2
SCANS = 16
ROWS = 32
PAD = 8
f32 = jnp.float32
bf16 = jnp.bfloat16


def real_right(table):
    return np.block([[table.real, table.imag], [-table.imag, table.real]])


def real_left(table):
    return np.block([[table.real, -table.imag], [table.imag, table.real]])


def stacked(table, axis):
    high = table.astype(np.float32).astype(bf16)
    low = (table - high.astype(np.float64)).astype(np.float32).astype(bf16)
    return np.concatenate([high, high, low], axis=axis)


def make_tables():
    half = np.arange(HALF)
    col_even = np.exp(-2j * np.pi * np.outer(half, half) / HALF) / 16
    col_odd = np.exp(-2j * np.pi * np.outer(half, 2 * half + 1) / SIDE) / 16
    row_even, row_odd = col_even.T, col_odd.T
    right = [col_even, col_odd, col_even.conj().T, col_odd.conj().T]
    left = [row_even, row_odd, row_even.conj().T, row_odd.conj().T]
    right = np.stack([stacked(real_right(t), 0) for t in right])
    left = np.stack([stacked(real_left(t), 1) for t in left])
    order = np.zeros((SIDE, SIDE), np.float32)
    order[2 * half, half] = 1.0
    order[2 * half + 1, half + HALF] = 1.0
    return right, left, order.astype(bf16)


def split(value):
    high = value.astype(bf16)
    return high, (value - high.astype(f32)).astype(bf16)


def mul(first, second):
    return jnp.dot(first, second, preferred_element_type=f32)


def put(ref, lead, rows, value):
    high, low = split(value)
    ref[lead + (0, rows)] = high
    ref[lead + (1, rows)] = low


def right_dot(ref, side, table, which):
    high, low = ref[side, 0], ref[side, 1]
    return mul(jnp.concatenate([high, low, high], axis=1), table[which])


def left_dot(table, which, ref, side):
    high, low = ref[side, 0], ref[side, 1]
    return mul(table[which], jnp.concatenate([high, low, high], axis=0))


def neighbours(ref, p, start):
    rows = lambda by: pl.ds(start + PAD + by, ROWS)
    low, high = ref[p, 0, rows(0)], ref[p, 1, rows(0)]
    lane = lax.broadcasted_iota(jnp.int32, low.shape, 1)
    first, last = lane == 0, lane == HALF - 1
    low_up, high_up = pltpu.roll(low, 1, 1), pltpu.roll(high, 1, 1)
    low_down, high_down = pltpu.roll(low, HALF - 1, 1), pltpu.roll(high, HALF - 1, 1)
    low_sum = jnp.where(first, 0.0, low_up) + jnp.where(last, high_down, low_down)
    high_sum = jnp.where(first, low_up, high_up) + jnp.where(last, 0.0, high_down)
    return (
        low_sum + (ref[p, 0, rows(-1)] + ref[p, 0, rows(1)]),
        high_sum + (ref[p, 1, rows(-1)] + ref[p, 1, rows(1)]),
    )


damping = 0.5 * fresnel_coef**2


def turn_rows(source, target, start, sign):
    turn = sign * fresnel_coef
    rows = pl.ds(start + PAD, ROWS)
    near_re, near_im = neighbours(source, 0, start), neighbours(source, 1, start)
    for h in range(2):
        re, im = source[0, h, rows], source[1, h, rows]
        target[0, h, rows] = 4.0 * damping * re - turn * im - damping * near_re[h]
        target[1, h, rows] = 4.0 * damping * im + turn * re - damping * near_im[h]


def end_rows(source, target, start):
    rows = pl.ds(start + PAD, ROWS)
    near = [neighbours(target, p, start) for p in range(2)]
    return [
        [source[p, h, rows] - 4.0 * target[p, h, rows] + near[p][h] for p in range(2)]
        for h in range(2)
    ]


def probe_copies(probe_ref, probe, sems, m):
    return [
        pltpu.make_async_copy(
            probe_ref.at[p, m, :, pl.ds(h * HALF, HALF)], probe.at[p, m, h], sems.at[p, m, h]
        )
        for p in range(2)
        for h in range(2)
    ]


def arrange(value, order, axis):
    high, low = split(value)
    rest = (value - high.astype(f32) - low.astype(f32)).astype(bf16)
    if axis == 1:
        return mul(high, order) + mul(low, order) + mul(rest, order)
    turned = order.T
    return mul(turned, high) + mul(turned, low) + mul(turned, rest)


def wave_kernel(
    corner_ref,
    below_ref,
    right_ref,
    diag_ref,
    other_below_ref,
    other_right_ref,
    other_diag_ref,
    own_far,
    probe_ref,
    measured_far,
    col_far,
    row_far,
    order_far,
    out_ref,
    own_ref,
    measured_ref,
    col_tab,
    row_tab,
    order_ref,
    hold,
    trans,
    wave,
    far,
    misfit,
    total,
    probe,
    sems,
    more_sems,
    field,
    turned,
    across,
    along,
):
    r, c = corner_ref[0], corner_ref[1]
    modes = probe_ref.shape[1]
    own_copy = pltpu.make_async_copy(own_far, own_ref, more_sems.at[0])
    later = [
        pltpu.make_async_copy(source, target, more_sems.at[n + 1])
        for n, (source, target) in enumerate(
            [
                (order_far, order_ref),
                (measured_far, measured_ref),
                (col_far, col_tab),
                (row_far, row_tab),
            ]
        )
    ]
    own_copy.start()
    for copy in probe_copies(probe_ref, probe, sems, 0):
        copy.start()
    for copy in later:
        copy.start()
    for m in range(1, modes):
        for copy in probe_copies(probe_ref, probe, sems, m):
            copy.start()
    rows = lax.broadcasted_iota(jnp.int32, (SIDE, SIDE), 0)
    cols = lax.broadcasted_iota(jnp.int32, (SIDE, SIDE), 1)
    top = rows[:HALF] < r
    near = cols[:, :HALF] < c
    back_c = lax.rem(SIDE - c, SIDE)
    own_copy.wait()
    for s in range(LAYERS):
        for p in range(2):
            held = corner_ref[2] == p
            right = jnp.where(held, right_ref[s], other_right_ref[s])
            below = jnp.where(held, below_ref[s], other_below_ref[s])
            diag = jnp.where(held, diag_ref[s], other_diag_ref[s])
            left = jnp.where(near, right, own_ref[s, p, :, :HALF])
            whole = jnp.concatenate([left, own_ref[s, p, :, HALF:]], axis=1)
            lower = jnp.concatenate(
                [jnp.where(near[:HALF], diag, below[:, :HALF]), below[:, HALF:]], axis=1
            )
            whole = jnp.concatenate([jnp.where(top, lower, whole[:HALF]), whole[HALF:]], axis=0)
            whole = pltpu.roll(whole, back_c, 1)
            for half in range(2):
                hold[0, half * SIDE : (half + 1) * SIDE] = whole[:, :HALF]
                hold[1, half * SIDE : (half + 1) * SIDE] = whole[:, HALF:]
            for h in range(2):
                view = hold[h, pl.ds(r, SIDE)]
                trans[s, p, h] = view + 1.0 if p == 0 else view

    for copy in later:
        copy.wait()
    order = order_ref[...]
    misfit[...] = -arrange(arrange(measured_ref[...], order, 1), order, 0)
    total[...] = jnp.zeros_like(total)
    field[...] = jnp.zeros_like(field)
    turned[...] = jnp.zeros_like(turned)
    starts = range(0, SIDE, ROWS)

    def forward(m, carry):
        for copy in probe_copies(probe_ref, probe, sems, m):
            copy.wait()
        for start in starts:
            rows, inner = pl.ds(start, ROWS), pl.ds(start + PAD, ROWS)
            for h in range(2):
                p_re, p_im = probe[0, m, h, rows], probe[1, m, h, rows]
                t_re, t_im = trans[0, 0, h, rows], trans[0, 1, h, rows]
                field[0, h, inner] = p_re * t_re - p_im * t_im
                field[1, h, inner] = p_re * t_im + p_im * t_re
        for start in starts:
            turn_rows(field, turned, start, 1.0)
        for start in starts:
            rows = pl.ds(start, ROWS)
            x = []
            for h, (w_re, w_im) in enumerate(end_rows(field, turned, start)):
                wave[0, m, h, rows] = w_re
                wave[1, m, h, rows] = w_im
                total[2, h, rows] += w_re * w_re + w_im * w_im
                t_re, t_im = trans[1, 0, h, rows], trans[1, 1, h, rows]
                x.append(
                    jnp.concatenate([w_re * t_re - w_im * t_im, w_re * t_im + w_im * t_re], axis=1)
                )
            put(across, (0,), rows, x[0] + x[1])
            put(across, (1,), rows, x[0] - x[1])
        even = right_dot(across, 0, col_tab, 0)
        odd = right_dot(across, 1, col_tab, 1)
        for start in range(0, HALF, ROWS):
            for q in range(2):
                lanes = slice(HALF * q, HALF * (q + 1))
                above, under = [
                    jnp.concatenate([even[part, lanes], odd[part, lanes]], axis=1)
                    for part in (slice(start, start + ROWS), slice(start + HALF, start + HALF + ROWS))
                ]
                rows = pl.ds(HALF * q + start, ROWS)
                put(along, (0,), rows, above + under)
                put(along, (1,), rows, above - under)
        for e in range(2):
            found = left_dot(row_tab, e, along, e)
            far[m, e] = found
            misfit[pl.ds(HALF * e, HALF)] += found[:HALF] * found[:HALF] + found[HALF:] * found[HALF:]
        return carry

    lax.fori_loop(0, modes, forward, 0)
    misfit[...] = 2.0 * misfit[...]

    def backward(m, carry):
        for e in range(2):
            for start in range(0, HALF, ROWS):
                scale = misfit[pl.ds(HALF * e + start, ROWS)]
                for q in range(2):
                    rows = pl.ds(HALF * q + start, ROWS)
                    put(along, (e,), rows, scale * far[m, e, rows])
        even = left_dot(row_tab, 2, along, 0)
        odd = left_dot(row_tab, 3, along, 1)
        for start in range(0, HALF, ROWS):
            re, im = slice(start, start + ROWS), slice(HALF + start, HALF + start + ROWS)
            for n in range(2):
                f_re = even[re] + odd[re] if n == 0 else even[re] - odd[re]
                f_im = even[im] + odd[im] if n == 0 else even[im] - odd[im]
                rows = pl.ds(HALF * n + start, ROWS)
                for q in range(2):
                    lanes = slice(HALF * q, HALF * (q + 1))
                    put(
                        across,
                        (q,),
                        rows,
                        jnp.concatenate([f_re[:, lanes], f_im[:, lanes]], axis=1),
                    )
        first = right_dot(across, 0, col_tab, 2)
        second = right_dot(across, 1, col_tab, 3)
        for start in starts:
            rows, inner = pl.ds(start, ROWS), pl.ds(start + PAD, ROWS)
            part = slice(start, start + ROWS)
            for h in range(2):
                both = first[part] + second[part] if h == 0 else first[part] - second[part]
                b_re, b_im = both[:, :HALF], both[:, HALF:]
                w_re, w_im = wave[0, m, h, rows], wave[1, m, h, rows]
                total[0, h, rows] += w_re * b_re + w_im * b_im
                total[1, h, rows] += w_re * b_im - w_im * b_re
                t_re, t_im = trans[1, 0, h, rows], trans[1, 1, h, rows]
                field[0, h, inner] = t_re * b_re + t_im * b_im
                field[1, h, inner] = t_re * b_im - t_im * b_re
        for start in starts:
            turn_rows(field, turned, start, -1.0)
        for start in starts:
            rows = pl.ds(start, ROWS)
            for h, (d_re, d_im) in enumerate(end_rows(field, turned, start)):
                p_re, p_im = probe[0, m, h, rows], probe[1, m, h, rows]
                total[3, h, rows] += p_re * d_re + p_im * d_im
                total[4, h, rows] += p_re * d_im - p_im * d_re
        return carry

    lax.fori_loop(0, modes, backward, 0)

    for k in range(5):
        for h in range(2):
            hold[h, :SIDE] = total[k, h]
            hold[h, SIDE:] = total[k, h]
        for n in range(SIDE // 8):
            rows = pl.ds(SIDE - r + 8 * n, 8)
            block = jnp.concatenate([hold[0, rows], hold[1, rows]], axis=1)
            out_ref[n % 16, 2 * k + n // 16] = pltpu.roll(block, c, 1)
    lane = lax.broadcasted_iota(jnp.int32, (8, SIDE), 1)
    mark = jnp.where(lane == 0, r, c).astype(f32)
    for i in range(SCANS):
        out_ref[i, 10] = mark


def glow_kernel(probe_ref, light_ref):
    @pl.when(pl.program_id(0) == 0)
    def _():
        light_ref[...] = jnp.zeros_like(light_ref)

    light = probe_ref[0, 0] * probe_ref[0, 0] + probe_ref[1, 0] * probe_ref[1, 0]
    light_ref[:SIDE] += light
    light_ref[SIDE:] += light


def run_glow(probe):
    modes = probe.shape[1]
    return pl.pallas_call(
        glow_kernel,
        grid=(modes,),
        out_shape=jax.ShapeDtypeStruct((2 * SIDE, SIDE), f32),
        in_specs=[pl.BlockSpec((2, 1, SIDE, SIDE), lambda m: (0, m, 0, 0))],
        out_specs=pl.BlockSpec((2 * SIDE, SIDE), lambda m: (0, 0)),
        compiler_params=pltpu.CompilerParams(vmem_limit_bytes=60 * 1024 * 1024),
        cost_estimate=pl.CostEstimate(
            flops=4 * modes * SIDE * SIDE, bytes_accessed=8 * modes * SIDE * SIDE, transcendentals=0
        ),
        name="glow",
    )(probe)


def cut_kernel(me_ref, object_ref, below_ref, right_ref, diag_ref, sems):
    core = lax.rem(me_ref[0], 2)
    copies = []
    for s in range(LAYERS):
        plane = object_ref.at[s, core]
        near = pl.ds(0, HALF)
        for n, (source, target) in enumerate(
            [
                (plane.at[near, :], below_ref.at[s]),
                (plane.at[:, near], right_ref.at[s]),
                (plane.at[near, near], diag_ref.at[s]),
            ]
        ):
            copies.append(pltpu.make_async_copy(source, target, sems.at[s, n]))
    for copy in copies:
        copy.start()
    for copy in copies:
        copy.wait()


def run_cut(me, current):
    vmem = pl.BlockSpec(memory_space=pltpu.VMEM)
    return pl.pallas_call(
        cut_kernel,
        out_shape=(
            jax.ShapeDtypeStruct((LAYERS, HALF, SIDE), f32),
            jax.ShapeDtypeStruct((LAYERS, SIDE, HALF), f32),
            jax.ShapeDtypeStruct((LAYERS, HALF, HALF), f32),
        ),
        in_specs=[pl.BlockSpec(memory_space=pltpu.SMEM), pl.BlockSpec(memory_space=pl.ANY)],
        out_specs=(vmem,) * 3,
        scratch_shapes=[pltpu.SemaphoreType.DMA((LAYERS, 3))],
        compiler_params=pltpu.CompilerParams(vmem_limit_bytes=60 * 1024 * 1024),
        name="cut",
    )(me, current)


def run_wave(corner, own, rims, probe, measured):
    right_table, left_table, order = make_tables()
    modes = probe.shape[1]
    vmem = pl.BlockSpec(memory_space=pltpu.VMEM)
    field = (2, SIDE, HALF)
    wide = (2, 2, SIDE + 2 * PAD, HALF)
    return pl.pallas_call(
        wave_kernel,
        out_shape=jax.ShapeDtypeStruct((SCANS, 11, 8, SIDE), f32),
        in_specs=[pl.BlockSpec(memory_space=pltpu.SMEM)]
        + [vmem] * 6
        + [pl.BlockSpec(memory_space=pl.ANY)] * 6,
        out_specs=vmem,
        scratch_shapes=[
            pltpu.VMEM((LAYERS, 2, SIDE, SIDE), f32),
            pltpu.VMEM((SIDE, SIDE), f32),
            pltpu.VMEM((4, 3 * SIDE, SIDE), bf16),
            pltpu.VMEM((4, SIDE, 3 * SIDE), bf16),
            pltpu.VMEM((SIDE, SIDE), bf16),
            pltpu.VMEM((2, 2 * SIDE, HALF), f32),
            pltpu.VMEM((LAYERS, 2) + field, f32),
            pltpu.VMEM((2, modes) + field, f32),
            pltpu.VMEM((modes, 2, SIDE, SIDE), f32),
            pltpu.VMEM((SIDE, SIDE), f32),
            pltpu.VMEM((5,) + field, f32),
            pltpu.VMEM((2, modes, 2, SIDE, HALF), f32),
            pltpu.SemaphoreType.DMA((2, modes, 2)),
            pltpu.SemaphoreType.DMA((5,)),
            pltpu.VMEM(wide, f32),
            pltpu.VMEM(wide, f32),
            pltpu.VMEM((2, 2, SIDE, SIDE), bf16),
            pltpu.VMEM((2, 2, SIDE, SIDE), bf16),
        ],
        compiler_params=pltpu.CompilerParams(vmem_limit_bytes=60 * 1024 * 1024),
        name="wave",
    )(
        corner,
        *rims,
        own,
        probe,
        measured,
        jnp.asarray(right_table),
        jnp.asarray(left_table),
        jnp.asarray(order),
    )


def sum_kernel(
    me_ref, parts_ref, light_ref, own_ref, right_ref, below_ref, diag_ref, marks_ref, sem
):
    me = me_ref[0]
    copy = pltpu.make_async_copy(parts_ref.at[:, 10, :, pl.ds(0, HALF)], marks_ref, sem)
    copy.start()
    own_ref[...] = jnp.zeros_like(own_ref)
    right_ref[...] = jnp.zeros_like(right_ref)
    below_ref[...] = jnp.zeros_like(below_ref)
    diag_ref[...] = jnp.zeros_like(diag_ref)
    sub = lax.broadcasted_iota(jnp.int32, (2, 8, SIDE), 1)
    side = lax.broadcasted_iota(jnp.int32, (2, 8, SIDE), 0)
    cols = lax.broadcasted_iota(jnp.int32, (2, 8, SIDE), 2)
    rows = HALF * side + 8 * me + sub
    copy.wait()
    for j in range(SCANS):
        r = marks_ref[j, 0, 0].astype(jnp.int32)
        c = marks_ref[j, 0, 1].astype(jnp.int32)
        lights = []
        for h in range(2):
            start = lax.rem(HALF * h + 8 * me + SIDE - r, SIDE)
            base = pl.multiple_of((start // 8) * 8, 8)
            block = light_ref[pl.ds(base, 16), :]
            block = pltpu.roll(block, lax.rem(16 - (start - base), 16), 0)[:8]
            lights.append(pltpu.roll(block, c, 1)[None])
        light = jnp.concatenate(lights, axis=0)
        inside_row, inside_col = rows >= r, cols >= c
        for k in range(6):
            value = parts_ref[j, 2 * k : 2 * k + 2] if k < 5 else light
            here = jnp.where(inside_row, value, 0.0)
            there = (value - here)[0]
            own_ref[k] += jnp.where(inside_col, here, 0.0)
            right_ref[k] += jnp.where(inside_col, 0.0, here)[:, :, :HALF]
            below_ref[k] += jnp.where(inside_col[0], there, 0.0)
            diag_ref[k] += jnp.where(inside_col[0], 0.0, there)[:, :HALF]


def run_sum(me, parts, light):
    smem = pl.BlockSpec(memory_space=pltpu.SMEM)
    vmem = pl.BlockSpec(memory_space=pltpu.VMEM)
    return pl.pallas_call(
        sum_kernel,
        out_shape=(
            jax.ShapeDtypeStruct((6, 2, 8, SIDE), f32),
            jax.ShapeDtypeStruct((6, 2, 8, HALF), f32),
            jax.ShapeDtypeStruct((6, 8, SIDE), f32),
            jax.ShapeDtypeStruct((6, 8, HALF), f32),
        ),
        in_specs=[smem, vmem, vmem],
        out_specs=(vmem,) * 4,
        scratch_shapes=[pltpu.SMEM((SCANS, 8, HALF), f32), pltpu.SemaphoreType.DMA],
        compiler_params=pltpu.CompilerParams(vmem_limit_bytes=8 * 1024 * 1024),
        name="sum",
    )(me, parts, light)


def update_kernel(me_ref, object_ref, own_ref, right_ref, below_ref, diag_ref, out_ref):
    me = me_ref[0]
    sums = []
    for k in range(6):
        near = own_ref[k, :, :, :HALF] + right_ref[k]
        whole = jnp.concatenate([near, own_ref[k, :, :, HALF:]], axis=2)
        low = jnp.concatenate(
            [below_ref[k, :, :HALF] + diag_ref[k], below_ref[k, :, HALF:]], axis=1
        )
        sums.append([whole[0] + low, whole[1]])
    for s in range(LAYERS):
        base = 3 * (1 - s)
        for h in range(2):
            scale = step_size / (sums[base + 2][h] + 1.0)
            start = pl.multiple_of(HALF * h + 8 * me, 8)
            for p in range(2):
                out_ref[s, p, h] = (
                    object_ref[s, p, pl.ds(start, 8), :] - scale * sums[base + p][h]
                )


def run_update(me, current, own, right, below, diag):
    smem = pl.BlockSpec(memory_space=pltpu.SMEM)
    vmem = pl.BlockSpec(memory_space=pltpu.VMEM)
    return pl.pallas_call(
        update_kernel,
        out_shape=jax.ShapeDtypeStruct((LAYERS, 2, 2, 8, SIDE), f32),
        in_specs=[smem] + [vmem] * 5,
        out_specs=vmem,
        compiler_params=pltpu.CompilerParams(vmem_limit_bytes=4 * 1024 * 1024),
        name="update",
    )(me, current, own, right, below, diag)


def place_kernel(me_ref, *refs):
    blocks, out_ref = refs[:-1], refs[-1]
    me = me_ref[0]
    y, z, core = me // 4, lax.rem(me // 2, 2), lax.rem(me, 2)
    count = 0
    for ref in blocks:
        for b in range(ref.shape[0]):
            dc, dy, dz = count // 8, (count // 2) % 4, count % 2
            i = lax.rem(y + 4 - dy, 4) * 4 + lax.rem(z + dz, 2) * 2 + lax.rem(core + dc, 2)
            for h in range(2):
                start = pl.multiple_of(HALF * h + 8 * i, 8)
                out_ref[:, :, pl.ds(start, 8), :] = ref[b, :, :, h]
            count += 1


def run_place(me, blocks):
    vmem = pl.BlockSpec(memory_space=pltpu.VMEM)
    return pl.pallas_call(
        place_kernel,
        out_shape=jax.ShapeDtypeStruct((LAYERS, 2, SIDE, SIDE), f32),
        in_specs=[pl.BlockSpec(memory_space=pltpu.SMEM)] + [vmem] * len(blocks),
        out_specs=vmem,
        compiler_params=pltpu.CompilerParams(vmem_limit_bytes=8 * 1024 * 1024),
        name="place",
    )(me, *blocks)


def shift(array, axis, by):
    count = lax.axis_size(axis)
    pairs = [(i, i + by) for i in range(count) if 0 <= i + by < count]
    return lax.ppermute(array, axis, pairs)


def shift_both(array, by):
    n_x, n_y = lax.axis_size("tx"), lax.axis_size("ty")
    pairs = [
        (a * n_y + b, (a + by) * n_y + b + by)
        for a in range(n_x)
        for b in range(n_y)
        if 0 <= a + by < n_x and 0 <= b + by < n_y
    ]
    return lax.ppermute(array, ("tx", "ty"), pairs)


def along_scan(array, dy, dz, dc):
    pairs = []
    for i in range(SCANS):
        y, z, core = i // 4, (i // 2) % 2, i % 2
        pairs.append((i, ((y + dy) % 4) * 4 + ((z + dz) % 2) * 2 + (core + dc) % 2))
    return lax.ppermute(array, "scan", pairs)


def on_device(object_slices, probe_modes, corners, measured):
    me = lax.axis_index("scan").astype(jnp.int32).reshape(1)
    corner = corners.reshape(2)
    rims = run_cut(me, object_slices)
    rims = (shift(rims[0], "tx", -1), shift(rims[1], "ty", -1), shift_both(rims[2], -1))
    light = run_glow(probe_modes)
    others = tuple(along_scan(rim, 0, 0, 1) for rim in rims)

    parts = run_wave(
        jnp.concatenate([corner, me % 2]),
        object_slices,
        rims + others,
        probe_modes,
        measured.reshape(SIDE, SIDE),
    )
    parts = lax.all_to_all(parts, "scan", 0, 0)
    own, to_right, to_below, to_diag = run_sum(me, parts, light)
    to_right = shift(to_right, "ty", 1)
    to_below = shift(to_below, "tx", 1)
    to_diag = shift_both(to_diag, 1)
    mine = run_update(me, object_slices, own, to_right, to_below, to_diag)[None]
    pair = jnp.concatenate([mine, along_scan(mine, 0, 1, 0)], axis=0)
    ring = [pair] + [along_scan(pair, dy, 0, 0) for dy in (1, 2, 3)]
    ring = jnp.concatenate(ring, axis=0)
    other = along_scan(ring, 0, 0, 1)
    return run_place(me, [ring, other])


def solution(mesh):
    placed = (
        P(None, None, "tx", "ty"),
        P(),
        P("tx", "ty", "scan", None),
        P("tx", "ty", "scan", None, None),
    )
    return jax.shard_map(
        on_device, mesh=mesh, in_specs=placed, out_specs=P(None, None, "tx", "ty"), check_vma=False
    )
```

```python
import functools
import math

import jax
import jax.numpy as jnp
import numpy as np
from jax import lax
from jax.experimental import pallas as pl
from jax.experimental.pallas import tpu as pltpu
from jax.sharding import PartitionSpec as P

fresnel_coef = 0.1
step_size = 4.0
SIDE = 256
HALF = 128
LAYERS = 2
SCANS = 16
ROWS = 32
PAD = 8
f32 = jnp.float32
bf16 = jnp.bfloat16


def real_right(table):
    return np.block([[table.real, table.imag], [-table.imag, table.real]])


def real_left(table):
    return np.block([[table.real, -table.imag], [table.imag, table.real]])


def stacked(table, axis):
    high = table.astype(np.float32).astype(bf16)
    low = (table - high.astype(np.float64)).astype(np.float32).astype(bf16)
    return np.concatenate([high, high, low], axis=axis)


def make_tables():
    half = np.arange(HALF)
    col_even = np.exp(-2j * np.pi * np.outer(half, half) / HALF) / 16
    col_odd = np.exp(-2j * np.pi * np.outer(half, 2 * half + 1) / SIDE) / 16
    row_even, row_odd = col_even.T, col_odd.T
    right = [col_even, col_odd, col_even.conj().T, col_odd.conj().T]
    left = [row_even, row_odd, row_even.conj().T, row_odd.conj().T]
    right = np.stack([stacked(real_right(t), 0) for t in right])
    left = np.stack([stacked(real_left(t), 1) for t in left])
    return right, left


def split(value):
    high = value.astype(bf16)
    return high, (value - high.astype(f32)).astype(bf16)


def mul(first, second):
    return jnp.dot(first, second, preferred_element_type=f32)


def put(ref, lead, rows, value):
    high, low = split(value)
    ref[lead + (0, rows)] = high
    ref[lead + (1, rows)] = low


def right_dot(ref, side, table, which):
    high, low = ref[side, 0], ref[side, 1]
    return mul(jnp.concatenate([high, low, high], axis=1), table[which])


def left_dot(table, which, ref, side):
    high, low = ref[side, 0], ref[side, 1]
    return mul(table[which], jnp.concatenate([high, low, high], axis=0))


def neighbours(ref, p, start):
    rows = lambda by: pl.ds(start + PAD + by, ROWS)
    low, high = ref[p, 0, rows(0)], ref[p, 1, rows(0)]
    lane = lax.broadcasted_iota(jnp.int32, low.shape, 1)
    first, last = lane == 0, lane == HALF - 1
    low_up, high_up = pltpu.roll(low, 1, 1), pltpu.roll(high, 1, 1)
    low_down, high_down = pltpu.roll(low, HALF - 1, 1), pltpu.roll(high, HALF - 1, 1)
    low_sum = jnp.where(first, 0.0, low_up) + jnp.where(last, high_down, low_down)
    high_sum = jnp.where(first, low_up, high_up) + jnp.where(last, 0.0, high_down)
    return (
        low_sum + (ref[p, 0, rows(-1)] + ref[p, 0, rows(1)]),
        high_sum + (ref[p, 1, rows(-1)] + ref[p, 1, rows(1)]),
    )


damping = 0.5 * fresnel_coef**2


def turn_rows(source, target, start, sign):
    turn = sign * fresnel_coef
    rows = pl.ds(start + PAD, ROWS)
    near_re, near_im = neighbours(source, 0, start), neighbours(source, 1, start)
    for h in range(2):
        re, im = source[0, h, rows], source[1, h, rows]
        target[0, h, rows] = 4.0 * damping * re - turn * im - damping * near_re[h]
        target[1, h, rows] = 4.0 * damping * im + turn * re - damping * near_im[h]


def end_rows(source, target, start):
    rows = pl.ds(start + PAD, ROWS)
    near = [neighbours(target, p, start) for p in range(2)]
    return [
        [source[p, h, rows] - 4.0 * target[p, h, rows] + near[p][h] for p in range(2)]
        for h in range(2)
    ]


def probe_copies(probe_ref, probe, sems, m):
    return [
        pltpu.make_async_copy(
            probe_ref.at[p, m, :, pl.ds(h * HALF, HALF)], probe.at[p, m, h], sems.at[p, m, h]
        )
        for p in range(2)
        for h in range(2)
    ]


def wave_kernel(
    corner_ref,
    me_ref,
    below_ref,
    right_ref,
    diag_ref,
    other_below_ref,
    other_right_ref,
    other_diag_ref,
    own_far,
    probe_ref,
    measured_far,
    col_far,
    row_far,
    out_ref,
    own_ref,
    measured_ref,
    col_tab,
    row_tab,
    hold,
    trans,
    wave,
    far,
    misfit,
    total,
    probe,
    sems,
    more_sems,
    field,
    turned,
    across_0,
    across_1,
    along_0,
    along_1,
):
    across, along = (across_0, across_1), (along_0, along_1)
    r, c = corner_ref[0], corner_ref[1]
    modes = probe_ref.shape[1]
    own_copy = pltpu.make_async_copy(own_far, own_ref, more_sems.at[0])
    later = [
        pltpu.make_async_copy(source, target, more_sems.at[n + 1])
        for n, (source, target) in enumerate(
            [
                (col_far, col_tab),
                (row_far, row_tab),
                (measured_far, measured_ref),
            ]
        )
    ]
    own_copy.start()
    for copy in probe_copies(probe_ref, probe, sems, 0):
        copy.start()
    for copy in later:
        copy.start()
    for m in range(1, modes):
        for copy in probe_copies(probe_ref, probe, sems, m):
            copy.start()
    rows = lax.broadcasted_iota(jnp.int32, (SIDE, SIDE), 0)
    cols = lax.broadcasted_iota(jnp.int32, (SIDE, SIDE), 1)
    top = rows[:HALF] < r
    near = cols[:, :HALF] < c
    back_c = lax.rem(SIDE - c, SIDE)
    own_copy.wait()
    for s in range(LAYERS):
        for p in range(2):
            held = lax.rem(me_ref[0], 2) == p
            right = jnp.where(held, right_ref[s], other_right_ref[s])
            below = jnp.where(held, below_ref[s], other_below_ref[s])
            diag = jnp.where(held, diag_ref[s], other_diag_ref[s])
            left = jnp.where(near, right, own_ref[s, p, :, :HALF])
            whole = jnp.concatenate([left, own_ref[s, p, :, HALF:]], axis=1)
            lower = jnp.concatenate(
                [jnp.where(near[:HALF], diag, below[:, :HALF]), below[:, HALF:]], axis=1
            )
            whole = jnp.concatenate([jnp.where(top, lower, whole[:HALF]), whole[HALF:]], axis=0)
            whole = pltpu.roll(whole, back_c, 1)
            for half in range(2):
                hold[0, half * SIDE : (half + 1) * SIDE] = whole[:, :HALF]
                hold[1, half * SIDE : (half + 1) * SIDE] = whole[:, HALF:]
            for h in range(2):
                view = hold[h, pl.ds(r, SIDE)]
                trans[s, p, h] = view + 1.0 if p == 0 else view

    misfit[...] = jnp.zeros_like(misfit)
    total[...] = jnp.zeros_like(total)
    field[...] = jnp.zeros_like(field)
    turned[...] = jnp.zeros_like(turned)
    far[modes] = jnp.zeros_like(far[modes])
    starts = range(0, SIDE, ROWS)

    def enter(m, side):
        held = jnp.minimum(m, modes - 1)
        for start in starts:
            rows, inner = pl.ds(start, ROWS), pl.ds(start + PAD, ROWS)
            for h in range(2):
                p_re, p_im = probe[0, held, h, rows], probe[1, held, h, rows]
                t_re, t_im = trans[0, 0, h, rows], trans[0, 1, h, rows]
                field[side, 0, h, inner] = p_re * t_re - p_im * t_im
                field[side, 1, h, inner] = p_re * t_im + p_im * t_re
            yield
        for start in starts:
            turn_rows(field.at[side], turned, start, 1.0)
            yield
        for start in starts:
            rows = pl.ds(start, ROWS)
            x = []
            for h, (w_re, w_im) in enumerate(end_rows(field.at[side], turned, start)):
                wave[0, m, h, rows] = w_re
                wave[1, m, h, rows] = w_im
                t_re, t_im = trans[1, 0, h, rows], trans[1, 1, h, rows]
                x.append(
                    jnp.concatenate([w_re * t_re - w_im * t_im, w_re * t_im + w_im * t_re], axis=1)
                )
            put(across[side], (0,), rows, x[0] + x[1])
            put(across[side], (1,), rows, x[0] - x[1])
            yield

    def transform(m, side):
        even = right_dot(across[side], 0, col_tab, 0)
        yield
        odd = right_dot(across[side], 1, col_tab, 1)
        yield
        for start in range(0, HALF, ROWS):
            for q in range(2):
                lanes = slice(HALF * q, HALF * (q + 1))
                above, under = [
                    jnp.concatenate([even[part, lanes], odd[part, lanes]], axis=1)
                    for part in (slice(start, start + ROWS), slice(start + HALF, start + HALF + ROWS))
                ]
                rows = pl.ds(HALF * q + start, ROWS)
                put(along[side], (0,), rows, above + under)
                put(along[side], (1,), rows, above - under)
            yield
        for e in range(2):
            found = left_dot(row_tab, e, along[side], e)
            yield
            for start in range(0, HALF, ROWS):
                re, im = found[start : start + ROWS], found[HALF + start : HALF + start + ROWS]
                far[m, e, pl.ds(start, ROWS)] = re
                far[m, e, pl.ds(HALF + start, ROWS)] = im
                misfit[pl.ds(HALF * e + start, ROWS)] += re * re + im * im
                yield
        for start in starts:
            rows = pl.ds(start, ROWS)
            for h in range(2):
                w_re, w_im = wave[0, m, h, rows], wave[1, m, h, rows]
                total[2, h, rows] += w_re * w_re + w_im * w_im
            yield

    def beside(*parts):
        live = list(parts)
        while live:
            live = [part for part in live if next(part, live) is not live]

    for m in range(modes):
        for copy in probe_copies(probe_ref, probe, sems, m):
            copy.wait()
    beside(enter(0, 0))
    for copy in later:
        copy.wait()

    def forward(j, carry):
        beside(transform(2 * j, 0), enter(2 * j + 1, 1))
        beside(transform(2 * j + 1, 1), enter(2 * j + 2, 0))
        return carry

    lax.fori_loop(0, modes // 2, forward, 0)
    misfit[...] = 2.0 * (misfit[...] - measured_ref[...])

    def restore(m, side):
        for e in range(2):
            for start in range(0, HALF, ROWS):
                scale = misfit[pl.ds(HALF * e + start, ROWS)]
                for q in range(2):
                    rows = pl.ds(HALF * q + start, ROWS)
                    put(along[side], (e,), rows, scale * far[m, e, rows])
                yield
        even = left_dot(row_tab, 2, along[side], 0)
        yield
        odd = left_dot(row_tab, 3, along[side], 1)
        yield
        for start in range(0, HALF, ROWS):
            re, im = slice(start, start + ROWS), slice(HALF + start, HALF + start + ROWS)
            for n in range(2):
                f_re = even[re] + odd[re] if n == 0 else even[re] - odd[re]
                f_im = even[im] + odd[im] if n == 0 else even[im] - odd[im]
                rows = pl.ds(HALF * n + start, ROWS)
                for q in range(2):
                    lanes = slice(HALF * q, HALF * (q + 1))
                    put(
                        across[side],
                        (q,),
                        rows,
                        jnp.concatenate([f_re[:, lanes], f_im[:, lanes]], axis=1),
                    )
            yield
        first = right_dot(across[side], 0, col_tab, 2)
        yield
        second = right_dot(across[side], 1, col_tab, 3)
        yield
        for start in starts:
            rows, inner = pl.ds(start, ROWS), pl.ds(start + PAD, ROWS)
            part = slice(start, start + ROWS)
            for h in range(2):
                both = first[part] + second[part] if h == 0 else first[part] - second[part]
                b_re, b_im = both[:, :HALF], both[:, HALF:]
                w_re, w_im = wave[0, m, h, rows], wave[1, m, h, rows]
                total[0, h, rows] += w_re * b_re + w_im * b_im
                total[1, h, rows] += w_re * b_im - w_im * b_re
                t_re, t_im = trans[1, 0, h, rows], trans[1, 1, h, rows]
                field[side, 0, h, inner] = t_re * b_re + t_im * b_im
                field[side, 1, h, inner] = t_re * b_im - t_im * b_re
            yield

    def leave(m, side):
        for start in starts:
            turn_rows(field.at[side], turned, start, -1.0)
            yield
        for start in starts:
            rows = pl.ds(start, ROWS)
            for h, (d_re, d_im) in enumerate(end_rows(field.at[side], turned, start)):
                p_re, p_im = probe[0, m, h, rows], probe[1, m, h, rows]
                total[3, h, rows] += p_re * d_re + p_im * d_im
                total[4, h, rows] += p_re * d_im - p_im * d_re
            yield

    beside(restore(0, 0))

    def backward(j, carry):
        beside(restore(2 * j + 1, 1), leave(2 * j, 0))
        beside(restore(2 * j + 2, 0), leave(2 * j + 1, 1))
        return carry

    lax.fori_loop(0, modes // 2, backward, 0)

    for k in range(5):
        for h in range(2):
            hold[h, :SIDE] = total[k, h]
            hold[h, SIDE:] = total[k, h]
        for n in range(SIDE // 8):
            rows = pl.ds(SIDE - r + 8 * n, 8)
            block = jnp.concatenate([hold[0, rows], hold[1, rows]], axis=1)
            out_ref[n % 16, 2 * k + n // 16] = pltpu.roll(block, c, 1)
    lane = lax.broadcasted_iota(jnp.int32, (8, SIDE), 1)
    mark = jnp.where(lane == 0, r, c).astype(f32)
    for i in range(SCANS):
        out_ref[i, 10] = mark


def glow_kernel(probe_ref, measured_ref, light_ref, expected_ref):
    @pl.when(pl.program_id(0) == 0)
    def _():
        light_ref[...] = jnp.zeros_like(light_ref)
        row = lax.broadcasted_iota(jnp.int32, (SIDE, SIDE), 0)
        col = lax.broadcasted_iota(jnp.int32, (SIDE, SIDE), 1)
        place = lambda k: jnp.where(k < HALF, 2 * k, 2 * (k - HALF) + 1)
        by_col = (row == place(col)).astype(f32).astype(bf16)
        by_row = (col == place(row)).astype(f32).astype(bf16)
        value = measured_ref[...]
        for left in (False, True):
            high, low = split(value)
            rest = (value - high.astype(f32) - low.astype(f32)).astype(bf16)
            if left:
                value = mul(by_row, high) + mul(by_row, low) + mul(by_row, rest)
            else:
                value = mul(high, by_col) + mul(low, by_col) + mul(rest, by_col)
        expected_ref[...] = value

    light = probe_ref[0, 0] * probe_ref[0, 0] + probe_ref[1, 0] * probe_ref[1, 0]
    light_ref[:SIDE] += light
    light_ref[SIDE:] += light


def run_glow(probe, measured):
    modes = probe.shape[1]
    return pl.pallas_call(
        glow_kernel,
        grid=(modes,),
        out_shape=(
            jax.ShapeDtypeStruct((2 * SIDE, SIDE), f32),
            jax.ShapeDtypeStruct((SIDE, SIDE), f32),
        ),
        in_specs=[
            pl.BlockSpec((2, 1, SIDE, SIDE), lambda m: (0, m, 0, 0)),
            pl.BlockSpec((SIDE, SIDE), lambda m: (0, 0)),
        ],
        out_specs=(
            pl.BlockSpec((2 * SIDE, SIDE), lambda m: (0, 0)),
            pl.BlockSpec((SIDE, SIDE), lambda m: (0, 0)),
        ),
        compiler_params=pltpu.CompilerParams(vmem_limit_bytes=60 * 1024 * 1024),
        cost_estimate=pl.CostEstimate(
            flops=4 * modes * SIDE * SIDE, bytes_accessed=8 * modes * SIDE * SIDE, transcendentals=0
        ),
        name="glow",
    )(probe, measured)


def cut_kernel(me_ref, object_ref, below_ref, right_ref, diag_ref, sems):
    core = lax.rem(me_ref[0], 2)
    copies = []
    for s in range(LAYERS):
        plane = object_ref.at[s, core]
        near = pl.ds(0, HALF)
        for n, (source, target) in enumerate(
            [
                (plane.at[near, :], below_ref.at[s]),
                (plane.at[:, near], right_ref.at[s]),
                (plane.at[near, near], diag_ref.at[s]),
            ]
        ):
            copies.append(pltpu.make_async_copy(source, target, sems.at[s, n]))
    for copy in copies:
        copy.start()
    for copy in copies:
        copy.wait()


def run_cut(me, current):
    vmem = pl.BlockSpec(memory_space=pltpu.VMEM)
    return pl.pallas_call(
        cut_kernel,
        out_shape=(
            jax.ShapeDtypeStruct((LAYERS, HALF, SIDE), f32),
            jax.ShapeDtypeStruct((LAYERS, SIDE, HALF), f32),
            jax.ShapeDtypeStruct((LAYERS, HALF, HALF), f32),
        ),
        in_specs=[pl.BlockSpec(memory_space=pltpu.SMEM), pl.BlockSpec(memory_space=pl.ANY)],
        out_specs=(vmem,) * 3,
        scratch_shapes=[pltpu.SemaphoreType.DMA((LAYERS, 3))],
        compiler_params=pltpu.CompilerParams(vmem_limit_bytes=60 * 1024 * 1024),
        name="cut",
    )(me, current)


def run_wave(corner, me, own, rims, probe, measured):
    right_table, left_table = make_tables()
    modes = probe.shape[1]
    vmem = pl.BlockSpec(memory_space=pltpu.VMEM)
    field = (2, SIDE, HALF)
    wide = (2, 2, SIDE + 2 * PAD, HALF)
    return pl.pallas_call(
        wave_kernel,
        out_shape=jax.ShapeDtypeStruct((SCANS, 11, 8, SIDE), f32),
        in_specs=[pl.BlockSpec(memory_space=pltpu.SMEM)] * 2
        + [vmem] * 6
        + [pl.BlockSpec(memory_space=pl.ANY)] * 5,
        out_specs=vmem,
        scratch_shapes=[
            pltpu.VMEM((LAYERS, 2, SIDE, SIDE), f32),
            pltpu.VMEM((SIDE, SIDE), f32),
            pltpu.VMEM((4, 3 * SIDE, SIDE), bf16),
            pltpu.VMEM((4, SIDE, 3 * SIDE), bf16),
            pltpu.VMEM((2, 2 * SIDE, HALF), f32),
            pltpu.VMEM((LAYERS, 2) + field, f32),
            pltpu.VMEM((2, modes + 1) + field, f32),
            pltpu.VMEM((modes + 1, 2, SIDE, SIDE), f32),
            pltpu.VMEM((SIDE, SIDE), f32),
            pltpu.VMEM((5,) + field, f32),
            pltpu.VMEM((2, modes, 2, SIDE, HALF), f32),
            pltpu.SemaphoreType.DMA((2, modes, 2)),
            pltpu.SemaphoreType.DMA((4,)),
            pltpu.VMEM((2,) + wide, f32),
            pltpu.VMEM(wide, f32),
            pltpu.VMEM((2, 2, SIDE, SIDE), bf16),
            pltpu.VMEM((2, 2, SIDE, SIDE), bf16),
            pltpu.VMEM((2, 2, SIDE, SIDE), bf16),
            pltpu.VMEM((2, 2, SIDE, SIDE), bf16),
        ],
        compiler_params=pltpu.CompilerParams(vmem_limit_bytes=60 * 1024 * 1024),
        name="wave",
    )(
        corner,
        me,
        *rims,
        own,
        probe,
        measured,
        jnp.asarray(right_table),
        jnp.asarray(left_table),
    )


def sum_kernel(
    me_ref, parts_ref, light_ref, own_ref, right_ref, below_ref, diag_ref, marks_ref, sem
):
    me = me_ref[0]
    copy = pltpu.make_async_copy(parts_ref.at[:, 10, :, pl.ds(0, HALF)], marks_ref, sem)
    copy.start()
    own_ref[...] = jnp.zeros_like(own_ref)
    right_ref[...] = jnp.zeros_like(right_ref)
    below_ref[...] = jnp.zeros_like(below_ref)
    diag_ref[...] = jnp.zeros_like(diag_ref)
    sub = lax.broadcasted_iota(jnp.int32, (2, 8, SIDE), 1)
    side = lax.broadcasted_iota(jnp.int32, (2, 8, SIDE), 0)
    cols = lax.broadcasted_iota(jnp.int32, (2, 8, SIDE), 2)
    rows = HALF * side + 8 * me + sub
    copy.wait()
    for j in range(SCANS):
        r = marks_ref[j, 0, 0].astype(jnp.int32)
        c = marks_ref[j, 0, 1].astype(jnp.int32)
        lights = []
        for h in range(2):
            start = lax.rem(HALF * h + 8 * me + SIDE - r, SIDE)
            base = pl.multiple_of((start // 8) * 8, 8)
            block = light_ref[pl.ds(base, 16), :]
            block = pltpu.roll(block, lax.rem(16 - (start - base), 16), 0)[:8]
            lights.append(pltpu.roll(block, c, 1)[None])
        light = jnp.concatenate(lights, axis=0)
        inside_row, inside_col = rows >= r, cols >= c
        for k in range(6):
            value = parts_ref[j, 2 * k : 2 * k + 2] if k < 5 else light
            here = jnp.where(inside_row, value, 0.0)
            there = (value - here)[0]
            own_ref[k] += jnp.where(inside_col, here, 0.0)
            right_ref[k] += jnp.where(inside_col, 0.0, here)[:, :, :HALF]
            below_ref[k] += jnp.where(inside_col[0], there, 0.0)
            diag_ref[k] += jnp.where(inside_col[0], 0.0, there)[:, :HALF]


def run_sum(me, parts, light):
    smem = pl.BlockSpec(memory_space=pltpu.SMEM)
    vmem = pl.BlockSpec(memory_space=pltpu.VMEM)
    return pl.pallas_call(
        sum_kernel,
        out_shape=(
            jax.ShapeDtypeStruct((6, 2, 8, SIDE), f32),
            jax.ShapeDtypeStruct((6, 2, 8, HALF), f32),
            jax.ShapeDtypeStruct((6, 8, SIDE), f32),
            jax.ShapeDtypeStruct((6, 8, HALF), f32),
        ),
        in_specs=[smem, vmem, vmem],
        out_specs=(vmem,) * 4,
        scratch_shapes=[pltpu.SMEM((SCANS, 8, HALF), f32), pltpu.SemaphoreType.DMA],
        compiler_params=pltpu.CompilerParams(vmem_limit_bytes=8 * 1024 * 1024),
        name="sum",
    )(me, parts, light)


def update_kernel(me_ref, object_ref, own_ref, right_ref, below_ref, diag_ref, out_ref):
    me = me_ref[0]
    sums = []
    for k in range(6):
        near = own_ref[k, :, :, :HALF] + right_ref[k]
        whole = jnp.concatenate([near, own_ref[k, :, :, HALF:]], axis=2)
        low = jnp.concatenate(
            [below_ref[k, :, :HALF] + diag_ref[k], below_ref[k, :, HALF:]], axis=1
        )
        sums.append([whole[0] + low, whole[1]])
    for s in range(LAYERS):
        base = 3 * (1 - s)
        for h in range(2):
            scale = step_size / (sums[base + 2][h] + 1.0)
            start = pl.multiple_of(HALF * h + 8 * me, 8)
            for p in range(2):
                out_ref[s, p, h] = (
                    object_ref[s, p, pl.ds(start, 8), :] - scale * sums[base + p][h]
                )


def run_update(me, current, own, right, below, diag):
    smem = pl.BlockSpec(memory_space=pltpu.SMEM)
    vmem = pl.BlockSpec(memory_space=pltpu.VMEM)
    return pl.pallas_call(
        update_kernel,
        out_shape=jax.ShapeDtypeStruct((LAYERS, 2, 2, 8, SIDE), f32),
        in_specs=[smem] + [vmem] * 5,
        out_specs=vmem,
        compiler_params=pltpu.CompilerParams(vmem_limit_bytes=4 * 1024 * 1024),
        name="update",
    )(me, current, own, right, below, diag)


def place_kernel(me_ref, *refs):
    blocks, out_ref = refs[:-1], refs[-1]
    me = me_ref[0]
    y, z, core = me // 4, lax.rem(me // 2, 2), lax.rem(me, 2)
    count = 0
    for ref in blocks:
        for b in range(ref.shape[0]):
            dc, dy, dz = count // 8, (count // 2) % 4, count % 2
            i = lax.rem(y + 4 - dy, 4) * 4 + lax.rem(z + dz, 2) * 2 + lax.rem(core + dc, 2)
            for h in range(2):
                start = pl.multiple_of(HALF * h + 8 * i, 8)
                out_ref[:, :, pl.ds(start, 8), :] = ref[b, :, :, h]
            count += 1


def run_place(me, blocks):
    vmem = pl.BlockSpec(memory_space=pltpu.VMEM)
    return pl.pallas_call(
        place_kernel,
        out_shape=jax.ShapeDtypeStruct((LAYERS, 2, SIDE, SIDE), f32),
        in_specs=[pl.BlockSpec(memory_space=pltpu.SMEM)] + [vmem] * len(blocks),
        out_specs=vmem,
        compiler_params=pltpu.CompilerParams(vmem_limit_bytes=8 * 1024 * 1024),
        name="place",
    )(me, *blocks)


def shift(array, axis, by):
    count = lax.axis_size(axis)
    pairs = [(i, i + by) for i in range(count) if 0 <= i + by < count]
    return lax.ppermute(array, axis, pairs)


def shift_both(array, by):
    n_x, n_y = lax.axis_size("tx"), lax.axis_size("ty")
    pairs = [
        (a * n_y + b, (a + by) * n_y + b + by)
        for a in range(n_x)
        for b in range(n_y)
        if 0 <= a + by < n_x and 0 <= b + by < n_y
    ]
    return lax.ppermute(array, ("tx", "ty"), pairs)


def along_scan(array, dy, dz, dc):
    pairs = []
    for i in range(SCANS):
        y, z, core = i // 4, (i // 2) % 2, i % 2
        pairs.append((i, ((y + dy) % 4) * 4 + ((z + dz) % 2) * 2 + (core + dc) % 2))
    return lax.ppermute(array, "scan", pairs)


def on_device(object_slices, probe_modes, corners, measured):
    me = lax.axis_index("scan").astype(jnp.int32).reshape(1)
    corner = corners.reshape(2)
    rims = run_cut(me, object_slices)
    rims = (shift(rims[0], "tx", -1), shift(rims[1], "ty", -1), shift_both(rims[2], -1))
    light, expected = run_glow(probe_modes, measured.reshape(SIDE, SIDE))
    rims, light, expected = lax.optimization_barrier((rims, light, expected))
    others = tuple(along_scan(rim, 0, 0, 1) for rim in rims)

    parts = run_wave(
        corner,
        me,
        object_slices,
        rims + others,
        probe_modes,
        expected,
    )
    parts = lax.all_to_all(parts, "scan", 0, 0)
    own, to_right, to_below, to_diag = run_sum(me, parts, light)
    to_right = shift(to_right, "ty", 1)
    to_below = shift(to_below, "tx", 1)
    to_diag = shift_both(to_diag, 1)
    mine = run_update(me, object_slices, own, to_right, to_below, to_diag)[None]
    pair = jnp.concatenate([mine, along_scan(mine, 0, 1, 0)], axis=0)
    ring = [pair] + [along_scan(pair, dy, 0, 0) for dy in (1, 2, 3)]
    ring = jnp.concatenate(ring, axis=0)
    other = along_scan(ring, 0, 0, 1)
    return run_place(me, [ring, other])


def solution(mesh):
    placed = (
        P(None, None, "tx", "ty"),
        P(),
        P("tx", "ty", "scan", None),
        P("tx", "ty", "scan", None, None),
    )
    return jax.shard_map(
        on_device, mesh=mesh, in_specs=placed, out_specs=P(None, None, "tx", "ty"), check_vma=False
    )
```

```python
import functools
import math

import jax
import jax.numpy as jnp
import numpy as np
from jax import lax
from jax.experimental import pallas as pl
from jax.experimental.pallas import tpu as pltpu
from jax.sharding import PartitionSpec as P

fresnel_coef = 0.1
step_size = 4.0
SIDE = 256
HALF = 128
LAYERS = 2
SCANS = 16
ROWS = 32
PAD = 8
f32 = jnp.float32
bf16 = jnp.bfloat16


def real_right(table):
    return np.block([[table.real, table.imag], [-table.imag, table.real]])


def real_left(table):
    return np.block([[table.real, -table.imag], [table.imag, table.real]])


def stacked(table, axis):
    high = table.astype(np.float32).astype(bf16)
    low = (table - high.astype(np.float64)).astype(np.float32).astype(bf16)
    return np.concatenate([high, high, low], axis=axis)


def make_tables():
    half = np.arange(HALF)
    col_even = np.exp(-2j * np.pi * np.outer(half, half) / HALF) / 16
    col_odd = np.exp(-2j * np.pi * np.outer(half, 2 * half + 1) / SIDE) / 16
    row_even, row_odd = col_even.T, col_odd.T
    right = [col_even, col_odd, col_even.conj().T, col_odd.conj().T]
    left = [row_even, row_odd, row_even.conj().T, row_odd.conj().T]
    right = np.stack([stacked(real_right(t), 0) for t in right])
    left = np.stack([stacked(real_left(t), 1) for t in left])
    return right, left


def split(value):
    high = value.astype(bf16)
    return high, (value - high.astype(f32)).astype(bf16)


def mul(first, second):
    return jnp.dot(first, second, preferred_element_type=f32)


def put(ref, lead, rows, value):
    high, low = split(value)
    ref[lead + (0, rows)] = high
    ref[lead + (1, rows)] = low


def right_dot(ref, side, table, which):
    high, low = ref[side, 0], ref[side, 1]
    return mul(jnp.concatenate([high, low, high], axis=1), table[which])


def left_dot(table, which, ref, side):
    high, low = ref[side, 0], ref[side, 1]
    return mul(table[which], jnp.concatenate([high, low, high], axis=0))


def neighbours(ref, p, start):
    rows = lambda by: pl.ds(start + PAD + by, ROWS)
    low, high = ref[p, 0, rows(0)], ref[p, 1, rows(0)]
    lane = lax.broadcasted_iota(jnp.int32, low.shape, 1)
    first, last = lane == 0, lane == HALF - 1
    low_up, high_up = pltpu.roll(low, 1, 1), pltpu.roll(high, 1, 1)
    low_down, high_down = pltpu.roll(low, HALF - 1, 1), pltpu.roll(high, HALF - 1, 1)
    low_sum = jnp.where(first, 0.0, low_up) + jnp.where(last, high_down, low_down)
    high_sum = jnp.where(first, low_up, high_up) + jnp.where(last, 0.0, high_down)
    return (
        low_sum + (ref[p, 0, rows(-1)] + ref[p, 0, rows(1)]),
        high_sum + (ref[p, 1, rows(-1)] + ref[p, 1, rows(1)]),
    )


damping = 0.5 * fresnel_coef**2


def turn_rows(source, target, start, sign):
    turn = sign * fresnel_coef
    rows = pl.ds(start + PAD, ROWS)
    near_re, near_im = neighbours(source, 0, start), neighbours(source, 1, start)
    for h in range(2):
        re, im = source[0, h, rows], source[1, h, rows]
        target[0, h, rows] = 4.0 * damping * re - turn * im - damping * near_re[h]
        target[1, h, rows] = 4.0 * damping * im + turn * re - damping * near_im[h]


def end_rows(source, target, start):
    rows = pl.ds(start + PAD, ROWS)
    near = [neighbours(target, p, start) for p in range(2)]
    return [
        [source[p, h, rows] - 4.0 * target[p, h, rows] + near[p][h] for p in range(2)]
        for h in range(2)
    ]


def wave_kernel(
    corner_ref,
    me_ref,
    below_far,
    right_far,
    diag_far,
    other_below_far,
    other_right_far,
    other_diag_far,
    own_far,
    probe,
    measured_far,
    col_far,
    row_far,
    out_ref,
    own_ref,
    measured_ref,
    col_tab,
    row_tab,
    hold,
    trans,
    wave,
    far,
    misfit,
    total,
    more_sems,
    field,
    turned,
    across_0,
    across_1,
    along_0,
    along_1,
    below_ref,
    right_ref,
    diag_ref,
    rim_sems,
):
    across, along = (across_0, across_1), (along_0, along_1)
    r, c = corner_ref[0], corner_ref[1]
    modes = probe.shape[1]
    own_copy = pltpu.make_async_copy(own_far, own_ref, more_sems.at[0])
    later = [
        pltpu.make_async_copy(source, target, more_sems.at[n + 1])
        for n, (source, target) in enumerate(
            [
                (col_far, col_tab),
                (row_far, row_tab),
                (measured_far, measured_ref),
            ]
        )
    ]
    core = lax.rem(me_ref[0], 2)
    rim_copies = [
        pltpu.make_async_copy(
            source, target.at[lax.rem(core + side, 2)], rim_sems.at[side, n]
        )
        for side, sources in enumerate(
            [(below_far, right_far, diag_far), (other_below_far, other_right_far, other_diag_far)]
        )
        for n, (source, target) in enumerate(zip(sources, (below_ref, right_ref, diag_ref)))
    ]
    own_copy.start()
    for copy in rim_copies:
        copy.start()
    for copy in later:
        copy.start()
    rows = lax.broadcasted_iota(jnp.int32, (SIDE, SIDE), 0)
    cols = lax.broadcasted_iota(jnp.int32, (SIDE, SIDE), 1)
    top = rows[:HALF] < r
    near = cols[:, :HALF] < c
    back_c = lax.rem(SIDE - c, SIDE)
    own_copy.wait()
    for copy in rim_copies:
        copy.wait()
    for s in range(LAYERS):
        for p in range(2):
            right, below, diag = right_ref[p, s], below_ref[p, s], diag_ref[p, s]
            left = jnp.where(near, right, own_ref[s, p, :, :HALF])
            whole = jnp.concatenate([left, own_ref[s, p, :, HALF:]], axis=1)
            lower = jnp.concatenate(
                [jnp.where(near[:HALF], diag, below[:, :HALF]), below[:, HALF:]], axis=1
            )
            whole = jnp.concatenate([jnp.where(top, lower, whole[:HALF]), whole[HALF:]], axis=0)
            whole = pltpu.roll(whole, back_c, 1)
            for half in range(2):
                hold[0, half * SIDE : (half + 1) * SIDE] = whole[:, :HALF]
                hold[1, half * SIDE : (half + 1) * SIDE] = whole[:, HALF:]
            for h in range(2):
                view = hold[h, pl.ds(r, SIDE)]
                trans[s, p, h] = view + 1.0 if p == 0 else view

    misfit[...] = jnp.zeros_like(misfit)
    total[...] = jnp.zeros_like(total)
    field[...] = jnp.zeros_like(field)
    turned[...] = jnp.zeros_like(turned)
    far[modes] = jnp.zeros_like(far[modes])
    starts = range(0, SIDE, ROWS)

    def enter(m, side):
        held = jnp.minimum(m, modes - 1)
        for start in starts:
            rows, inner = pl.ds(start, ROWS), pl.ds(start + PAD, ROWS)
            for h in range(2):
                p_re, p_im = probe[0, held, h, rows], probe[1, held, h, rows]
                t_re, t_im = trans[0, 0, h, rows], trans[0, 1, h, rows]
                field[side, 0, h, inner] = p_re * t_re - p_im * t_im
                field[side, 1, h, inner] = p_re * t_im + p_im * t_re
            yield
        for start in starts:
            turn_rows(field.at[side], turned, start, 1.0)
            yield
        for start in starts:
            rows = pl.ds(start, ROWS)
            x = []
            for h, (w_re, w_im) in enumerate(end_rows(field.at[side], turned, start)):
                wave[0, m, h, rows] = w_re
                wave[1, m, h, rows] = w_im
                t_re, t_im = trans[1, 0, h, rows], trans[1, 1, h, rows]
                x.append(
                    jnp.concatenate([w_re * t_re - w_im * t_im, w_re * t_im + w_im * t_re], axis=1)
                )
            put(across[side], (0,), rows, x[0] + x[1])
            put(across[side], (1,), rows, x[0] - x[1])
            yield

    def transform(m, side):
        even = right_dot(across[side], 0, col_tab, 0)
        yield
        odd = right_dot(across[side], 1, col_tab, 1)
        yield
        for start in range(0, HALF, ROWS):
            for q in range(2):
                lanes = slice(HALF * q, HALF * (q + 1))
                above, under = [
                    jnp.concatenate([even[part, lanes], odd[part, lanes]], axis=1)
                    for part in (slice(start, start + ROWS), slice(start + HALF, start + HALF + ROWS))
                ]
                rows = pl.ds(HALF * q + start, ROWS)
                put(along[side], (0,), rows, above + under)
                put(along[side], (1,), rows, above - under)
            yield
        for e in range(2):
            found = left_dot(row_tab, e, along[side], e)
            yield
            for start in range(0, HALF, ROWS):
                re, im = found[start : start + ROWS], found[HALF + start : HALF + start + ROWS]
                far[m, e, pl.ds(start, ROWS)] = re
                far[m, e, pl.ds(HALF + start, ROWS)] = im
                misfit[pl.ds(HALF * e + start, ROWS)] += re * re + im * im
                yield
        for start in starts:
            rows = pl.ds(start, ROWS)
            for h in range(2):
                w_re, w_im = wave[0, m, h, rows], wave[1, m, h, rows]
                total[2, h, rows] += w_re * w_re + w_im * w_im
            yield

    def beside(*parts):
        live = list(parts)
        while live:
            live = [part for part in live if next(part, live) is not live]

    beside(enter(0, 0))
    for copy in later:
        copy.wait()

    def forward(j, carry):
        beside(transform(2 * j, 0), enter(2 * j + 1, 1))
        beside(transform(2 * j + 1, 1), enter(2 * j + 2, 0))
        return carry

    lax.fori_loop(0, modes // 2, forward, 0)
    misfit[...] = 2.0 * (misfit[...] - measured_ref[...])

    def restore(m, side):
        for e in range(2):
            for start in range(0, HALF, ROWS):
                scale = misfit[pl.ds(HALF * e + start, ROWS)]
                for q in range(2):
                    rows = pl.ds(HALF * q + start, ROWS)
                    put(along[side], (e,), rows, scale * far[m, e, rows])
                yield
        even = left_dot(row_tab, 2, along[side], 0)
        yield
        odd = left_dot(row_tab, 3, along[side], 1)
        yield
        for start in range(0, HALF, ROWS):
            re, im = slice(start, start + ROWS), slice(HALF + start, HALF + start + ROWS)
            for n in range(2):
                f_re = even[re] + odd[re] if n == 0 else even[re] - odd[re]
                f_im = even[im] + odd[im] if n == 0 else even[im] - odd[im]
                rows = pl.ds(HALF * n + start, ROWS)
                for q in range(2):
                    lanes = slice(HALF * q, HALF * (q + 1))
                    put(
                        across[side],
                        (q,),
                        rows,
                        jnp.concatenate([f_re[:, lanes], f_im[:, lanes]], axis=1),
                    )
            yield
        first = right_dot(across[side], 0, col_tab, 2)
        yield
        second = right_dot(across[side], 1, col_tab, 3)
        yield
        for start in starts:
            rows, inner = pl.ds(start, ROWS), pl.ds(start + PAD, ROWS)
            part = slice(start, start + ROWS)
            for h in range(2):
                both = first[part] + second[part] if h == 0 else first[part] - second[part]
                b_re, b_im = both[:, :HALF], both[:, HALF:]
                w_re, w_im = wave[0, m, h, rows], wave[1, m, h, rows]
                total[0, h, rows] += w_re * b_re + w_im * b_im
                total[1, h, rows] += w_re * b_im - w_im * b_re
                t_re, t_im = trans[1, 0, h, rows], trans[1, 1, h, rows]
                field[side, 0, h, inner] = t_re * b_re + t_im * b_im
                field[side, 1, h, inner] = t_re * b_im - t_im * b_re
            yield

    def leave(m, side):
        for start in starts:
            turn_rows(field.at[side], turned, start, -1.0)
            yield
        for start in starts:
            rows = pl.ds(start, ROWS)
            for h, (d_re, d_im) in enumerate(end_rows(field.at[side], turned, start)):
                p_re, p_im = probe[0, m, h, rows], probe[1, m, h, rows]
                total[3, h, rows] += p_re * d_re + p_im * d_im
                total[4, h, rows] += p_re * d_im - p_im * d_re
            yield

    beside(restore(0, 0))

    def backward(j, carry):
        beside(restore(2 * j + 1, 1), leave(2 * j, 0))
        beside(restore(2 * j + 2, 0), leave(2 * j + 1, 1))
        return carry

    lax.fori_loop(0, modes // 2, backward, 0)

    for k in range(5):
        for h in range(2):
            hold[h, :SIDE] = total[k, h]
            hold[h, SIDE:] = total[k, h]
        for n in range(SIDE // 8):
            rows = pl.ds(SIDE - r + 8 * n, 8)
            block = jnp.concatenate([hold[0, rows], hold[1, rows]], axis=1)
            out_ref[n % 16, 2 * k + n // 16] = pltpu.roll(block, c, 1)
    lane = lax.broadcasted_iota(jnp.int32, (8, SIDE), 1)
    mark = jnp.where(lane == 0, r, c).astype(f32)
    for i in range(SCANS):
        out_ref[i, 10] = mark


def glow_kernel(probe_ref, measured_ref, light_ref, expected_ref, halves_ref):
    @pl.when(pl.program_id(0) == 0)
    def _():
        light_ref[...] = jnp.zeros_like(light_ref)
        row = lax.broadcasted_iota(jnp.int32, (SIDE, SIDE), 0)
        col = lax.broadcasted_iota(jnp.int32, (SIDE, SIDE), 1)
        place = lambda k: jnp.where(k < HALF, 2 * k, 2 * (k - HALF) + 1)
        by_col = (row == place(col)).astype(f32).astype(bf16)
        by_row = (col == place(row)).astype(f32).astype(bf16)
        value = measured_ref[...]
        for left in (False, True):
            high, low = split(value)
            rest = (value - high.astype(f32) - low.astype(f32)).astype(bf16)
            if left:
                value = mul(by_row, high) + mul(by_row, low) + mul(by_row, rest)
            else:
                value = mul(high, by_col) + mul(low, by_col) + mul(rest, by_col)
        expected_ref[...] = value

    for p in range(2):
        for h in range(2):
            halves_ref[p, 0, h] = probe_ref[p, 0, :, h * HALF : (h + 1) * HALF]
    light = probe_ref[0, 0] * probe_ref[0, 0] + probe_ref[1, 0] * probe_ref[1, 0]
    light_ref[:SIDE] += light
    light_ref[SIDE:] += light


def run_glow(probe, measured):
    modes = probe.shape[1]
    return pl.pallas_call(
        glow_kernel,
        grid=(modes,),
        out_shape=(
            jax.ShapeDtypeStruct((2 * SIDE, SIDE), f32),
            jax.ShapeDtypeStruct((SIDE, SIDE), f32),
            jax.ShapeDtypeStruct((2, modes, 2, SIDE, HALF), f32),
        ),
        in_specs=[
            pl.BlockSpec((2, 1, SIDE, SIDE), lambda m: (0, m, 0, 0)),
            pl.BlockSpec((SIDE, SIDE), lambda m: (0, 0)),
        ],
        out_specs=(
            pl.BlockSpec((2 * SIDE, SIDE), lambda m: (0, 0)),
            pl.BlockSpec((SIDE, SIDE), lambda m: (0, 0)),
            pl.BlockSpec((2, 1, 2, SIDE, HALF), lambda m: (0, m, 0, 0, 0)),
        ),
        compiler_params=pltpu.CompilerParams(vmem_limit_bytes=10 * 1024 * 1024),
        cost_estimate=pl.CostEstimate(
            flops=4 * modes * SIDE * SIDE, bytes_accessed=8 * modes * SIDE * SIDE, transcendentals=0
        ),
        name="glow",
    )(probe, measured)


def cut_kernel(me_ref, object_ref, below_ref, right_ref, diag_ref, sems):
    core = lax.rem(me_ref[0], 2)
    copies = []
    for s in range(LAYERS):
        plane = object_ref.at[s, core]
        near = pl.ds(0, HALF)
        for n, (source, target) in enumerate(
            [
                (plane.at[near, :], below_ref.at[s]),
                (plane.at[:, near], right_ref.at[s]),
                (plane.at[near, near], diag_ref.at[s]),
            ]
        ):
            copies.append(pltpu.make_async_copy(source, target, sems.at[s, n]))
    for copy in copies:
        copy.start()
    for copy in copies:
        copy.wait()


def run_cut(me, current):
    far = pl.BlockSpec(memory_space=pl.ANY)
    return pl.pallas_call(
        cut_kernel,
        out_shape=(
            jax.ShapeDtypeStruct((LAYERS, HALF, SIDE), f32),
            jax.ShapeDtypeStruct((LAYERS, SIDE, HALF), f32),
            jax.ShapeDtypeStruct((LAYERS, HALF, HALF), f32),
        ),
        in_specs=[pl.BlockSpec(memory_space=pltpu.SMEM), far],
        out_specs=(pl.BlockSpec(memory_space=pltpu.VMEM),) * 3,
        scratch_shapes=[pltpu.SemaphoreType.DMA((LAYERS, 3))],
        compiler_params=pltpu.CompilerParams(vmem_limit_bytes=4 * 1024 * 1024),
        name="cut",
    )(me, current)


def run_wave(corner, me, own, rims, probe, measured):
    right_table, left_table = make_tables()
    modes = probe.shape[1]
    vmem = pl.BlockSpec(memory_space=pltpu.VMEM)
    field = (2, SIDE, HALF)
    wide = (2, 2, SIDE + 2 * PAD, HALF)
    return pl.pallas_call(
        wave_kernel,
        out_shape=jax.ShapeDtypeStruct((SCANS, 11, 8, SIDE), f32),
        in_specs=[pl.BlockSpec(memory_space=pltpu.SMEM)] * 2
        + [pl.BlockSpec(memory_space=pl.ANY)] * 7
        + [vmem]
        + [pl.BlockSpec(memory_space=pl.ANY)] * 3,
        out_specs=vmem,
        scratch_shapes=[
            pltpu.VMEM((LAYERS, 2, SIDE, SIDE), f32),
            pltpu.VMEM((SIDE, SIDE), f32),
            pltpu.VMEM((4, 3 * SIDE, SIDE), bf16),
            pltpu.VMEM((4, SIDE, 3 * SIDE), bf16),
            pltpu.VMEM((2, 2 * SIDE, HALF), f32),
            pltpu.VMEM((LAYERS, 2) + field, f32),
            pltpu.VMEM((2, modes + 1) + field, f32),
            pltpu.VMEM((modes + 1, 2, SIDE, SIDE), f32),
            pltpu.VMEM((SIDE, SIDE), f32),
            pltpu.VMEM((5,) + field, f32),
            pltpu.SemaphoreType.DMA((4,)),
            pltpu.VMEM((2,) + wide, f32),
            pltpu.VMEM(wide, f32),
            pltpu.VMEM((2, 2, SIDE, SIDE), bf16),
            pltpu.VMEM((2, 2, SIDE, SIDE), bf16),
            pltpu.VMEM((2, 2, SIDE, SIDE), bf16),
            pltpu.VMEM((2, 2, SIDE, SIDE), bf16),
            pltpu.VMEM((2, LAYERS, HALF, SIDE), f32),
            pltpu.VMEM((2, LAYERS, SIDE, HALF), f32),
            pltpu.VMEM((2, LAYERS, HALF, HALF), f32),
            pltpu.SemaphoreType.DMA((2, 3)),
        ],
        compiler_params=pltpu.CompilerParams(vmem_limit_bytes=36 * 1024 * 1024),
        name="wave",
    )(
        corner,
        me,
        *rims,
        own,
        probe,
        measured,
        jnp.asarray(right_table),
        jnp.asarray(left_table),
    )


def sum_kernel(
    me_ref, parts_ref, light_ref, own_ref, right_ref, below_ref, diag_ref, marks_ref, sem
):
    me = me_ref[0]
    copy = pltpu.make_async_copy(parts_ref.at[:, 10, :, pl.ds(0, HALF)], marks_ref, sem)
    copy.start()
    own_ref[...] = jnp.zeros_like(own_ref)
    right_ref[...] = jnp.zeros_like(right_ref)
    below_ref[...] = jnp.zeros_like(below_ref)
    diag_ref[...] = jnp.zeros_like(diag_ref)
    sub = lax.broadcasted_iota(jnp.int32, (2, 8, SIDE), 1)
    side = lax.broadcasted_iota(jnp.int32, (2, 8, SIDE), 0)
    cols = lax.broadcasted_iota(jnp.int32, (2, 8, SIDE), 2)
    rows = HALF * side + 8 * me + sub
    copy.wait()
    for j in range(SCANS):
        r = marks_ref[j, 0, 0].astype(jnp.int32)
        c = marks_ref[j, 0, 1].astype(jnp.int32)
        lights = []
        for h in range(2):
            start = lax.rem(HALF * h + 8 * me + SIDE - r, SIDE)
            base = pl.multiple_of((start // 8) * 8, 8)
            block = light_ref[pl.ds(base, 16), :]
            block = pltpu.roll(block, lax.rem(16 - (start - base), 16), 0)[:8]
            lights.append(pltpu.roll(block, c, 1)[None])
        light = jnp.concatenate(lights, axis=0)
        inside_row, inside_col = rows >= r, cols >= c
        for k in range(6):
            value = parts_ref[j, 2 * k : 2 * k + 2] if k < 5 else light
            here = jnp.where(inside_row, value, 0.0)
            there = (value - here)[0]
            own_ref[k] += jnp.where(inside_col, here, 0.0)
            right_ref[k] += jnp.where(inside_col, 0.0, here)[:, :, :HALF]
            below_ref[k] += jnp.where(inside_col[0], there, 0.0)
            diag_ref[k] += jnp.where(inside_col[0], 0.0, there)[:, :HALF]


def run_sum(me, parts, light):
    smem = pl.BlockSpec(memory_space=pltpu.SMEM)
    vmem = pl.BlockSpec(memory_space=pltpu.VMEM)
    return pl.pallas_call(
        sum_kernel,
        out_shape=(
            jax.ShapeDtypeStruct((6, 2, 8, SIDE), f32),
            jax.ShapeDtypeStruct((6, 2, 8, HALF), f32),
            jax.ShapeDtypeStruct((6, 8, SIDE), f32),
            jax.ShapeDtypeStruct((6, 8, HALF), f32),
        ),
        in_specs=[smem, vmem, vmem],
        out_specs=(vmem,) * 4,
        scratch_shapes=[pltpu.SMEM((SCANS, 8, HALF), f32), pltpu.SemaphoreType.DMA],
        compiler_params=pltpu.CompilerParams(vmem_limit_bytes=8 * 1024 * 1024),
        name="sum",
    )(me, parts, light)


def update_kernel(me_ref, object_ref, own_ref, right_ref, below_ref, diag_ref, out_ref):
    me = me_ref[0]
    sums = []
    for k in range(6):
        near = own_ref[k, :, :, :HALF] + right_ref[k]
        whole = jnp.concatenate([near, own_ref[k, :, :, HALF:]], axis=2)
        low = jnp.concatenate(
            [below_ref[k, :, :HALF] + diag_ref[k], below_ref[k, :, HALF:]], axis=1
        )
        sums.append([whole[0] + low, whole[1]])
    for s in range(LAYERS):
        base = 3 * (1 - s)
        for h in range(2):
            scale = step_size / (sums[base + 2][h] + 1.0)
            start = pl.multiple_of(HALF * h + 8 * me, 8)
            for p in range(2):
                out_ref[s, p, h] = (
                    object_ref[s, p, pl.ds(start, 8), :] - scale * sums[base + p][h]
                )


def run_update(me, current, own, right, below, diag):
    smem = pl.BlockSpec(memory_space=pltpu.SMEM)
    vmem = pl.BlockSpec(memory_space=pltpu.VMEM)
    return pl.pallas_call(
        update_kernel,
        out_shape=jax.ShapeDtypeStruct((LAYERS, 2, 2, 8, SIDE), f32),
        in_specs=[smem] + [vmem] * 5,
        out_specs=vmem,
        compiler_params=pltpu.CompilerParams(vmem_limit_bytes=4 * 1024 * 1024),
        name="update",
    )(me, current, own, right, below, diag)


def place_kernel(me_ref, *refs):
    blocks, out_ref = refs[:-1], refs[-1]
    me = me_ref[0]
    y, z, core = me // 4, lax.rem(me // 2, 2), lax.rem(me, 2)
    count = 0
    for ref in blocks:
        for b in range(ref.shape[0]):
            dc, dy, dz = count // 8, (count // 2) % 4, count % 2
            i = lax.rem(y + 4 - dy, 4) * 4 + lax.rem(z + dz, 2) * 2 + lax.rem(core + dc, 2)
            for h in range(2):
                start = pl.multiple_of(HALF * h + 8 * i, 8)
                out_ref[:, :, pl.ds(start, 8), :] = ref[b, :, :, h]
            count += 1


def run_place(me, blocks):
    vmem = pl.BlockSpec(memory_space=pltpu.VMEM)
    return pl.pallas_call(
        place_kernel,
        out_shape=jax.ShapeDtypeStruct((LAYERS, 2, SIDE, SIDE), f32),
        in_specs=[pl.BlockSpec(memory_space=pltpu.SMEM)] + [vmem] * len(blocks),
        out_specs=vmem,
        compiler_params=pltpu.CompilerParams(vmem_limit_bytes=8 * 1024 * 1024),
        name="place",
    )(me, *blocks)


def shift(array, axis, by):
    count = lax.axis_size(axis)
    pairs = [(i, i + by) for i in range(count) if 0 <= i + by < count]
    return lax.ppermute(array, axis, pairs)


def shift_both(array, by):
    n_x, n_y = lax.axis_size("tx"), lax.axis_size("ty")
    pairs = [
        (a * n_y + b, (a + by) * n_y + b + by)
        for a in range(n_x)
        for b in range(n_y)
        if 0 <= a + by < n_x and 0 <= b + by < n_y
    ]
    return lax.ppermute(array, ("tx", "ty"), pairs)


def along_scan(array, dy, dz, dc):
    pairs = []
    for i in range(SCANS):
        y, z, core = i // 4, (i // 2) % 2, i % 2
        pairs.append((i, ((y + dy) % 4) * 4 + ((z + dz) % 2) * 2 + (core + dc) % 2))
    return lax.ppermute(array, "scan", pairs)


def on_device(object_slices, probe_modes, corners, measured):
    me = lax.axis_index("scan").astype(jnp.int32).reshape(1)
    corner = corners.reshape(2)
    rims = run_cut(me, object_slices)
    rims = (shift(rims[0], "tx", -1), shift(rims[1], "ty", -1), shift_both(rims[2], -1))
    light, expected, halves = run_glow(probe_modes, measured.reshape(SIDE, SIDE))
    rims, light, expected, halves = lax.optimization_barrier((rims, light, expected, halves))
    others = tuple(along_scan(rim, 0, 0, 1) for rim in rims)

    parts = run_wave(
        corner,
        me,
        object_slices,
        rims + others,
        halves,
        expected,
    )
    parts = lax.all_to_all(parts, "scan", 0, 0)
    own, to_right, to_below, to_diag = run_sum(me, parts, light)
    to_right = shift(to_right, "ty", 1)
    to_below = shift(to_below, "tx", 1)
    to_diag = shift_both(to_diag, 1)
    mine = run_update(me, object_slices, own, to_right, to_below, to_diag)[None]
    pair = jnp.concatenate([mine, along_scan(mine, 0, 1, 0)], axis=0)
    ring = [pair] + [along_scan(pair, dy, 0, 0) for dy in (1, 2, 3)]
    ring = jnp.concatenate(ring, axis=0)
    other = along_scan(ring, 0, 0, 1)
    return run_place(me, [ring, other])


def solution(mesh):
    placed = (
        P(None, None, "tx", "ty"),
        P(),
        P("tx", "ty", "scan", None),
        P("tx", "ty", "scan", None, None),
    )
    return jax.shard_map(
        on_device, mesh=mesh, in_specs=placed, out_specs=P(None, None, "tx", "ty"), check_vma=False
    )
```

```python
import functools
import math

import jax
import jax.numpy as jnp
import numpy as np
from jax import lax
from jax.experimental import pallas as pl
from jax.experimental.pallas import tpu as pltpu
from jax.sharding import PartitionSpec as P

fresnel_coef = 0.1
step_size = 4.0
SIDE = 256
HALF = 128
LAYERS = 2
SCANS = 16
ROWS = 32
PAD = 8
f32 = jnp.float32
bf16 = jnp.bfloat16


def real_right(table):
    return np.block([[table.real, table.imag], [-table.imag, table.real]])


def real_left(table):
    return np.block([[table.real, -table.imag], [table.imag, table.real]])


def stacked(table, axis):
    high = table.astype(np.float32).astype(bf16)
    low = (table - high.astype(np.float64)).astype(np.float32).astype(bf16)
    return np.concatenate([high, high, low], axis=axis)


def make_tables():
    half = np.arange(HALF)
    col_even = np.exp(-2j * np.pi * np.outer(half, half) / HALF) / 16
    col_odd = np.exp(-2j * np.pi * np.outer(half, 2 * half + 1) / SIDE) / 16
    row_even, row_odd = col_even.T, col_odd.T
    right = [col_even, col_odd, col_even.conj().T, col_odd.conj().T]
    left = [row_even, row_odd, row_even.conj().T, row_odd.conj().T]
    right = np.stack([stacked(real_right(t), 0) for t in right])
    left = np.stack([stacked(real_left(t), 1) for t in left])
    return right, left


def split(value):
    high = value.astype(bf16)
    return high, (value - high.astype(f32)).astype(bf16)


def mul(first, second):
    return jnp.dot(first, second, preferred_element_type=f32)


def put(ref, lead, rows, value):
    high, low = split(value)
    ref[lead + (0, rows)] = high
    ref[lead + (1, rows)] = low


def right_dot(ref, side, table, which):
    high, low = ref[side, 0], ref[side, 1]
    return mul(jnp.concatenate([high, low, high], axis=1), table[which])


def left_dot(table, which, ref, side):
    high, low = ref[side, 0], ref[side, 1]
    return mul(table[which], jnp.concatenate([high, low, high], axis=0))


def neighbours(ref, p, start):
    rows = lambda by: pl.ds(start + PAD + by, ROWS)
    low, high = ref[p, 0, rows(0)], ref[p, 1, rows(0)]
    lane = lax.broadcasted_iota(jnp.int32, low.shape, 1)
    first, last = lane == 0, lane == HALF - 1
    low_up, high_up = pltpu.roll(low, 1, 1), pltpu.roll(high, 1, 1)
    low_down, high_down = pltpu.roll(low, HALF - 1, 1), pltpu.roll(high, HALF - 1, 1)
    low_sum = jnp.where(first, 0.0, low_up) + jnp.where(last, high_down, low_down)
    high_sum = jnp.where(first, low_up, high_up) + jnp.where(last, 0.0, high_down)
    return (
        low_sum + (ref[p, 0, rows(-1)] + ref[p, 0, rows(1)]),
        high_sum + (ref[p, 1, rows(-1)] + ref[p, 1, rows(1)]),
    )


damping = 0.5 * fresnel_coef**2


def turn_rows(source, target, start, sign):
    turn = sign * fresnel_coef
    rows = pl.ds(start + PAD, ROWS)
    near_re, near_im = neighbours(source, 0, start), neighbours(source, 1, start)
    for h in range(2):
        re, im = source[0, h, rows], source[1, h, rows]
        target[0, h, rows] = 4.0 * damping * re - turn * im - damping * near_re[h]
        target[1, h, rows] = 4.0 * damping * im + turn * re - damping * near_im[h]


def end_rows(source, target, start):
    rows = pl.ds(start + PAD, ROWS)
    near = [neighbours(target, p, start) for p in range(2)]
    return [
        [source[p, h, rows] - 4.0 * target[p, h, rows] + near[p][h] for p in range(2)]
        for h in range(2)
    ]


def wave_kernel(
    corner_ref,
    me_ref,
    below_far,
    right_far,
    diag_far,
    other_below_far,
    other_right_far,
    other_diag_far,
    own_far,
    probe,
    measured_far,
    col_far,
    row_far,
    out_ref,
    own_ref,
    measured_ref,
    col_tab,
    row_tab,
    hold,
    trans,
    wave,
    far,
    misfit,
    total,
    more_sems,
    field,
    turned,
    across_0,
    across_1,
    along_0,
    along_1,
    below_ref,
    right_ref,
    diag_ref,
    rim_sems,
):
    across, along = (across_0, across_1), (along_0, along_1)
    r, c = corner_ref[0], corner_ref[1]
    modes = probe.shape[1]
    own_copy = pltpu.make_async_copy(own_far, own_ref, more_sems.at[0])
    later = [
        pltpu.make_async_copy(source, target, more_sems.at[n + 1])
        for n, (source, target) in enumerate(
            [
                (col_far, col_tab),
                (row_far, row_tab),
                (measured_far, measured_ref),
            ]
        )
    ]
    core = lax.rem(me_ref[0], 2)
    rim_copies = [
        pltpu.make_async_copy(
            source, target.at[lax.rem(core + side, 2)], rim_sems.at[side, n]
        )
        for side, sources in enumerate(
            [(below_far, right_far, diag_far), (other_below_far, other_right_far, other_diag_far)]
        )
        for n, (source, target) in enumerate(zip(sources, (below_ref, right_ref, diag_ref)))
    ]
    own_copy.start()
    for copy in rim_copies:
        copy.start()
    for copy in later:
        copy.start()
    rows = lax.broadcasted_iota(jnp.int32, (SIDE, SIDE), 0)
    cols = lax.broadcasted_iota(jnp.int32, (SIDE, SIDE), 1)
    top = rows[:HALF] < r
    near = cols[:, :HALF] < c
    back_c = lax.rem(SIDE - c, SIDE)
    own_copy.wait()
    for copy in rim_copies:
        copy.wait()
    for s in range(LAYERS):
        for p in range(2):
            right, below, diag = right_ref[p, s], below_ref[p, s], diag_ref[p, s]
            left = jnp.where(near, right, own_ref[s, p, :, :HALF])
            whole = jnp.concatenate([left, own_ref[s, p, :, HALF:]], axis=1)
            lower = jnp.concatenate(
                [jnp.where(near[:HALF], diag, below[:, :HALF]), below[:, HALF:]], axis=1
            )
            whole = jnp.concatenate([jnp.where(top, lower, whole[:HALF]), whole[HALF:]], axis=0)
            whole = pltpu.roll(whole, back_c, 1)
            for half in range(2):
                hold[0, half * SIDE : (half + 1) * SIDE] = whole[:, :HALF]
                hold[1, half * SIDE : (half + 1) * SIDE] = whole[:, HALF:]
            for h in range(2):
                view = hold[h, pl.ds(r, SIDE)]
                trans[s, p, h] = view + 1.0 if p == 0 else view

    misfit[...] = jnp.zeros_like(misfit)
    total[...] = jnp.zeros_like(total)
    field[...] = jnp.zeros_like(field)
    turned[...] = jnp.zeros_like(turned)
    far[modes] = jnp.zeros_like(far[modes])
    starts = range(0, SIDE, ROWS)

    def enter(m, side):
        held = jnp.minimum(m, modes - 1)
        for start in starts:
            rows, inner = pl.ds(start, ROWS), pl.ds(start + PAD, ROWS)
            for h in range(2):
                p_re, p_im = probe[0, held, h, rows], probe[1, held, h, rows]
                t_re, t_im = trans[0, 0, h, rows], trans[0, 1, h, rows]
                field[side, 0, h, inner] = p_re * t_re - p_im * t_im
                field[side, 1, h, inner] = p_re * t_im + p_im * t_re
            yield
        for start in starts:
            turn_rows(field.at[side], turned, start, 1.0)
            yield
        for start in starts:
            rows = pl.ds(start, ROWS)
            x = []
            for h, (w_re, w_im) in enumerate(end_rows(field.at[side], turned, start)):
                wave[0, m, h, rows] = w_re
                wave[1, m, h, rows] = w_im
                t_re, t_im = trans[1, 0, h, rows], trans[1, 1, h, rows]
                x.append(
                    jnp.concatenate([w_re * t_re - w_im * t_im, w_re * t_im + w_im * t_re], axis=1)
                )
            put(across[side], (0,), rows, x[0] + x[1])
            put(across[side], (1,), rows, x[0] - x[1])
            yield

    def transform(m, side):
        even = right_dot(across[side], 0, col_tab, 0)
        yield
        odd = right_dot(across[side], 1, col_tab, 1)
        yield
        for start in range(0, HALF, ROWS):
            for q in range(2):
                lanes = slice(HALF * q, HALF * (q + 1))
                above, under = [
                    jnp.concatenate([even[part, lanes], odd[part, lanes]], axis=1)
                    for part in (slice(start, start + ROWS), slice(start + HALF, start + HALF + ROWS))
                ]
                rows = pl.ds(HALF * q + start, ROWS)
                put(along[side], (0,), rows, above + under)
                put(along[side], (1,), rows, above - under)
            yield
        for e in range(2):
            found = left_dot(row_tab, e, along[side], e)
            yield
            for start in range(0, HALF, ROWS):
                re, im = found[start : start + ROWS], found[HALF + start : HALF + start + ROWS]
                far[m, e, pl.ds(start, ROWS)] = re
                far[m, e, pl.ds(HALF + start, ROWS)] = im
                misfit[pl.ds(HALF * e + start, ROWS)] += re * re + im * im
                yield
        for start in starts:
            rows = pl.ds(start, ROWS)
            for h in range(2):
                w_re, w_im = wave[0, m, h, rows], wave[1, m, h, rows]
                total[2, h, rows] += w_re * w_re + w_im * w_im
            yield

    def beside(*parts):
        live = list(parts)
        while live:
            live = [part for part in live if next(part, live) is not live]

    beside(enter(0, 0))
    for copy in later:
        copy.wait()

    def forward(j, carry):
        beside(transform(2 * j, 0), enter(2 * j + 1, 1))
        beside(transform(2 * j + 1, 1), enter(2 * j + 2, 0))
        return carry

    lax.fori_loop(0, modes // 2, forward, 0)
    misfit[...] = 2.0 * (misfit[...] - measured_ref[...])

    def restore(m, side):
        for e in range(2):
            for start in range(0, HALF, ROWS):
                scale = misfit[pl.ds(HALF * e + start, ROWS)]
                for q in range(2):
                    rows = pl.ds(HALF * q + start, ROWS)
                    put(along[side], (e,), rows, scale * far[m, e, rows])
                yield
        even = left_dot(row_tab, 2, along[side], 0)
        yield
        odd = left_dot(row_tab, 3, along[side], 1)
        yield
        for start in range(0, HALF, ROWS):
            re, im = slice(start, start + ROWS), slice(HALF + start, HALF + start + ROWS)
            for n in range(2):
                f_re = even[re] + odd[re] if n == 0 else even[re] - odd[re]
                f_im = even[im] + odd[im] if n == 0 else even[im] - odd[im]
                rows = pl.ds(HALF * n + start, ROWS)
                for q in range(2):
                    lanes = slice(HALF * q, HALF * (q + 1))
                    put(
                        across[side],
                        (q,),
                        rows,
                        jnp.concatenate([f_re[:, lanes], f_im[:, lanes]], axis=1),
                    )
            yield
        first = right_dot(across[side], 0, col_tab, 2)
        yield
        second = right_dot(across[side], 1, col_tab, 3)
        yield
        for start in starts:
            rows, inner = pl.ds(start, ROWS), pl.ds(start + PAD, ROWS)
            part = slice(start, start + ROWS)
            for h in range(2):
                both = first[part] + second[part] if h == 0 else first[part] - second[part]
                b_re, b_im = both[:, :HALF], both[:, HALF:]
                w_re, w_im = wave[0, m, h, rows], wave[1, m, h, rows]
                total[0, h, rows] += w_re * b_re + w_im * b_im
                total[1, h, rows] += w_re * b_im - w_im * b_re
                t_re, t_im = trans[1, 0, h, rows], trans[1, 1, h, rows]
                field[side, 0, h, inner] = t_re * b_re + t_im * b_im
                field[side, 1, h, inner] = t_re * b_im - t_im * b_re
            yield

    def leave(m, side):
        for start in starts:
            turn_rows(field.at[side], turned, start, -1.0)
            yield
        for start in starts:
            rows = pl.ds(start, ROWS)
            for h, (d_re, d_im) in enumerate(end_rows(field.at[side], turned, start)):
                p_re, p_im = probe[0, m, h, rows], probe[1, m, h, rows]
                total[3, h, rows] += p_re * d_re + p_im * d_im
                total[4, h, rows] += p_re * d_im - p_im * d_re
            yield

    beside(restore(0, 0))

    def backward(j, carry):
        beside(restore(2 * j + 1, 1), leave(2 * j, 0))
        beside(restore(2 * j + 2, 0), leave(2 * j + 1, 1))
        return carry

    lax.fori_loop(0, modes // 2, backward, 0)

    for k in range(5):
        for h in range(2):
            hold[h, :SIDE] = total[k, h]
            hold[h, SIDE:] = total[k, h]
        for n in range(SIDE // 8):
            rows = pl.ds(SIDE - r + 8 * n, 8)
            block = jnp.concatenate([hold[0, rows], hold[1, rows]], axis=1)
            block = pltpu.roll(block, c, 1)
            for h in range(2):
                out_ref[n % 16, 4 * k + 2 * h + n // 16] = block[:, h * HALF : (h + 1) * HALF]
    lane = lax.broadcasted_iota(jnp.int32, (8, HALF), 1)
    mark = jnp.where(lane == 0, r, c).astype(f32)
    for i in range(SCANS):
        out_ref[i, 20] = mark


def glow_kernel(probe_ref, measured_ref, light_ref, expected_ref, halves_ref):
    @pl.when(pl.program_id(0) == 0)
    def _():
        light_ref[...] = jnp.zeros_like(light_ref)
        row = lax.broadcasted_iota(jnp.int32, (SIDE, SIDE), 0)
        col = lax.broadcasted_iota(jnp.int32, (SIDE, SIDE), 1)
        place = lambda k: jnp.where(k < HALF, 2 * k, 2 * (k - HALF) + 1)
        by_col = (row == place(col)).astype(f32).astype(bf16)
        by_row = (col == place(row)).astype(f32).astype(bf16)
        value = measured_ref[...]
        for left in (False, True):
            high, low = split(value)
            rest = (value - high.astype(f32) - low.astype(f32)).astype(bf16)
            if left:
                value = mul(by_row, high) + mul(by_row, low) + mul(by_row, rest)
            else:
                value = mul(high, by_col) + mul(low, by_col) + mul(rest, by_col)
        expected_ref[...] = value

    for p in range(2):
        for h in range(2):
            halves_ref[p, 0, h] = probe_ref[p, 0, :, h * HALF : (h + 1) * HALF]
    light = probe_ref[0, 0] * probe_ref[0, 0] + probe_ref[1, 0] * probe_ref[1, 0]
    light_ref[:SIDE] += light
    light_ref[SIDE:] += light


def run_glow(probe, measured):
    modes = probe.shape[1]
    return pl.pallas_call(
        glow_kernel,
        grid=(modes,),
        out_shape=(
            jax.ShapeDtypeStruct((2 * SIDE, SIDE), f32),
            jax.ShapeDtypeStruct((SIDE, SIDE), f32),
            jax.ShapeDtypeStruct((2, modes, 2, SIDE, HALF), f32),
        ),
        in_specs=[
            pl.BlockSpec((2, 1, SIDE, SIDE), lambda m: (0, m, 0, 0)),
            pl.BlockSpec((SIDE, SIDE), lambda m: (0, 0)),
        ],
        out_specs=(
            pl.BlockSpec((2 * SIDE, SIDE), lambda m: (0, 0)),
            pl.BlockSpec((SIDE, SIDE), lambda m: (0, 0)),
            pl.BlockSpec((2, 1, 2, SIDE, HALF), lambda m: (0, m, 0, 0, 0)),
        ),
        compiler_params=pltpu.CompilerParams(vmem_limit_bytes=10 * 1024 * 1024),
        cost_estimate=pl.CostEstimate(
            flops=4 * modes * SIDE * SIDE, bytes_accessed=8 * modes * SIDE * SIDE, transcendentals=0
        ),
        name="glow",
    )(probe, measured)


def cut_kernel(me_ref, object_ref, below_ref, right_ref, diag_ref, sems):
    core = lax.rem(me_ref[0], 2)
    copies = []
    for s in range(LAYERS):
        plane = object_ref.at[s, core]
        near = pl.ds(0, HALF)
        for n, (source, target) in enumerate(
            [
                (plane.at[near, :], below_ref.at[s]),
                (plane.at[:, near], right_ref.at[s]),
                (plane.at[near, near], diag_ref.at[s]),
            ]
        ):
            copies.append(pltpu.make_async_copy(source, target, sems.at[s, n]))
    for copy in copies:
        copy.start()
    for copy in copies:
        copy.wait()


def run_cut(me, current):
    far = pl.BlockSpec(memory_space=pl.ANY)
    return pl.pallas_call(
        cut_kernel,
        out_shape=(
            jax.ShapeDtypeStruct((LAYERS, HALF, SIDE), f32),
            jax.ShapeDtypeStruct((LAYERS, SIDE, HALF), f32),
            jax.ShapeDtypeStruct((LAYERS, HALF, HALF), f32),
        ),
        in_specs=[pl.BlockSpec(memory_space=pltpu.SMEM), far],
        out_specs=(pl.BlockSpec(memory_space=pltpu.VMEM),) * 3,
        scratch_shapes=[pltpu.SemaphoreType.DMA((LAYERS, 3))],
        compiler_params=pltpu.CompilerParams(vmem_limit_bytes=4 * 1024 * 1024),
        name="cut",
    )(me, current)


def run_wave(corner, me, own, rims, probe, measured):
    right_table, left_table = make_tables()
    modes = probe.shape[1]
    vmem = pl.BlockSpec(memory_space=pltpu.VMEM)
    field = (2, SIDE, HALF)
    wide = (2, 2, SIDE + 2 * PAD, HALF)
    return pl.pallas_call(
        wave_kernel,
        out_shape=jax.ShapeDtypeStruct((SCANS, 21, 8, HALF), f32),
        in_specs=[pl.BlockSpec(memory_space=pltpu.SMEM)] * 2
        + [pl.BlockSpec(memory_space=pl.ANY)] * 7
        + [vmem]
        + [pl.BlockSpec(memory_space=pl.ANY)] * 3,
        out_specs=vmem,
        scratch_shapes=[
            pltpu.VMEM((LAYERS, 2, SIDE, SIDE), f32),
            pltpu.VMEM((SIDE, SIDE), f32),
            pltpu.VMEM((4, 3 * SIDE, SIDE), bf16),
            pltpu.VMEM((4, SIDE, 3 * SIDE), bf16),
            pltpu.VMEM((2, 2 * SIDE, HALF), f32),
            pltpu.VMEM((LAYERS, 2) + field, f32),
            pltpu.VMEM((2, modes + 1) + field, f32),
            pltpu.VMEM((modes + 1, 2, SIDE, SIDE), f32),
            pltpu.VMEM((SIDE, SIDE), f32),
            pltpu.VMEM((5,) + field, f32),
            pltpu.SemaphoreType.DMA((4,)),
            pltpu.VMEM((2,) + wide, f32),
            pltpu.VMEM(wide, f32),
            pltpu.VMEM((2, 2, SIDE, SIDE), bf16),
            pltpu.VMEM((2, 2, SIDE, SIDE), bf16),
            pltpu.VMEM((2, 2, SIDE, SIDE), bf16),
            pltpu.VMEM((2, 2, SIDE, SIDE), bf16),
            pltpu.VMEM((2, LAYERS, HALF, SIDE), f32),
            pltpu.VMEM((2, LAYERS, SIDE, HALF), f32),
            pltpu.VMEM((2, LAYERS, HALF, HALF), f32),
            pltpu.SemaphoreType.DMA((2, 3)),
        ],
        compiler_params=pltpu.CompilerParams(vmem_limit_bytes=36 * 1024 * 1024),
        name="wave",
    )(
        corner,
        me,
        *rims,
        own,
        probe,
        measured,
        jnp.asarray(right_table),
        jnp.asarray(left_table),
    )


def sum_kernel(
    me_ref, parts_ref, light_ref, own_ref, right_ref, below_ref, diag_ref, marks_ref, sem
):
    me = me_ref[0]
    copy = pltpu.make_async_copy(parts_ref.at[:, 20], marks_ref, sem)
    copy.start()
    own_ref[...] = jnp.zeros_like(own_ref)
    right_ref[...] = jnp.zeros_like(right_ref)
    below_ref[...] = jnp.zeros_like(below_ref)
    diag_ref[...] = jnp.zeros_like(diag_ref)
    sub = lax.broadcasted_iota(jnp.int32, (2, 8, SIDE), 1)
    side = lax.broadcasted_iota(jnp.int32, (2, 8, SIDE), 0)
    cols = lax.broadcasted_iota(jnp.int32, (2, 8, SIDE), 2)
    rows = HALF * side + 8 * me + sub
    copy.wait()
    for j in range(SCANS):
        r = marks_ref[j, 0, 0].astype(jnp.int32)
        c = marks_ref[j, 0, 1].astype(jnp.int32)
        lights = []
        for h in range(2):
            start = lax.rem(HALF * h + 8 * me + SIDE - r, SIDE)
            base = pl.multiple_of((start // 8) * 8, 8)
            block = light_ref[pl.ds(base, 16), :]
            block = pltpu.roll(block, lax.rem(16 - (start - base), 16), 0)[:8]
            lights.append(pltpu.roll(block, c, 1)[None])
        light = jnp.concatenate(lights, axis=0)
        inside_row, inside_col = rows >= r, cols >= c
        for k in range(6):
            value = light
            if k < 5:
                halves = [parts_ref[j, 4 * k + 2 * h : 4 * k + 2 * h + 2] for h in range(2)]
                value = jnp.concatenate(halves, axis=2)
            here = jnp.where(inside_row, value, 0.0)
            there = (value - here)[0]
            own_ref[k] += jnp.where(inside_col, here, 0.0)
            right_ref[k] += jnp.where(inside_col, 0.0, here)[:, :, :HALF]
            below_ref[k] += jnp.where(inside_col[0], there, 0.0)
            diag_ref[k] += jnp.where(inside_col[0], 0.0, there)[:, :HALF]


def run_sum(me, parts, light):
    smem = pl.BlockSpec(memory_space=pltpu.SMEM)
    vmem = pl.BlockSpec(memory_space=pltpu.VMEM)
    return pl.pallas_call(
        sum_kernel,
        out_shape=(
            jax.ShapeDtypeStruct((6, 2, 8, SIDE), f32),
            jax.ShapeDtypeStruct((6, 2, 8, HALF), f32),
            jax.ShapeDtypeStruct((6, 8, SIDE), f32),
            jax.ShapeDtypeStruct((6, 8, HALF), f32),
        ),
        in_specs=[smem, vmem, vmem],
        out_specs=(vmem,) * 4,
        scratch_shapes=[pltpu.SMEM((SCANS, 8, HALF), f32), pltpu.SemaphoreType.DMA],
        compiler_params=pltpu.CompilerParams(vmem_limit_bytes=8 * 1024 * 1024),
        name="sum",
    )(me, parts, light)


def update_kernel(me_ref, object_ref, own_ref, right_ref, below_ref, diag_ref, out_ref):
    me = me_ref[0]
    sums = []
    for k in range(6):
        near = own_ref[k, :, :, :HALF] + right_ref[k]
        whole = jnp.concatenate([near, own_ref[k, :, :, HALF:]], axis=2)
        low = jnp.concatenate(
            [below_ref[k, :, :HALF] + diag_ref[k], below_ref[k, :, HALF:]], axis=1
        )
        sums.append([whole[0] + low, whole[1]])
    for s in range(LAYERS):
        base = 3 * (1 - s)
        for h in range(2):
            scale = step_size / (sums[base + 2][h] + 1.0)
            start = pl.multiple_of(HALF * h + 8 * me, 8)
            for p in range(2):
                out_ref[s, p, h] = (
                    object_ref[s, p, pl.ds(start, 8), :] - scale * sums[base + p][h]
                )


def run_update(me, current, own, right, below, diag):
    smem = pl.BlockSpec(memory_space=pltpu.SMEM)
    vmem = pl.BlockSpec(memory_space=pltpu.VMEM)
    return pl.pallas_call(
        update_kernel,
        out_shape=jax.ShapeDtypeStruct((LAYERS, 2, 2, 8, SIDE), f32),
        in_specs=[smem] + [vmem] * 5,
        out_specs=vmem,
        compiler_params=pltpu.CompilerParams(vmem_limit_bytes=4 * 1024 * 1024),
        name="update",
    )(me, current, own, right, below, diag)


def place_kernel(me_ref, *refs):
    blocks, out_ref = refs[:-1], refs[-1]
    me = me_ref[0]
    y, z, core = me // 4, lax.rem(me // 2, 2), lax.rem(me, 2)
    count = 0
    for ref in blocks:
        for b in range(ref.shape[0]):
            dc, dy, dz = count // 8, (count // 2) % 4, count % 2
            i = lax.rem(y + 4 - dy, 4) * 4 + lax.rem(z + dz, 2) * 2 + lax.rem(core + dc, 2)
            for h in range(2):
                start = pl.multiple_of(HALF * h + 8 * i, 8)
                out_ref[:, :, pl.ds(start, 8), :] = ref[b, :, :, h]
            count += 1


def run_place(me, blocks):
    vmem = pl.BlockSpec(memory_space=pltpu.VMEM)
    return pl.pallas_call(
        place_kernel,
        out_shape=jax.ShapeDtypeStruct((LAYERS, 2, SIDE, SIDE), f32),
        in_specs=[pl.BlockSpec(memory_space=pltpu.SMEM)] + [vmem] * len(blocks),
        out_specs=vmem,
        compiler_params=pltpu.CompilerParams(vmem_limit_bytes=8 * 1024 * 1024),
        name="place",
    )(me, *blocks)


def shift(array, axis, by):
    count = lax.axis_size(axis)
    pairs = [(i, i + by) for i in range(count) if 0 <= i + by < count]
    return lax.ppermute(array, axis, pairs)


def shift_both(array, by):
    n_x, n_y = lax.axis_size("tx"), lax.axis_size("ty")
    pairs = [
        (a * n_y + b, (a + by) * n_y + b + by)
        for a in range(n_x)
        for b in range(n_y)
        if 0 <= a + by < n_x and 0 <= b + by < n_y
    ]
    return lax.ppermute(array, ("tx", "ty"), pairs)


def along_scan(array, dy, dz, dc):
    pairs = []
    for i in range(SCANS):
        y, z, core = i // 4, (i // 2) % 2, i % 2
        pairs.append((i, ((y + dy) % 4) * 4 + ((z + dz) % 2) * 2 + (core + dc) % 2))
    return lax.ppermute(array, "scan", pairs)


def on_device(object_slices, probe_modes, corners, measured):
    me = lax.axis_index("scan").astype(jnp.int32).reshape(1)
    corner = corners.reshape(2)
    rims = run_cut(me, object_slices)
    diag = shift_both(rims[2], -1)
    rims = (shift(rims[0], "tx", -1), shift(rims[1], "ty", -1), diag)
    light, expected, halves = run_glow(probe_modes, measured.reshape(SIDE, SIDE))
    rims, light, expected, halves = lax.optimization_barrier((rims, light, expected, halves))
    others = tuple(along_scan(rim, 0, 0, 1) for rim in rims)

    parts = run_wave(
        corner,
        me,
        object_slices,
        rims + others,
        halves,
        expected,
    )
    parts = lax.all_to_all(parts, "scan", 0, 0)
    own, to_right, to_below, to_diag = run_sum(me, parts, light)
    to_right = shift(to_right, "ty", 1)
    to_below = shift(to_below, "tx", 1)
    to_diag = shift_both(to_diag, 1)
    mine = run_update(me, object_slices, own, to_right, to_below, to_diag)[None]
    pair = jnp.concatenate([mine, along_scan(mine, 0, 1, 0)], axis=0)
    ring = [pair] + [along_scan(pair, dy, 0, 0) for dy in (1, 2, 3)]
    return run_place(me, ring + [along_scan(block, 0, 0, 1) for block in ring])


def solution(mesh):
    placed = (
        P(None, None, "tx", "ty"),
        P(),
        P("tx", "ty", "scan", None),
        P("tx", "ty", "scan", None, None),
    )
    return jax.shard_map(
        on_device, mesh=mesh, in_specs=placed, out_specs=P(None, None, "tx", "ty"), check_vma=False
    )
```

```python
import functools
import math

import jax
import jax.numpy as jnp
import numpy as np
from jax import lax
from jax.experimental import pallas as pl
from jax.experimental.pallas import tpu as pltpu
from jax.sharding import PartitionSpec as P

fresnel_coef = 0.1
step_size = 4.0
SIDE = 256
HALF = 128
LAYERS = 2
SCANS = 16
ROWS = 32
PAD = 8
f32 = jnp.float32
bf16 = jnp.bfloat16


def real_right(table):
    return np.block([[table.real, table.imag], [-table.imag, table.real]])


def real_left(table):
    return np.block([[table.real, -table.imag], [table.imag, table.real]])


def stacked(table, axis):
    high = table.astype(np.float32).astype(bf16)
    low = (table - high.astype(np.float64)).astype(np.float32).astype(bf16)
    return np.concatenate([high, high, low], axis=axis)


def make_tables():
    half = np.arange(HALF)
    col_even = np.exp(-2j * np.pi * np.outer(half, half) / HALF) / 16
    col_odd = np.exp(-2j * np.pi * np.outer(half, 2 * half + 1) / SIDE) / 16
    row_even, row_odd = col_even.T, col_odd.T
    right = [col_even, col_odd, col_even.conj().T, col_odd.conj().T]
    left = [row_even, row_odd, row_even.conj().T, row_odd.conj().T]
    right = np.stack([stacked(real_right(t), 0) for t in right])
    left = np.stack([stacked(real_left(t), 1) for t in left])
    return right, left


def split(value):
    high = value.astype(bf16)
    return high, (value - high.astype(f32)).astype(bf16)


def mul(first, second):
    return jnp.dot(first, second, preferred_element_type=f32)


def put(ref, lead, rows, value):
    high, low = split(value)
    ref[lead + (0, rows)] = high
    ref[lead + (1, rows)] = low


def right_dot(ref, side, table, which):
    high, low = ref[side, 0], ref[side, 1]
    return mul(jnp.concatenate([high, low, high], axis=1), table[which])


def left_dot(table, which, ref, side):
    high, low = ref[side, 0], ref[side, 1]
    return mul(table[which], jnp.concatenate([high, low, high], axis=0))


def neighbours(ref, p, start):
    rows = lambda by: pl.ds(start + PAD + by, ROWS)
    low, high = ref[p, 0, rows(0)], ref[p, 1, rows(0)]
    lane = lax.broadcasted_iota(jnp.int32, low.shape, 1)
    first, last = lane == 0, lane == HALF - 1
    low_up, high_up = pltpu.roll(low, 1, 1), pltpu.roll(high, 1, 1)
    low_down, high_down = pltpu.roll(low, HALF - 1, 1), pltpu.roll(high, HALF - 1, 1)
    low_sum = jnp.where(first, 0.0, low_up) + jnp.where(last, high_down, low_down)
    high_sum = jnp.where(first, low_up, high_up) + jnp.where(last, 0.0, high_down)
    return (
        low_sum + (ref[p, 0, rows(-1)] + ref[p, 0, rows(1)]),
        high_sum + (ref[p, 1, rows(-1)] + ref[p, 1, rows(1)]),
    )


damping = 0.5 * fresnel_coef**2


def turn_rows(source, target, start, sign):
    turn = sign * fresnel_coef
    rows = pl.ds(start + PAD, ROWS)
    near_re, near_im = neighbours(source, 0, start), neighbours(source, 1, start)
    for h in range(2):
        re, im = source[0, h, rows], source[1, h, rows]
        target[0, h, rows] = 4.0 * damping * re - turn * im - damping * near_re[h]
        target[1, h, rows] = 4.0 * damping * im + turn * re - damping * near_im[h]


def end_rows(source, target, start):
    rows = pl.ds(start + PAD, ROWS)
    near = [neighbours(target, p, start) for p in range(2)]
    return [
        [source[p, h, rows] - 4.0 * target[p, h, rows] + near[p][h] for p in range(2)]
        for h in range(2)
    ]


def wave_kernel(
    corner_ref,
    me_ref,
    below_far,
    right_far,
    diag_far,
    other_below_far,
    other_right_far,
    other_diag_far,
    own_far,
    probe,
    measured_far,
    col_far,
    row_far,
    out_ref,
    own_ref,
    measured_ref,
    col_tab,
    row_tab,
    hold,
    trans,
    wave,
    far,
    misfit,
    total,
    more_sems,
    field,
    turned,
    across_0,
    across_1,
    along_0,
    along_1,
    below_ref,
    right_ref,
    diag_ref,
    rim_sems,
):
    across, along = (across_0, across_1), (along_0, along_1)
    r, c = corner_ref[0], corner_ref[1]
    modes = probe.shape[1]
    own_copy = pltpu.make_async_copy(own_far, own_ref, more_sems.at[0])
    later = [
        pltpu.make_async_copy(source, target, more_sems.at[n + 1])
        for n, (source, target) in enumerate(
            [
                (col_far, col_tab),
                (row_far, row_tab),
                (measured_far, measured_ref),
            ]
        )
    ]
    core = lax.rem(me_ref[0], 2)
    rim_copies = [
        pltpu.make_async_copy(
            source, target.at[lax.rem(core + side, 2)], rim_sems.at[side, n]
        )
        for side, sources in enumerate(
            [(below_far, right_far, diag_far), (other_below_far, other_right_far, other_diag_far)]
        )
        for n, (source, target) in enumerate(zip(sources, (below_ref, right_ref, diag_ref)))
    ]
    own_copy.start()
    for copy in rim_copies:
        copy.start()
    for copy in later:
        copy.start()
    rows = lax.broadcasted_iota(jnp.int32, (SIDE, SIDE), 0)
    cols = lax.broadcasted_iota(jnp.int32, (SIDE, SIDE), 1)
    top = rows[:HALF] < r
    near = cols[:, :HALF] < c
    back_c = lax.rem(SIDE - c, SIDE)
    own_copy.wait()
    for copy in rim_copies:
        copy.wait()
    for s in range(LAYERS):
        for p in range(2):
            right, below, diag = right_ref[p, s], below_ref[p, s], diag_ref[p, s]
            left = jnp.where(near, right, own_ref[s, p, :, :HALF])
            whole = jnp.concatenate([left, own_ref[s, p, :, HALF:]], axis=1)
            lower = jnp.concatenate(
                [jnp.where(near[:HALF], diag, below[:, :HALF]), below[:, HALF:]], axis=1
            )
            whole = jnp.concatenate([jnp.where(top, lower, whole[:HALF]), whole[HALF:]], axis=0)
            whole = pltpu.roll(whole, back_c, 1)
            for half in range(2):
                hold[0, half * SIDE : (half + 1) * SIDE] = whole[:, :HALF]
                hold[1, half * SIDE : (half + 1) * SIDE] = whole[:, HALF:]
            for h in range(2):
                view = hold[h, pl.ds(r, SIDE)]
                trans[s, p, h] = view + 1.0 if p == 0 else view

    misfit[...] = jnp.zeros_like(misfit)
    total[...] = jnp.zeros_like(total)
    field[...] = jnp.zeros_like(field)
    turned[...] = jnp.zeros_like(turned)
    starts = range(0, SIDE, ROWS)

    def enter(m, side):
        for start in starts:
            rows, inner = pl.ds(start, ROWS), pl.ds(start + PAD, ROWS)
            for h in range(2):
                p_re, p_im = probe[0, m, h, rows], probe[1, m, h, rows]
                t_re, t_im = trans[0, 0, h, rows], trans[0, 1, h, rows]
                field[side, 0, h, inner] = p_re * t_re - p_im * t_im
                field[side, 1, h, inner] = p_re * t_im + p_im * t_re
            yield
        for start in starts:
            turn_rows(field.at[side], turned, start, 1.0)
            yield
        for start in starts:
            rows = pl.ds(start, ROWS)
            x = []
            for h, (w_re, w_im) in enumerate(end_rows(field.at[side], turned, start)):
                wave[0, m, h, rows] = w_re
                wave[1, m, h, rows] = w_im
                t_re, t_im = trans[1, 0, h, rows], trans[1, 1, h, rows]
                x.append(
                    jnp.concatenate([w_re * t_re - w_im * t_im, w_re * t_im + w_im * t_re], axis=1)
                )
            put(across[side], (0,), rows, x[0] + x[1])
            put(across[side], (1,), rows, x[0] - x[1])
            yield

    def transform(m, side):
        even = right_dot(across[side], 0, col_tab, 0)
        yield
        odd = right_dot(across[side], 1, col_tab, 1)
        yield
        for start in range(0, HALF, ROWS):
            for q in range(2):
                lanes = slice(HALF * q, HALF * (q + 1))
                above, under = [
                    jnp.concatenate([even[part, lanes], odd[part, lanes]], axis=1)
                    for part in (slice(start, start + ROWS), slice(start + HALF, start + HALF + ROWS))
                ]
                rows = pl.ds(HALF * q + start, ROWS)
                put(along[side], (0,), rows, above + under)
                put(along[side], (1,), rows, above - under)
            yield
        for e in range(2):
            found = left_dot(row_tab, e, along[side], e)
            yield
            for start in range(0, HALF, ROWS):
                re, im = found[start : start + ROWS], found[HALF + start : HALF + start + ROWS]
                far[m, e, pl.ds(start, ROWS)] = re
                far[m, e, pl.ds(HALF + start, ROWS)] = im
                misfit[pl.ds(HALF * e + start, ROWS)] += re * re + im * im
                yield
        for start in starts:
            rows = pl.ds(start, ROWS)
            for h in range(2):
                w_re, w_im = wave[0, m, h, rows], wave[1, m, h, rows]
                total[2, h, rows] += w_re * w_re + w_im * w_im
            yield

    def beside(*parts):
        live = list(parts)
        while live:
            live = [part for part in live if next(part, live) is not live]

    beside(enter(0, 0))
    for copy in later:
        copy.wait()

    def forward(j, carry):
        beside(transform(2 * j, 0), enter(2 * j + 1, 1))
        beside(transform(2 * j + 1, 1), enter(2 * j + 2, 0))
        return carry

    lax.fori_loop(0, modes // 2 - 1, forward, 0)
    beside(transform(modes - 2, 0), enter(modes - 1, 1))
    beside(transform(modes - 1, 1))
    misfit[...] = 2.0 * (misfit[...] - measured_ref[...])

    def restore(m, side):
        for e in range(2):
            for start in range(0, HALF, ROWS):
                scale = misfit[pl.ds(HALF * e + start, ROWS)]
                for q in range(2):
                    rows = pl.ds(HALF * q + start, ROWS)
                    put(along[side], (e,), rows, scale * far[m, e, rows])
                yield
        even = left_dot(row_tab, 2, along[side], 0)
        yield
        odd = left_dot(row_tab, 3, along[side], 1)
        yield
        for start in range(0, HALF, ROWS):
            re, im = slice(start, start + ROWS), slice(HALF + start, HALF + start + ROWS)
            for n in range(2):
                f_re = even[re] + odd[re] if n == 0 else even[re] - odd[re]
                f_im = even[im] + odd[im] if n == 0 else even[im] - odd[im]
                rows = pl.ds(HALF * n + start, ROWS)
                for q in range(2):
                    lanes = slice(HALF * q, HALF * (q + 1))
                    put(
                        across[side],
                        (q,),
                        rows,
                        jnp.concatenate([f_re[:, lanes], f_im[:, lanes]], axis=1),
                    )
            yield
        first = right_dot(across[side], 0, col_tab, 2)
        yield
        second = right_dot(across[side], 1, col_tab, 3)
        yield
        for start in starts:
            rows, inner = pl.ds(start, ROWS), pl.ds(start + PAD, ROWS)
            part = slice(start, start + ROWS)
            for h in range(2):
                both = first[part] + second[part] if h == 0 else first[part] - second[part]
                b_re, b_im = both[:, :HALF], both[:, HALF:]
                w_re, w_im = wave[0, m, h, rows], wave[1, m, h, rows]
                total[0, h, rows] += w_re * b_re + w_im * b_im
                total[1, h, rows] += w_re * b_im - w_im * b_re
                t_re, t_im = trans[1, 0, h, rows], trans[1, 1, h, rows]
                field[side, 0, h, inner] = t_re * b_re + t_im * b_im
                field[side, 1, h, inner] = t_re * b_im - t_im * b_re
            yield

    def leave(m, side):
        for start in starts:
            turn_rows(field.at[side], turned, start, -1.0)
            yield
        for start in starts:
            rows = pl.ds(start, ROWS)
            for h, (d_re, d_im) in enumerate(end_rows(field.at[side], turned, start)):
                p_re, p_im = probe[0, m, h, rows], probe[1, m, h, rows]
                total[3, h, rows] += p_re * d_re + p_im * d_im
                total[4, h, rows] += p_re * d_im - p_im * d_re
            yield

    def hand_out(*planes):
        for k in planes:
            for h in range(2):
                hold[h, :SIDE] = total[k, h]
                hold[h, SIDE:] = total[k, h]
                yield
            for n in range(SIDE // 8):
                rows = pl.ds(SIDE - r + 8 * n, 8)
                block = jnp.concatenate([hold[0, rows], hold[1, rows]], axis=1)
                block = pltpu.roll(block, c, 1)
                for h in range(2):
                    out_ref[n % 16, 4 * k + 2 * h + n // 16] = block[:, h * HALF : (h + 1) * HALF]
                if n % 4 == 3:
                    yield

    beside(restore(0, 0))

    def backward(j, carry):
        beside(restore(2 * j + 1, 1), leave(2 * j, 0))
        beside(restore(2 * j + 2, 0), leave(2 * j + 1, 1))
        return carry

    lax.fori_loop(0, modes // 2 - 1, backward, 0)
    beside(restore(modes - 1, 1), leave(modes - 2, 0))
    beside(leave(modes - 1, 1), hand_out(0, 1, 2))
    beside(hand_out(3, 4))

    lane = lax.broadcasted_iota(jnp.int32, (8, HALF), 1)
    mark = jnp.where(lane == 0, r, c).astype(f32)
    for i in range(SCANS):
        out_ref[i, 20] = mark


def glow_kernel(probe_ref, measured_ref, light_ref, expected_ref, halves_ref):
    @pl.when(pl.program_id(0) == 0)
    def _():
        light_ref[...] = jnp.zeros_like(light_ref)
        row = lax.broadcasted_iota(jnp.int32, (SIDE, SIDE), 0)
        col = lax.broadcasted_iota(jnp.int32, (SIDE, SIDE), 1)
        place = lambda k: jnp.where(k < HALF, 2 * k, 2 * (k - HALF) + 1)
        by_col = (row == place(col)).astype(f32).astype(bf16)
        by_row = (col == place(row)).astype(f32).astype(bf16)
        value = measured_ref[...]
        for left in (False, True):
            high, low = split(value)
            rest = (value - high.astype(f32) - low.astype(f32)).astype(bf16)
            if left:
                value = mul(by_row, high) + mul(by_row, low) + mul(by_row, rest)
            else:
                value = mul(high, by_col) + mul(low, by_col) + mul(rest, by_col)
        expected_ref[...] = value

    for p in range(2):
        for h in range(2):
            halves_ref[p, 0, h] = probe_ref[p, 0, :, h * HALF : (h + 1) * HALF]
    light = probe_ref[0, 0] * probe_ref[0, 0] + probe_ref[1, 0] * probe_ref[1, 0]
    light_ref[:SIDE] += light
    light_ref[SIDE:] += light


def run_glow(probe, measured):
    modes = probe.shape[1]
    return pl.pallas_call(
        glow_kernel,
        grid=(modes,),
        out_shape=(
            jax.ShapeDtypeStruct((2 * SIDE, SIDE), f32),
            jax.ShapeDtypeStruct((SIDE, SIDE), f32),
            jax.ShapeDtypeStruct((2, modes, 2, SIDE, HALF), f32),
        ),
        in_specs=[
            pl.BlockSpec((2, 1, SIDE, SIDE), lambda m: (0, m, 0, 0)),
            pl.BlockSpec((SIDE, SIDE), lambda m: (0, 0)),
        ],
        out_specs=(
            pl.BlockSpec((2 * SIDE, SIDE), lambda m: (0, 0)),
            pl.BlockSpec((SIDE, SIDE), lambda m: (0, 0)),
            pl.BlockSpec((2, 1, 2, SIDE, HALF), lambda m: (0, m, 0, 0, 0)),
        ),
        compiler_params=pltpu.CompilerParams(vmem_limit_bytes=10 * 1024 * 1024),
        cost_estimate=pl.CostEstimate(
            flops=4 * modes * SIDE * SIDE, bytes_accessed=8 * modes * SIDE * SIDE, transcendentals=0
        ),
        name="glow",
    )(probe, measured)


def cut_kernel(me_ref, object_ref, below_ref, right_ref, diag_ref, sems):
    core = lax.rem(me_ref[0], 2)
    copies = []
    for s in range(LAYERS):
        plane = object_ref.at[s, core]
        near = pl.ds(0, HALF)
        for n, (source, target) in enumerate(
            [
                (plane.at[near, :], below_ref.at[s]),
                (plane.at[:, near], right_ref.at[s]),
                (plane.at[near, near], diag_ref.at[s]),
            ]
        ):
            copies.append(pltpu.make_async_copy(source, target, sems.at[s, n]))
    for copy in copies:
        copy.start()
    for copy in copies:
        copy.wait()


def run_cut(me, current):
    far = pl.BlockSpec(memory_space=pl.ANY)
    return pl.pallas_call(
        cut_kernel,
        out_shape=(
            jax.ShapeDtypeStruct((LAYERS, HALF, SIDE), f32),
            jax.ShapeDtypeStruct((LAYERS, SIDE, HALF), f32),
            jax.ShapeDtypeStruct((LAYERS, HALF, HALF), f32),
        ),
        in_specs=[pl.BlockSpec(memory_space=pltpu.SMEM), far],
        out_specs=(pl.BlockSpec(memory_space=pltpu.VMEM),) * 3,
        scratch_shapes=[pltpu.SemaphoreType.DMA((LAYERS, 3))],
        compiler_params=pltpu.CompilerParams(vmem_limit_bytes=4 * 1024 * 1024),
        name="cut",
    )(me, current)


def run_wave(corner, me, own, rims, probe, measured):
    right_table, left_table = make_tables()
    modes = probe.shape[1]
    vmem = pl.BlockSpec(memory_space=pltpu.VMEM)
    field = (2, SIDE, HALF)
    wide = (2, 2, SIDE + 2 * PAD, HALF)
    return pl.pallas_call(
        wave_kernel,
        out_shape=jax.ShapeDtypeStruct((SCANS, 21, 8, HALF), f32),
        in_specs=[pl.BlockSpec(memory_space=pltpu.SMEM)] * 2
        + [pl.BlockSpec(memory_space=pl.ANY)] * 7
        + [vmem]
        + [pl.BlockSpec(memory_space=pl.ANY)] * 3,
        out_specs=vmem,
        scratch_shapes=[
            pltpu.VMEM((LAYERS, 2, SIDE, SIDE), f32),
            pltpu.VMEM((SIDE, SIDE), f32),
            pltpu.VMEM((4, 3 * SIDE, SIDE), bf16),
            pltpu.VMEM((4, SIDE, 3 * SIDE), bf16),
            pltpu.VMEM((2, 2 * SIDE, HALF), f32),
            pltpu.VMEM((LAYERS, 2) + field, f32),
            pltpu.VMEM((2, modes) + field, f32),
            pltpu.VMEM((modes, 2, SIDE, SIDE), f32),
            pltpu.VMEM((SIDE, SIDE), f32),
            pltpu.VMEM((5,) + field, f32),
            pltpu.SemaphoreType.DMA((4,)),
            pltpu.VMEM((2,) + wide, f32),
            pltpu.VMEM(wide, f32),
            pltpu.VMEM((2, 2, SIDE, SIDE), bf16),
            pltpu.VMEM((2, 2, SIDE, SIDE), bf16),
            pltpu.VMEM((2, 2, SIDE, SIDE), bf16),
            pltpu.VMEM((2, 2, SIDE, SIDE), bf16),
            pltpu.VMEM((2, LAYERS, HALF, SIDE), f32),
            pltpu.VMEM((2, LAYERS, SIDE, HALF), f32),
            pltpu.VMEM((2, LAYERS, HALF, HALF), f32),
            pltpu.SemaphoreType.DMA((2, 3)),
        ],
        compiler_params=pltpu.CompilerParams(vmem_limit_bytes=36 * 1024 * 1024),
        name="wave",
    )(
        corner,
        me,
        *rims,
        own,
        probe,
        measured,
        jnp.asarray(right_table),
        jnp.asarray(left_table),
    )


def sum_kernel(
    me_ref, parts_ref, light_ref, own_ref, right_ref, below_ref, diag_ref, marks_ref, sem
):
    me = me_ref[0]
    copy = pltpu.make_async_copy(parts_ref.at[:, 20, pl.ds(0, 1)], marks_ref, sem)
    copy.start()
    own_ref[...] = jnp.zeros_like(own_ref)
    right_ref[...] = jnp.zeros_like(right_ref)
    below_ref[...] = jnp.zeros_like(below_ref)
    diag_ref[...] = jnp.zeros_like(diag_ref)
    sub = lax.broadcasted_iota(jnp.int32, (2, 8, SIDE), 1)
    side = lax.broadcasted_iota(jnp.int32, (2, 8, SIDE), 0)
    cols = lax.broadcasted_iota(jnp.int32, (2, 8, SIDE), 2)
    rows = HALF * side + 8 * me + sub
    copy.wait()
    for j in range(SCANS):
        r = marks_ref[j, 0, 0].astype(jnp.int32)
        c = marks_ref[j, 0, 1].astype(jnp.int32)
        lights = []
        for h in range(2):
            start = lax.rem(HALF * h + 8 * me + SIDE - r, SIDE)
            base = pl.multiple_of((start // 8) * 8, 8)
            block = light_ref[pl.ds(base, 16), :]
            block = pltpu.roll(block, lax.rem(16 - (start - base), 16), 0)[:8]
            lights.append(pltpu.roll(block, c, 1)[None])
        light = jnp.concatenate(lights, axis=0)
        inside_row, inside_col = rows >= r, cols >= c
        for k in range(6):
            value = light
            if k < 5:
                halves = [parts_ref[j, 4 * k + 2 * h : 4 * k + 2 * h + 2] for h in range(2)]
                value = jnp.concatenate(halves, axis=2)
            here = jnp.where(inside_row, value, 0.0)
            there = (value - here)[0]
            own_ref[k] += jnp.where(inside_col, here, 0.0)
            right_ref[k] += jnp.where(inside_col, 0.0, here)[:, :, :HALF]
            below_ref[k] += jnp.where(inside_col[0], there, 0.0)
            diag_ref[k] += jnp.where(inside_col[0], 0.0, there)[:, :HALF]


def run_sum(me, parts, light):
    smem = pl.BlockSpec(memory_space=pltpu.SMEM)
    vmem = pl.BlockSpec(memory_space=pltpu.VMEM)
    return pl.pallas_call(
        sum_kernel,
        out_shape=(
            jax.ShapeDtypeStruct((6, 2, 8, SIDE), f32),
            jax.ShapeDtypeStruct((6, 2, 8, HALF), f32),
            jax.ShapeDtypeStruct((6, 8, SIDE), f32),
            jax.ShapeDtypeStruct((6, 8, HALF), f32),
        ),
        in_specs=[smem, vmem, vmem],
        out_specs=(vmem,) * 4,
        scratch_shapes=[pltpu.SMEM((SCANS, 1, HALF), f32), pltpu.SemaphoreType.DMA],
        compiler_params=pltpu.CompilerParams(vmem_limit_bytes=8 * 1024 * 1024),
        name="sum",
    )(me, parts, light)


def update_kernel(me_ref, object_ref, own_ref, right_ref, below_ref, diag_ref, out_ref):
    me = me_ref[0]
    sums = []
    for k in range(6):
        near = own_ref[k, :, :, :HALF] + right_ref[k]
        whole = jnp.concatenate([near, own_ref[k, :, :, HALF:]], axis=2)
        low = jnp.concatenate(
            [below_ref[k, :, :HALF] + diag_ref[k], below_ref[k, :, HALF:]], axis=1
        )
        sums.append([whole[0] + low, whole[1]])
    for s in range(LAYERS):
        base = 3 * (1 - s)
        for h in range(2):
            scale = step_size / (sums[base + 2][h] + 1.0)
            start = pl.multiple_of(HALF * h + 8 * me, 8)
            for p in range(2):
                out_ref[s, p, h] = (
                    object_ref[s, p, pl.ds(start, 8), :] - scale * sums[base + p][h]
                )


def run_update(me, current, own, right, below, diag):
    smem = pl.BlockSpec(memory_space=pltpu.SMEM)
    vmem = pl.BlockSpec(memory_space=pltpu.VMEM)
    return pl.pallas_call(
        update_kernel,
        out_shape=jax.ShapeDtypeStruct((LAYERS, 2, 2, 8, SIDE), f32),
        in_specs=[smem] + [vmem] * 5,
        out_specs=vmem,
        compiler_params=pltpu.CompilerParams(vmem_limit_bytes=4 * 1024 * 1024),
        name="update",
    )(me, current, own, right, below, diag)


def place_kernel(me_ref, *refs):
    blocks, out_ref = refs[:-1], refs[-1]
    me = me_ref[0]
    y, z, core = me // 4, lax.rem(me // 2, 2), lax.rem(me, 2)
    count = 0
    for ref in blocks:
        for b in range(ref.shape[0]):
            dc, dy, dz = count // 8, (count // 2) % 4, count % 2
            i = lax.rem(y + 4 - dy, 4) * 4 + lax.rem(z + dz, 2) * 2 + lax.rem(core + dc, 2)
            for h in range(2):
                start = pl.multiple_of(HALF * h + 8 * i, 8)
                out_ref[:, :, pl.ds(start, 8), :] = ref[b, :, :, h]
            count += 1


def run_place(me, blocks):
    vmem = pl.BlockSpec(memory_space=pltpu.VMEM)
    return pl.pallas_call(
        place_kernel,
        out_shape=jax.ShapeDtypeStruct((LAYERS, 2, SIDE, SIDE), f32),
        in_specs=[pl.BlockSpec(memory_space=pltpu.SMEM)] + [vmem] * len(blocks),
        out_specs=vmem,
        compiler_params=pltpu.CompilerParams(vmem_limit_bytes=8 * 1024 * 1024),
        name="place",
    )(me, *blocks)


def shift(array, axis, by):
    count = lax.axis_size(axis)
    pairs = [(i, i + by) for i in range(count) if 0 <= i + by < count]
    return lax.ppermute(array, axis, pairs)


def shift_both(array, by):
    n_x, n_y = lax.axis_size("tx"), lax.axis_size("ty")
    pairs = [
        (a * n_y + b, (a + by) * n_y + b + by)
        for a in range(n_x)
        for b in range(n_y)
        if 0 <= a + by < n_x and 0 <= b + by < n_y
    ]
    return lax.ppermute(array, ("tx", "ty"), pairs)


def along_scan(array, dy, dz, dc):
    pairs = []
    for i in range(SCANS):
        y, z, core = i // 4, (i // 2) % 2, i % 2
        pairs.append((i, ((y + dy) % 4) * 4 + ((z + dz) % 2) * 2 + (core + dc) % 2))
    return lax.ppermute(array, "scan", pairs)


def on_device(object_slices, probe_modes, corners, measured):
    me = lax.axis_index("scan").astype(jnp.int32).reshape(1)
    corner = corners.reshape(2)
    rims = run_cut(me, object_slices)
    diag = shift_both(rims[2], -1)
    rims = (shift(rims[0], "tx", -1), shift(rims[1], "ty", -1), diag)
    light, expected, halves = run_glow(probe_modes, measured.reshape(SIDE, SIDE))
    rims, light, expected, halves = lax.optimization_barrier((rims, light, expected, halves))
    others = tuple(along_scan(rim, 0, 0, 1) for rim in rims)

    parts = run_wave(
        corner,
        me,
        object_slices,
        rims + others,
        halves,
        expected,
    )
    parts = lax.all_to_all(parts, "scan", 0, 0)
    own, to_right, to_below, to_diag = run_sum(me, parts, light)
    to_right = shift(to_right, "ty", 1)
    to_below = shift(to_below, "tx", 1)
    to_diag = shift_both(to_diag, 1)
    mine = run_update(me, object_slices, own, to_right, to_below, to_diag)[None]
    pair = jnp.concatenate([mine, along_scan(mine, 0, 1, 0)], axis=0)
    ring = [pair] + [along_scan(pair, dy, 0, 0) for dy in (1, 2, 3)]
    return run_place(me, ring + [along_scan(block, 0, 0, 1) for block in ring])


def solution(mesh):
    placed = (
        P(None, None, "tx", "ty"),
        P(),
        P("tx", "ty", "scan", None),
        P("tx", "ty", "scan", None, None),
    )
    return jax.shard_map(
        on_device, mesh=mesh, in_specs=placed, out_specs=P(None, None, "tx", "ty"), check_vma=False
    )
```

```python
import functools
import math

import jax
import jax.numpy as jnp
import numpy as np
from jax import lax
from jax.experimental import pallas as pl
from jax.experimental.pallas import tpu as pltpu
from jax.sharding import PartitionSpec as P

fresnel_coef = 0.1
step_size = 4.0
SIDE = 256
HALF = 128
LAYERS = 2
SCANS = 16
ROWS = 16
PAD = 8
f32 = jnp.float32
bf16 = jnp.bfloat16


def real_right(table):
    return np.block([[table.real, table.imag], [-table.imag, table.real]])


def real_left(table):
    return np.block([[table.real, -table.imag], [table.imag, table.real]])


def stacked(table, axis):
    high = table.astype(np.float32).astype(bf16)
    low = (table - high.astype(np.float64)).astype(np.float32).astype(bf16)
    return np.concatenate([high, high, low], axis=axis)


def make_tables():
    half = np.arange(HALF)
    col_even = np.exp(-2j * np.pi * np.outer(half, half) / HALF) / 16
    col_odd = np.exp(-2j * np.pi * np.outer(half, 2 * half + 1) / SIDE) / 16
    row_even, row_odd = col_even.T, col_odd.T
    right = [col_even, col_odd, col_even.conj().T, col_odd.conj().T]
    left = [row_even, row_odd, row_even.conj().T, row_odd.conj().T]
    right = np.stack([stacked(real_right(t), 0) for t in right])
    left = np.stack([stacked(real_left(t), 1) for t in left])
    return right, left


def split(value):
    high = value.astype(bf16)
    return high, (value - high.astype(f32)).astype(bf16)


def mul(first, second):
    return jnp.dot(first, second, preferred_element_type=f32)


def put(ref, lead, rows, value):
    high, low = split(value)
    ref[lead + (0, rows)] = high
    ref[lead + (1, rows)] = low


def right_dot(ref, side, table, which):
    high, low = ref[side, 0], ref[side, 1]
    return mul(jnp.concatenate([high, low, high], axis=1), table[which])


def left_dot(table, which, ref, side):
    high, low = ref[side, 0], ref[side, 1]
    return mul(table[which], jnp.concatenate([high, low, high], axis=0))


def neighbours(ref, p, start):
    rows = lambda by: pl.ds(start + PAD + by, ROWS)
    low, high = ref[p, 0, rows(0)], ref[p, 1, rows(0)]
    lane = lax.broadcasted_iota(jnp.int32, low.shape, 1)
    first, last = lane == 0, lane == HALF - 1
    low_up, high_up = pltpu.roll(low, 1, 1), pltpu.roll(high, 1, 1)
    low_down, high_down = pltpu.roll(low, HALF - 1, 1), pltpu.roll(high, HALF - 1, 1)
    low_sum = jnp.where(first, 0.0, low_up) + jnp.where(last, high_down, low_down)
    high_sum = jnp.where(first, low_up, high_up) + jnp.where(last, 0.0, high_down)
    return (
        low_sum + (ref[p, 0, rows(-1)] + ref[p, 0, rows(1)]),
        high_sum + (ref[p, 1, rows(-1)] + ref[p, 1, rows(1)]),
    )


damping = 0.5 * fresnel_coef**2


def turn_rows(source, target, start, sign):
    turn = sign * fresnel_coef
    rows = pl.ds(start + PAD, ROWS)
    near_re, near_im = neighbours(source, 0, start), neighbours(source, 1, start)
    for h in range(2):
        re, im = source[0, h, rows], source[1, h, rows]
        target[0, h, rows] = 4.0 * damping * re - turn * im - damping * near_re[h]
        target[1, h, rows] = 4.0 * damping * im + turn * re - damping * near_im[h]


def end_rows(source, target, start):
    rows = pl.ds(start + PAD, ROWS)
    near = [neighbours(target, p, start) for p in range(2)]
    return [
        [source[p, h, rows] - 4.0 * target[p, h, rows] + near[p][h] for p in range(2)]
        for h in range(2)
    ]


def wave_kernel(
    corner_ref,
    me_ref,
    below_far,
    right_far,
    diag_far,
    other_below_far,
    other_right_far,
    other_diag_far,
    own_far,
    probe,
    measured_far,
    col_far,
    row_far,
    out_ref,
    own_ref,
    measured_ref,
    col_tab,
    row_tab,
    hold,
    trans,
    wave,
    far,
    misfit,
    total,
    more_sems,
    field,
    turned,
    across_0,
    across_1,
    along_0,
    along_1,
    below_ref,
    right_ref,
    diag_ref,
    rim_sems,
):
    across, along = (across_0, across_1), (along_0, along_1)
    r, c = corner_ref[0], corner_ref[1]
    modes = probe.shape[1]
    own_copy = pltpu.make_async_copy(own_far, own_ref, more_sems.at[0])
    later = [
        pltpu.make_async_copy(source, target, more_sems.at[n + 1])
        for n, (source, target) in enumerate(
            [
                (col_far, col_tab),
                (row_far, row_tab),
                (measured_far, measured_ref),
            ]
        )
    ]
    core = lax.rem(me_ref[0], 2)
    rim_copies = [
        pltpu.make_async_copy(
            source, target.at[lax.rem(core + side, 2)], rim_sems.at[side, n]
        )
        for side, sources in enumerate(
            [(below_far, right_far, diag_far), (other_below_far, other_right_far, other_diag_far)]
        )
        for n, (source, target) in enumerate(zip(sources, (below_ref, right_ref, diag_ref)))
    ]
    own_copy.start()
    for copy in rim_copies:
        copy.start()
    for copy in later:
        copy.start()
    rows = lax.broadcasted_iota(jnp.int32, (SIDE, SIDE), 0)
    cols = lax.broadcasted_iota(jnp.int32, (SIDE, SIDE), 1)
    top = rows[:HALF] < r
    near = cols[:, :HALF] < c
    back_c = lax.rem(SIDE - c, SIDE)
    own_copy.wait()
    for copy in rim_copies:
        copy.wait()
    for s in range(LAYERS):
        for p in range(2):
            right, below, diag = right_ref[p, s], below_ref[p, s], diag_ref[p, s]
            left = jnp.where(near, right, own_ref[s, p, :, :HALF])
            whole = jnp.concatenate([left, own_ref[s, p, :, HALF:]], axis=1)
            lower = jnp.concatenate(
                [jnp.where(near[:HALF], diag, below[:, :HALF]), below[:, HALF:]], axis=1
            )
            whole = jnp.concatenate([jnp.where(top, lower, whole[:HALF]), whole[HALF:]], axis=0)
            whole = pltpu.roll(whole, back_c, 1)
            for half in range(2):
                hold[0, half * SIDE : (half + 1) * SIDE] = whole[:, :HALF]
                hold[1, half * SIDE : (half + 1) * SIDE] = whole[:, HALF:]
            for h in range(2):
                view = hold[h, pl.ds(r, SIDE)]
                trans[s, p, h] = view + 1.0 if p == 0 else view

    misfit[...] = jnp.zeros_like(misfit)
    total[...] = jnp.zeros_like(total)
    field[...] = jnp.zeros_like(field)
    turned[...] = jnp.zeros_like(turned)
    starts = range(0, SIDE, ROWS)

    def enter(m, side):
        for start in starts:
            rows, inner = pl.ds(start, ROWS), pl.ds(start + PAD, ROWS)
            for h in range(2):
                p_re, p_im = probe[0, m, h, rows], probe[1, m, h, rows]
                t_re, t_im = trans[0, 0, h, rows], trans[0, 1, h, rows]
                field[side, 0, h, inner] = p_re * t_re - p_im * t_im
                field[side, 1, h, inner] = p_re * t_im + p_im * t_re
            yield
        for start in starts:
            turn_rows(field.at[side], turned, start, 1.0)
            yield
        for start in starts:
            rows = pl.ds(start, ROWS)
            x = []
            for h, (w_re, w_im) in enumerate(end_rows(field.at[side], turned, start)):
                wave[0, m, h, rows] = w_re
                wave[1, m, h, rows] = w_im
                t_re, t_im = trans[1, 0, h, rows], trans[1, 1, h, rows]
                x.append(
                    jnp.concatenate([w_re * t_re - w_im * t_im, w_re * t_im + w_im * t_re], axis=1)
                )
            put(across[side], (0,), rows, x[0] + x[1])
            put(across[side], (1,), rows, x[0] - x[1])
            yield

    def transform(m, side):
        even = right_dot(across[side], 0, col_tab, 0)
        yield
        odd = right_dot(across[side], 1, col_tab, 1)
        yield
        for start in range(0, HALF, ROWS):
            for q in range(2):
                lanes = slice(HALF * q, HALF * (q + 1))
                above, under = [
                    jnp.concatenate([even[part, lanes], odd[part, lanes]], axis=1)
                    for part in (slice(start, start + ROWS), slice(start + HALF, start + HALF + ROWS))
                ]
                rows = pl.ds(HALF * q + start, ROWS)
                put(along[side], (0,), rows, above + under)
                put(along[side], (1,), rows, above - under)
            yield
        for e in range(2):
            found = left_dot(row_tab, e, along[side], e)
            yield
            for start in range(0, HALF, ROWS):
                re, im = found[start : start + ROWS], found[HALF + start : HALF + start + ROWS]
                far[m, e, pl.ds(start, ROWS)] = re
                far[m, e, pl.ds(HALF + start, ROWS)] = im
                misfit[pl.ds(HALF * e + start, ROWS)] += re * re + im * im
                yield
        for start in starts:
            rows = pl.ds(start, ROWS)
            for h in range(2):
                w_re, w_im = wave[0, m, h, rows], wave[1, m, h, rows]
                total[2, h, rows] += w_re * w_re + w_im * w_im
            yield

    def beside(*parts):
        live = list(parts)
        while live:
            live = [part for part in live if next(part, live) is not live]

    beside(enter(0, 0))
    for copy in later:
        copy.wait()

    def forward(j, carry):
        beside(transform(2 * j, 0), enter(2 * j + 1, 1))
        beside(transform(2 * j + 1, 1), enter(2 * j + 2, 0))
        return carry

    lax.fori_loop(0, modes // 2 - 1, forward, 0)
    beside(transform(modes - 2, 0), enter(modes - 1, 1))
    beside(transform(modes - 1, 1))
    misfit[...] = 2.0 * (misfit[...] - measured_ref[...])

    def restore(m, side):
        for e in range(2):
            for start in range(0, HALF, ROWS):
                scale = misfit[pl.ds(HALF * e + start, ROWS)]
                for q in range(2):
                    rows = pl.ds(HALF * q + start, ROWS)
                    put(along[side], (e,), rows, scale * far[m, e, rows])
                yield
        even = left_dot(row_tab, 2, along[side], 0)
        yield
        odd = left_dot(row_tab, 3, along[side], 1)
        yield
        for start in range(0, HALF, ROWS):
            re, im = slice(start, start + ROWS), slice(HALF + start, HALF + start + ROWS)
            for n in range(2):
                f_re = even[re] + odd[re] if n == 0 else even[re] - odd[re]
                f_im = even[im] + odd[im] if n == 0 else even[im] - odd[im]
                rows = pl.ds(HALF * n + start, ROWS)
                for q in range(2):
                    lanes = slice(HALF * q, HALF * (q + 1))
                    put(
                        across[side],
                        (q,),
                        rows,
                        jnp.concatenate([f_re[:, lanes], f_im[:, lanes]], axis=1),
                    )
            yield
        first = right_dot(across[side], 0, col_tab, 2)
        yield
        second = right_dot(across[side], 1, col_tab, 3)
        yield
        for start in starts:
            rows, inner = pl.ds(start, ROWS), pl.ds(start + PAD, ROWS)
            part = slice(start, start + ROWS)
            for h in range(2):
                both = first[part] + second[part] if h == 0 else first[part] - second[part]
                b_re, b_im = both[:, :HALF], both[:, HALF:]
                w_re, w_im = wave[0, m, h, rows], wave[1, m, h, rows]
                total[0, h, rows] += w_re * b_re + w_im * b_im
                total[1, h, rows] += w_re * b_im - w_im * b_re
                t_re, t_im = trans[1, 0, h, rows], trans[1, 1, h, rows]
                field[side, 0, h, inner] = t_re * b_re + t_im * b_im
                field[side, 1, h, inner] = t_re * b_im - t_im * b_re
            yield

    def leave(m, side):
        for start in starts:
            turn_rows(field.at[side], turned, start, -1.0)
            yield
        for start in starts:
            rows = pl.ds(start, ROWS)
            for h, (d_re, d_im) in enumerate(end_rows(field.at[side], turned, start)):
                p_re, p_im = probe[0, m, h, rows], probe[1, m, h, rows]
                total[3, h, rows] += p_re * d_re + p_im * d_im
                total[4, h, rows] += p_re * d_im - p_im * d_re
            yield

    def hand_out(*planes):
        for k in planes:
            for h in range(2):
                hold[h, :SIDE] = total[k, h]
                hold[h, SIDE:] = total[k, h]
                yield
            for n in range(SIDE // 8):
                rows = pl.ds(SIDE - r + 8 * n, 8)
                block = jnp.concatenate([hold[0, rows], hold[1, rows]], axis=1)
                block = pltpu.roll(block, c, 1)
                for h in range(2):
                    out_ref[n % 16, 4 * k + 2 * h + n // 16] = block[:, h * HALF : (h + 1) * HALF]
                if n % 4 == 3:
                    yield

    beside(restore(0, 0))

    def backward(j, carry):
        beside(restore(2 * j + 1, 1), leave(2 * j, 0))
        beside(restore(2 * j + 2, 0), leave(2 * j + 1, 1))
        return carry

    lax.fori_loop(0, modes // 2 - 1, backward, 0)
    beside(restore(modes - 1, 1), leave(modes - 2, 0))
    beside(leave(modes - 1, 1), hand_out(0, 1, 2))
    beside(hand_out(3, 4))

    lane = lax.broadcasted_iota(jnp.int32, (8, HALF), 1)
    mark = jnp.where(lane == 0, r, c).astype(f32)
    for i in range(SCANS):
        out_ref[i, 20] = mark


def glow_kernel(probe_ref, measured_ref, light_ref, expected_ref, halves_ref):
    @pl.when(pl.program_id(0) == 0)
    def _():
        light_ref[...] = jnp.zeros_like(light_ref)
        row = lax.broadcasted_iota(jnp.int32, (SIDE, SIDE), 0)
        col = lax.broadcasted_iota(jnp.int32, (SIDE, SIDE), 1)
        place = lambda k: jnp.where(k < HALF, 2 * k, 2 * (k - HALF) + 1)
        by_col = (row == place(col)).astype(f32).astype(bf16)
        by_row = (col == place(row)).astype(f32).astype(bf16)
        value = measured_ref[...]
        for left in (False, True):
            high, low = split(value)
            rest = (value - high.astype(f32) - low.astype(f32)).astype(bf16)
            if left:
                value = mul(by_row, high) + mul(by_row, low) + mul(by_row, rest)
            else:
                value = mul(high, by_col) + mul(low, by_col) + mul(rest, by_col)
        expected_ref[...] = value

    for p in range(2):
        for h in range(2):
            halves_ref[p, 0, h] = probe_ref[p, 0, :, h * HALF : (h + 1) * HALF]
    light = probe_ref[0, 0] * probe_ref[0, 0] + probe_ref[1, 0] * probe_ref[1, 0]
    light_ref[:SIDE] += light
    light_ref[SIDE:] += light


def run_glow(probe, measured):
    modes = probe.shape[1]
    return pl.pallas_call(
        glow_kernel,
        grid=(modes,),
        out_shape=(
            jax.ShapeDtypeStruct((2 * SIDE, SIDE), f32),
            jax.ShapeDtypeStruct((SIDE, SIDE), f32),
            jax.ShapeDtypeStruct((2, modes, 2, SIDE, HALF), f32),
        ),
        in_specs=[
            pl.BlockSpec((2, 1, SIDE, SIDE), lambda m: (0, m, 0, 0)),
            pl.BlockSpec((SIDE, SIDE), lambda m: (0, 0)),
        ],
        out_specs=(
            pl.BlockSpec((2 * SIDE, SIDE), lambda m: (0, 0)),
            pl.BlockSpec((SIDE, SIDE), lambda m: (0, 0)),
            pl.BlockSpec((2, 1, 2, SIDE, HALF), lambda m: (0, m, 0, 0, 0)),
        ),
        compiler_params=pltpu.CompilerParams(vmem_limit_bytes=10 * 1024 * 1024),
        cost_estimate=pl.CostEstimate(
            flops=4 * modes * SIDE * SIDE, bytes_accessed=8 * modes * SIDE * SIDE, transcendentals=0
        ),
        name="glow",
    )(probe, measured)


def cut_kernel(me_ref, object_ref, below_ref, right_ref, diag_ref, sems):
    core = lax.rem(me_ref[0], 2)
    copies = []
    for s in range(LAYERS):
        plane = object_ref.at[s, core]
        near = pl.ds(0, HALF)
        for n, (source, target) in enumerate(
            [
                (plane.at[near, :], below_ref.at[s]),
                (plane.at[:, near], right_ref.at[s]),
                (plane.at[near, near], diag_ref.at[s]),
            ]
        ):
            copies.append(pltpu.make_async_copy(source, target, sems.at[s, n]))
    for copy in copies:
        copy.start()
    for copy in copies:
        copy.wait()


def run_cut(me, current):
    far = pl.BlockSpec(memory_space=pl.ANY)
    return pl.pallas_call(
        cut_kernel,
        out_shape=(
            jax.ShapeDtypeStruct((LAYERS, HALF, SIDE), f32),
            jax.ShapeDtypeStruct((LAYERS, SIDE, HALF), f32),
            jax.ShapeDtypeStruct((LAYERS, HALF, HALF), f32),
        ),
        in_specs=[pl.BlockSpec(memory_space=pltpu.SMEM), far],
        out_specs=(pl.BlockSpec(memory_space=pltpu.VMEM),) * 3,
        scratch_shapes=[pltpu.SemaphoreType.DMA((LAYERS, 3))],
        compiler_params=pltpu.CompilerParams(vmem_limit_bytes=4 * 1024 * 1024),
        name="cut",
    )(me, current)


def run_wave(corner, me, own, rims, probe, measured):
    right_table, left_table = make_tables()
    modes = probe.shape[1]
    vmem = pl.BlockSpec(memory_space=pltpu.VMEM)
    field = (2, SIDE, HALF)
    wide = (2, 2, SIDE + 2 * PAD, HALF)
    return pl.pallas_call(
        wave_kernel,
        out_shape=jax.ShapeDtypeStruct((SCANS, 21, 8, HALF), f32),
        in_specs=[pl.BlockSpec(memory_space=pltpu.SMEM)] * 2
        + [pl.BlockSpec(memory_space=pl.ANY)] * 7
        + [vmem]
        + [pl.BlockSpec(memory_space=pl.ANY)] * 3,
        out_specs=vmem,
        scratch_shapes=[
            pltpu.VMEM((LAYERS, 2, SIDE, SIDE), f32),
            pltpu.VMEM((SIDE, SIDE), f32),
            pltpu.VMEM((4, 3 * SIDE, SIDE), bf16),
            pltpu.VMEM((4, SIDE, 3 * SIDE), bf16),
            pltpu.VMEM((2, 2 * SIDE, HALF), f32),
            pltpu.VMEM((LAYERS, 2) + field, f32),
            pltpu.VMEM((2, modes) + field, f32),
            pltpu.VMEM((modes, 2, SIDE, SIDE), f32),
            pltpu.VMEM((SIDE, SIDE), f32),
            pltpu.VMEM((5,) + field, f32),
            pltpu.SemaphoreType.DMA((4,)),
            pltpu.VMEM((2,) + wide, f32),
            pltpu.VMEM(wide, f32),
            pltpu.VMEM((2, 2, SIDE, SIDE), bf16),
            pltpu.VMEM((2, 2, SIDE, SIDE), bf16),
            pltpu.VMEM((2, 2, SIDE, SIDE), bf16),
            pltpu.VMEM((2, 2, SIDE, SIDE), bf16),
            pltpu.VMEM((2, LAYERS, HALF, SIDE), f32),
            pltpu.VMEM((2, LAYERS, SIDE, HALF), f32),
            pltpu.VMEM((2, LAYERS, HALF, HALF), f32),
            pltpu.SemaphoreType.DMA((2, 3)),
        ],
        compiler_params=pltpu.CompilerParams(vmem_limit_bytes=36 * 1024 * 1024),
        name="wave",
    )(
        corner,
        me,
        *rims,
        own,
        probe,
        measured,
        jnp.asarray(right_table),
        jnp.asarray(left_table),
    )


def sum_kernel(
    me_ref, parts_ref, light_ref, own_ref, right_ref, below_ref, diag_ref, marks_ref, sem
):
    me = me_ref[0]
    copy = pltpu.make_async_copy(parts_ref.at[:, 20, pl.ds(0, 1)], marks_ref, sem)
    copy.start()
    own_ref[...] = jnp.zeros_like(own_ref)
    right_ref[...] = jnp.zeros_like(right_ref)
    below_ref[...] = jnp.zeros_like(below_ref)
    diag_ref[...] = jnp.zeros_like(diag_ref)
    sub = lax.broadcasted_iota(jnp.int32, (2, 8, SIDE), 1)
    side = lax.broadcasted_iota(jnp.int32, (2, 8, SIDE), 0)
    cols = lax.broadcasted_iota(jnp.int32, (2, 8, SIDE), 2)
    rows = HALF * side + 8 * me + sub
    copy.wait()
    for j in range(SCANS):
        r = marks_ref[j, 0, 0].astype(jnp.int32)
        c = marks_ref[j, 0, 1].astype(jnp.int32)
        lights = []
        for h in range(2):
            start = lax.rem(HALF * h + 8 * me + SIDE - r, SIDE)
            base = pl.multiple_of((start // 8) * 8, 8)
            block = light_ref[pl.ds(base, 16), :]
            block = pltpu.roll(block, lax.rem(16 - (start - base), 16), 0)[:8]
            lights.append(pltpu.roll(block, c, 1)[None])
        light = jnp.concatenate(lights, axis=0)
        inside_row, inside_col = rows >= r, cols >= c
        for k in range(6):
            value = light
            if k < 5:
                halves = [parts_ref[j, 4 * k + 2 * h : 4 * k + 2 * h + 2] for h in range(2)]
                value = jnp.concatenate(halves, axis=2)
            here = jnp.where(inside_row, value, 0.0)
            there = (value - here)[0]
            own_ref[k] += jnp.where(inside_col, here, 0.0)
            right_ref[k] += jnp.where(inside_col, 0.0, here)[:, :, :HALF]
            below_ref[k] += jnp.where(inside_col[0], there, 0.0)
            diag_ref[k] += jnp.where(inside_col[0], 0.0, there)[:, :HALF]


def run_sum(me, parts, light):
    smem = pl.BlockSpec(memory_space=pltpu.SMEM)
    vmem = pl.BlockSpec(memory_space=pltpu.VMEM)
    return pl.pallas_call(
        sum_kernel,
        out_shape=(
            jax.ShapeDtypeStruct((6, 2, 8, SIDE), f32),
            jax.ShapeDtypeStruct((6, 2, 8, HALF), f32),
            jax.ShapeDtypeStruct((6, 8, SIDE), f32),
            jax.ShapeDtypeStruct((6, 8, HALF), f32),
        ),
        in_specs=[smem, vmem, vmem],
        out_specs=(vmem,) * 4,
        scratch_shapes=[pltpu.SMEM((SCANS, 1, HALF), f32), pltpu.SemaphoreType.DMA],
        compiler_params=pltpu.CompilerParams(vmem_limit_bytes=8 * 1024 * 1024),
        name="sum",
    )(me, parts, light)


def update_kernel(me_ref, object_ref, own_ref, right_ref, below_ref, diag_ref, out_ref):
    me = me_ref[0]
    sums = []
    for k in range(6):
        near = own_ref[k, :, :, :HALF] + right_ref[k]
        whole = jnp.concatenate([near, own_ref[k, :, :, HALF:]], axis=2)
        low = jnp.concatenate(
            [below_ref[k, :, :HALF] + diag_ref[k], below_ref[k, :, HALF:]], axis=1
        )
        sums.append([whole[0] + low, whole[1]])
    for s in range(LAYERS):
        base = 3 * (1 - s)
        for h in range(2):
            scale = step_size / (sums[base + 2][h] + 1.0)
            start = pl.multiple_of(HALF * h + 8 * me, 8)
            for p in range(2):
                out_ref[s, p, h] = (
                    object_ref[s, p, pl.ds(start, 8), :] - scale * sums[base + p][h]
                )


def run_update(me, current, own, right, below, diag):
    smem = pl.BlockSpec(memory_space=pltpu.SMEM)
    vmem = pl.BlockSpec(memory_space=pltpu.VMEM)
    return pl.pallas_call(
        update_kernel,
        out_shape=jax.ShapeDtypeStruct((LAYERS, 2, 2, 8, SIDE), f32),
        in_specs=[smem] + [vmem] * 5,
        out_specs=vmem,
        compiler_params=pltpu.CompilerParams(vmem_limit_bytes=4 * 1024 * 1024),
        name="update",
    )(me, current, own, right, below, diag)


def place_kernel(me_ref, *refs):
    blocks, out_ref = refs[:-1], refs[-1]
    me = me_ref[0]
    y, z, core = me // 4, lax.rem(me // 2, 2), lax.rem(me, 2)
    count = 0
    for ref in blocks:
        for b in range(ref.shape[0]):
            dc, dy, dz = count // 8, (count // 2) % 4, count % 2
            i = lax.rem(y + 4 - dy, 4) * 4 + lax.rem(z + dz, 2) * 2 + lax.rem(core + dc, 2)
            for h in range(2):
                start = pl.multiple_of(HALF * h + 8 * i, 8)
                out_ref[:, :, pl.ds(start, 8), :] = ref[b, :, :, h]
            count += 1


def run_place(me, blocks):
    vmem = pl.BlockSpec(memory_space=pltpu.VMEM)
    return pl.pallas_call(
        place_kernel,
        out_shape=jax.ShapeDtypeStruct((LAYERS, 2, SIDE, SIDE), f32),
        in_specs=[pl.BlockSpec(memory_space=pltpu.SMEM)] + [vmem] * len(blocks),
        out_specs=vmem,
        compiler_params=pltpu.CompilerParams(vmem_limit_bytes=8 * 1024 * 1024),
        name="place",
    )(me, *blocks)


def shift(array, axis, by):
    count = lax.axis_size(axis)
    pairs = [(i, i + by) for i in range(count) if 0 <= i + by < count]
    return lax.ppermute(array, axis, pairs)


def shift_both(array, by):
    n_x, n_y = lax.axis_size("tx"), lax.axis_size("ty")
    pairs = [
        (a * n_y + b, (a + by) * n_y + b + by)
        for a in range(n_x)
        for b in range(n_y)
        if 0 <= a + by < n_x and 0 <= b + by < n_y
    ]
    return lax.ppermute(array, ("tx", "ty"), pairs)


def along_scan(array, dy, dz, dc):
    pairs = []
    for i in range(SCANS):
        y, z, core = i // 4, (i // 2) % 2, i % 2
        pairs.append((i, ((y + dy) % 4) * 4 + ((z + dz) % 2) * 2 + (core + dc) % 2))
    return lax.ppermute(array, "scan", pairs)


def on_device(object_slices, probe_modes, corners, measured):
    me = lax.axis_index("scan").astype(jnp.int32).reshape(1)
    corner = corners.reshape(2)
    rims = run_cut(me, object_slices)
    diag = shift_both(rims[2], -1)
    rims = (shift(rims[0], "tx", -1), shift(rims[1], "ty", -1), diag)
    light, expected, halves = run_glow(probe_modes, measured.reshape(SIDE, SIDE))
    rims, light, expected, halves = lax.optimization_barrier((rims, light, expected, halves))
    others = tuple(along_scan(rim, 0, 0, 1) for rim in rims)

    parts = run_wave(
        corner,
        me,
        object_slices,
        rims + others,
        halves,
        expected,
    )
    parts = lax.all_to_all(parts, "scan", 0, 0)
    own, to_right, to_below, to_diag = run_sum(me, parts, light)
    to_right = shift(to_right, "ty", 1)
    to_below = shift(to_below, "tx", 1)
    to_diag = shift_both(to_diag, 1)
    mine = run_update(me, object_slices, own, to_right, to_below, to_diag)[None]
    pair = jnp.concatenate([mine, along_scan(mine, 0, 1, 0)], axis=0)
    ring = [pair] + [along_scan(pair, dy, 0, 0) for dy in (1, 2, 3)]
    return run_place(me, ring + [along_scan(block, 0, 0, 1) for block in ring])


def solution(mesh):
    placed = (
        P(None, None, "tx", "ty"),
        P(),
        P("tx", "ty", "scan", None),
        P("tx", "ty", "scan", None, None),
    )
    return jax.shard_map(
        on_device, mesh=mesh, in_specs=placed, out_specs=P(None, None, "tx", "ty"), check_vma=False
    )
```

```python
import functools
import math

import jax
import jax.numpy as jnp
import numpy as np
from jax import lax
from jax.experimental import pallas as pl
from jax.experimental.pallas import tpu as pltpu
from jax.sharding import PartitionSpec as P

fresnel_coef = 0.1
step_size = 4.0
SIDE = 256
HALF = 128
LAYERS = 2
SCANS = 16
ROWS = 16
PAD = 8
f32 = jnp.float32
bf16 = jnp.bfloat16


def real_right(table):
    return np.block([[table.real, table.imag], [-table.imag, table.real]])


def real_left(table):
    return np.block([[table.real, -table.imag], [table.imag, table.real]])


def stacked(table, axis):
    high = table.astype(np.float32).astype(bf16)
    low = (table - high.astype(np.float64)).astype(np.float32).astype(bf16)
    return np.concatenate([high, high, low], axis=axis)


def make_tables():
    half = np.arange(HALF)
    col_even = np.exp(-2j * np.pi * np.outer(half, half) / HALF) / 16
    col_odd = np.exp(-2j * np.pi * np.outer(half, 2 * half + 1) / SIDE) / 16
    row_even, row_odd = col_even.T, col_odd.T
    right = [col_even, col_odd, col_even.conj().T, col_odd.conj().T]
    left = [row_even, row_odd, row_even.conj().T, row_odd.conj().T]
    right = np.stack([stacked(real_right(t), 0) for t in right])
    left = np.stack([stacked(real_left(t), 1) for t in left])
    return right, left


def split(value):
    high = value.astype(bf16)
    return high, (value - high.astype(f32)).astype(bf16)


def mul(first, second):
    return jnp.dot(first, second, preferred_element_type=f32)


def put(ref, lead, rows, value):
    high, low = split(value)
    ref[lead + (0, rows)] = high
    ref[lead + (1, rows)] = low


def right_dot(ref, side, table, which):
    high, low = ref[side, 0], ref[side, 1]
    return mul(jnp.concatenate([high, low, high], axis=1), table[which])


def left_dot(table, which, ref, side):
    high, low = ref[side, 0], ref[side, 1]
    return mul(table[which], jnp.concatenate([high, low, high], axis=0))


def neighbours(ref, p, start):
    rows = lambda by: pl.ds(start + PAD + by, ROWS)
    low, high = ref[p, 0, rows(0)], ref[p, 1, rows(0)]
    lane = lax.broadcasted_iota(jnp.int32, low.shape, 1)
    first, last = lane == 0, lane == HALF - 1
    low_up, high_up = pltpu.roll(low, 1, 1), pltpu.roll(high, 1, 1)
    low_down, high_down = pltpu.roll(low, HALF - 1, 1), pltpu.roll(high, HALF - 1, 1)
    low_sum = jnp.where(first, 0.0, low_up) + jnp.where(last, high_down, low_down)
    high_sum = jnp.where(first, low_up, high_up) + jnp.where(last, 0.0, high_down)
    return (
        low_sum + (ref[p, 0, rows(-1)] + ref[p, 0, rows(1)]),
        high_sum + (ref[p, 1, rows(-1)] + ref[p, 1, rows(1)]),
    )


damping = 0.5 * fresnel_coef**2


def turn_rows(source, target, start, sign):
    turn = sign * fresnel_coef
    rows = pl.ds(start + PAD, ROWS)
    near_re, near_im = neighbours(source, 0, start), neighbours(source, 1, start)
    for h in range(2):
        re, im = source[0, h, rows], source[1, h, rows]
        target[0, h, rows] = 4.0 * damping * re - turn * im - damping * near_re[h]
        target[1, h, rows] = 4.0 * damping * im + turn * re - damping * near_im[h]


def end_rows(source, target, start):
    rows = pl.ds(start + PAD, ROWS)
    near = [neighbours(target, p, start) for p in range(2)]
    return [
        [source[p, h, rows] - 4.0 * target[p, h, rows] + near[p][h] for p in range(2)]
        for h in range(2)
    ]


def wave_kernel(
    corner_ref,
    me_ref,
    below_far,
    right_far,
    diag_far,
    other_below_far,
    other_right_far,
    other_diag_far,
    own_far,
    probe,
    measured_far,
    col_far,
    row_far,
    out_ref,
    own_ref,
    measured_ref,
    col_tab,
    row_tab,
    hold,
    trans,
    wave,
    far,
    misfit,
    total,
    more_sems,
    field,
    turned,
    across_0,
    across_1,
    along_0,
    along_1,
    below_ref,
    right_ref,
    diag_ref,
    rim_sems,
):
    across, along = (across_0, across_1), (along_0, along_1)
    r, c = corner_ref[0], corner_ref[1]
    modes = probe.shape[1]
    own_copy = pltpu.make_async_copy(own_far, own_ref, more_sems.at[0])
    later = [
        pltpu.make_async_copy(source, target, more_sems.at[n + 1])
        for n, (source, target) in enumerate(
            [
                (col_far, col_tab),
                (row_far, row_tab),
                (measured_far, measured_ref),
            ]
        )
    ]
    core = lax.rem(me_ref[0], 2)
    rim_copies = [
        pltpu.make_async_copy(
            source, target.at[lax.rem(core + side, 2)], rim_sems.at[side, n]
        )
        for side, sources in enumerate(
            [(below_far, right_far, diag_far), (other_below_far, other_right_far, other_diag_far)]
        )
        for n, (source, target) in enumerate(zip(sources, (below_ref, right_ref, diag_ref)))
    ]
    own_copy.start()
    for copy in rim_copies:
        copy.start()
    for copy in later:
        copy.start()
    rows = lax.broadcasted_iota(jnp.int32, (SIDE, SIDE), 0)
    cols = lax.broadcasted_iota(jnp.int32, (SIDE, SIDE), 1)
    top = rows[:HALF] < r
    near = cols[:, :HALF] < c
    back_c = lax.rem(SIDE - c, SIDE)
    own_copy.wait()
    for copy in rim_copies:
        copy.wait()
    for s in range(LAYERS):
        for p in range(2):
            right, below, diag = right_ref[p, s], below_ref[p, s], diag_ref[p, s]
            left = jnp.where(near, right, own_ref[s, p, :, :HALF])
            whole = jnp.concatenate([left, own_ref[s, p, :, HALF:]], axis=1)
            lower = jnp.concatenate(
                [jnp.where(near[:HALF], diag, below[:, :HALF]), below[:, HALF:]], axis=1
            )
            whole = jnp.concatenate([jnp.where(top, lower, whole[:HALF]), whole[HALF:]], axis=0)
            whole = pltpu.roll(whole, back_c, 1)
            for half in range(2):
                hold[0, half * SIDE : (half + 1) * SIDE] = whole[:, :HALF]
                hold[1, half * SIDE : (half + 1) * SIDE] = whole[:, HALF:]
            for h in range(2):
                view = hold[h, pl.ds(r, SIDE)]
                trans[s, p, h] = view + 1.0 if p == 0 else view

    misfit[...] = jnp.zeros_like(misfit)
    total[...] = jnp.zeros_like(total)
    field[...] = jnp.zeros_like(field)
    turned[...] = jnp.zeros_like(turned)
    starts = range(0, SIDE, ROWS)

    def enter(m, side):
        for start in starts:
            rows, inner = pl.ds(start, ROWS), pl.ds(start + PAD, ROWS)
            for h in range(2):
                p_re, p_im = probe[0, m, h, rows], probe[1, m, h, rows]
                t_re, t_im = trans[0, 0, h, rows], trans[0, 1, h, rows]
                field[side, 0, h, inner] = p_re * t_re - p_im * t_im
                field[side, 1, h, inner] = p_re * t_im + p_im * t_re
            yield
        for start in starts:
            turn_rows(field.at[side], turned, start, 1.0)
            yield
        for start in starts:
            rows = pl.ds(start, ROWS)
            x = []
            for h, (w_re, w_im) in enumerate(end_rows(field.at[side], turned, start)):
                wave[0, m, h, rows] = w_re
                wave[1, m, h, rows] = w_im
                t_re, t_im = trans[1, 0, h, rows], trans[1, 1, h, rows]
                x.append(
                    jnp.concatenate([w_re * t_re - w_im * t_im, w_re * t_im + w_im * t_re], axis=1)
                )
            put(across[side], (0,), rows, x[0] + x[1])
            put(across[side], (1,), rows, x[0] - x[1])
            yield

    def transform(m, side):
        even = right_dot(across[side], 0, col_tab, 0)
        yield
        odd = right_dot(across[side], 1, col_tab, 1)
        yield
        for start in range(0, HALF, ROWS):
            for q in range(2):
                lanes = slice(HALF * q, HALF * (q + 1))
                above, under = [
                    jnp.concatenate([even[part, lanes], odd[part, lanes]], axis=1)
                    for part in (slice(start, start + ROWS), slice(start + HALF, start + HALF + ROWS))
                ]
                rows = pl.ds(HALF * q + start, ROWS)
                put(along[side], (0,), rows, above + under)
                put(along[side], (1,), rows, above - under)
            yield
        for e in range(2):
            found = left_dot(row_tab, e, along[side], e)
            yield
            for start in range(0, HALF, ROWS):
                re, im = found[start : start + ROWS], found[HALF + start : HALF + start + ROWS]
                far[m, e, pl.ds(start, ROWS)] = re
                far[m, e, pl.ds(HALF + start, ROWS)] = im
                misfit[pl.ds(HALF * e + start, ROWS)] += re * re + im * im
                yield
        for start in starts:
            rows = pl.ds(start, ROWS)
            for h in range(2):
                w_re, w_im = wave[0, m, h, rows], wave[1, m, h, rows]
                total[2, h, rows] += w_re * w_re + w_im * w_im
            yield

    def beside(*parts):
        live = list(parts)
        while live:
            live = [part for part in live if next(part, live) is not live]

    beside(enter(0, 0))
    for copy in later:
        copy.wait()

    def forward(j, carry):
        beside(transform(2 * j, 0), enter(2 * j + 1, 1))
        beside(transform(2 * j + 1, 1), enter(2 * j + 2, 0))
        return carry

    lax.fori_loop(0, modes // 2 - 1, forward, 0)
    beside(transform(modes - 2, 0), enter(modes - 1, 1))
    beside(transform(modes - 1, 1))
    misfit[...] = 2.0 * (misfit[...] - measured_ref[...])

    def restore(m, side):
        for e in range(2):
            for start in range(0, HALF, ROWS):
                scale = misfit[pl.ds(HALF * e + start, ROWS)]
                for q in range(2):
                    rows = pl.ds(HALF * q + start, ROWS)
                    put(along[side], (e,), rows, scale * far[m, e, rows])
                yield
        even = left_dot(row_tab, 2, along[side], 0)
        yield
        odd = left_dot(row_tab, 3, along[side], 1)
        yield
        for start in range(0, HALF, ROWS):
            re, im = slice(start, start + ROWS), slice(HALF + start, HALF + start + ROWS)
            for n in range(2):
                f_re = even[re] + odd[re] if n == 0 else even[re] - odd[re]
                f_im = even[im] + odd[im] if n == 0 else even[im] - odd[im]
                rows = pl.ds(HALF * n + start, ROWS)
                for q in range(2):
                    lanes = slice(HALF * q, HALF * (q + 1))
                    put(
                        across[side],
                        (q,),
                        rows,
                        jnp.concatenate([f_re[:, lanes], f_im[:, lanes]], axis=1),
                    )
            yield
        first = right_dot(across[side], 0, col_tab, 2)
        yield
        second = right_dot(across[side], 1, col_tab, 3)
        yield
        for start in starts:
            rows, inner = pl.ds(start, ROWS), pl.ds(start + PAD, ROWS)
            part = slice(start, start + ROWS)
            for h in range(2):
                both = first[part] + second[part] if h == 0 else first[part] - second[part]
                b_re, b_im = both[:, :HALF], both[:, HALF:]
                w_re, w_im = wave[0, m, h, rows], wave[1, m, h, rows]
                total[0, h, rows] += w_re * b_re + w_im * b_im
                total[1, h, rows] += w_re * b_im - w_im * b_re
                t_re, t_im = trans[1, 0, h, rows], trans[1, 1, h, rows]
                field[side, 0, h, inner] = t_re * b_re + t_im * b_im
                field[side, 1, h, inner] = t_re * b_im - t_im * b_re
            yield

    def leave(m, side):
        for start in starts:
            turn_rows(field.at[side], turned, start, -1.0)
            yield
        for start in starts:
            rows = pl.ds(start, ROWS)
            for h, (d_re, d_im) in enumerate(end_rows(field.at[side], turned, start)):
                p_re, p_im = probe[0, m, h, rows], probe[1, m, h, rows]
                total[3, h, rows] += p_re * d_re + p_im * d_im
                total[4, h, rows] += p_re * d_im - p_im * d_re
            yield

    def hand_out(*planes):
        for k in planes:
            for h in range(2):
                hold[h, :SIDE] = total[k, h]
                hold[h, SIDE:] = total[k, h]
                yield
            for n in range(SIDE // 8):
                rows = pl.ds(SIDE - r + 8 * n, 8)
                block = jnp.concatenate([hold[0, rows], hold[1, rows]], axis=1)
                block = pltpu.roll(block, c, 1)
                for h in range(2):
                    out_ref[n % 16, 4 * k + 2 * h + n // 16] = block[:, h * HALF : (h + 1) * HALF]
                if n % 4 == 3:
                    yield

    beside(restore(0, 0))

    def backward(j, carry):
        beside(restore(2 * j + 1, 1), leave(2 * j, 0))
        beside(restore(2 * j + 2, 0), leave(2 * j + 1, 1))
        return carry

    lax.fori_loop(0, modes // 2 - 1, backward, 0)
    beside(restore(modes - 1, 1), leave(modes - 2, 0))
    beside(leave(modes - 1, 1), hand_out(0, 1, 2))
    beside(hand_out(3, 4))

    lane = lax.broadcasted_iota(jnp.int32, (8, HALF), 1)
    mark = jnp.where(lane == 0, r, c).astype(f32)
    for i in range(SCANS):
        out_ref[i, 20] = mark


def glow_kernel(probe_ref, measured_ref, light_ref, expected_ref, halves_ref):
    @pl.when(pl.program_id(0) == 0)
    def _():
        light_ref[...] = jnp.zeros_like(light_ref)
        row = lax.broadcasted_iota(jnp.int32, (SIDE, SIDE), 0)
        col = lax.broadcasted_iota(jnp.int32, (SIDE, SIDE), 1)
        place = lambda k: jnp.where(k < HALF, 2 * k, 2 * (k - HALF) + 1)
        by_col = (row == place(col)).astype(f32).astype(bf16)
        by_row = (col == place(row)).astype(f32).astype(bf16)
        value = measured_ref[...]
        for left in (False, True):
            high, low = split(value)
            rest = (value - high.astype(f32) - low.astype(f32)).astype(bf16)
            if left:
                value = mul(by_row, high) + mul(by_row, low) + mul(by_row, rest)
            else:
                value = mul(high, by_col) + mul(low, by_col) + mul(rest, by_col)
        expected_ref[...] = value

    for p in range(2):
        for h in range(2):
            halves_ref[p, 0, h] = probe_ref[p, 0, :, h * HALF : (h + 1) * HALF]
    light = probe_ref[0, 0] * probe_ref[0, 0] + probe_ref[1, 0] * probe_ref[1, 0]
    light_ref[:SIDE] += light
    light_ref[SIDE:] += light


def run_glow(probe, measured):
    modes = probe.shape[1]
    return pl.pallas_call(
        glow_kernel,
        grid=(modes,),
        out_shape=(
            jax.ShapeDtypeStruct((2 * SIDE, SIDE), f32),
            jax.ShapeDtypeStruct((SIDE, SIDE), f32),
            jax.ShapeDtypeStruct((2, modes, 2, SIDE, HALF), f32),
        ),
        in_specs=[
            pl.BlockSpec((2, 1, SIDE, SIDE), lambda m: (0, m, 0, 0)),
            pl.BlockSpec((SIDE, SIDE), lambda m: (0, 0)),
        ],
        out_specs=(
            pl.BlockSpec((2 * SIDE, SIDE), lambda m: (0, 0)),
            pl.BlockSpec((SIDE, SIDE), lambda m: (0, 0)),
            pl.BlockSpec((2, 1, 2, SIDE, HALF), lambda m: (0, m, 0, 0, 0)),
        ),
        compiler_params=pltpu.CompilerParams(vmem_limit_bytes=10 * 1024 * 1024),
        cost_estimate=pl.CostEstimate(
            flops=4 * modes * SIDE * SIDE, bytes_accessed=8 * modes * SIDE * SIDE, transcendentals=0
        ),
        name="glow",
    )(probe, measured)


def cut_kernel(me_ref, object_ref, below_ref, right_ref, diag_ref, sems):
    core = lax.rem(me_ref[0], 2)
    copies = []
    for s in range(LAYERS):
        plane = object_ref.at[s, core]
        near = pl.ds(0, HALF)
        for n, (source, target) in enumerate(
            [
                (plane.at[near, :], below_ref.at[s]),
                (plane.at[:, near], right_ref.at[s]),
                (plane.at[near, near], diag_ref.at[s]),
            ]
        ):
            copies.append(pltpu.make_async_copy(source, target, sems.at[s, n]))
    for copy in copies:
        copy.start()
    for copy in copies:
        copy.wait()


def run_cut(me, current):
    far = pl.BlockSpec(memory_space=pl.ANY)
    return pl.pallas_call(
        cut_kernel,
        out_shape=(
            jax.ShapeDtypeStruct((LAYERS, HALF, SIDE), f32),
            jax.ShapeDtypeStruct((LAYERS, SIDE, HALF), f32),
            jax.ShapeDtypeStruct((LAYERS, HALF, HALF), f32),
        ),
        in_specs=[pl.BlockSpec(memory_space=pltpu.SMEM), far],
        out_specs=(pl.BlockSpec(memory_space=pltpu.VMEM),) * 3,
        scratch_shapes=[pltpu.SemaphoreType.DMA((LAYERS, 3))],
        compiler_params=pltpu.CompilerParams(vmem_limit_bytes=4 * 1024 * 1024),
        name="cut",
    )(me, current)


def run_wave(corner, me, own, rims, probe, measured):
    right_table, left_table = make_tables()
    modes = probe.shape[1]
    vmem = pl.BlockSpec(memory_space=pltpu.VMEM)
    field = (2, SIDE, HALF)
    wide = (2, 2, SIDE + 2 * PAD, HALF)
    return pl.pallas_call(
        wave_kernel,
        out_shape=jax.ShapeDtypeStruct((SCANS, 21, 8, HALF), f32),
        in_specs=[pl.BlockSpec(memory_space=pltpu.SMEM)] * 2
        + [pl.BlockSpec(memory_space=pl.ANY)] * 7
        + [vmem]
        + [pl.BlockSpec(memory_space=pl.ANY)] * 3,
        out_specs=vmem,
        scratch_shapes=[
            pltpu.VMEM((LAYERS, 2, SIDE, SIDE), f32),
            pltpu.VMEM((SIDE, SIDE), f32),
            pltpu.VMEM((4, 3 * SIDE, SIDE), bf16),
            pltpu.VMEM((4, SIDE, 3 * SIDE), bf16),
            pltpu.VMEM((2, 2 * SIDE, HALF), f32),
            pltpu.VMEM((LAYERS, 2) + field, f32),
            pltpu.VMEM((2, modes) + field, f32),
            pltpu.VMEM((modes, 2, SIDE, SIDE), f32),
            pltpu.VMEM((SIDE, SIDE), f32),
            pltpu.VMEM((5,) + field, f32),
            pltpu.SemaphoreType.DMA((4,)),
            pltpu.VMEM((2,) + wide, f32),
            pltpu.VMEM(wide, f32),
            pltpu.VMEM((2, 2, SIDE, SIDE), bf16),
            pltpu.VMEM((2, 2, SIDE, SIDE), bf16),
            pltpu.VMEM((2, 2, SIDE, SIDE), bf16),
            pltpu.VMEM((2, 2, SIDE, SIDE), bf16),
            pltpu.VMEM((2, LAYERS, HALF, SIDE), f32),
            pltpu.VMEM((2, LAYERS, SIDE, HALF), f32),
            pltpu.VMEM((2, LAYERS, HALF, HALF), f32),
            pltpu.SemaphoreType.DMA((2, 3)),
        ],
        compiler_params=pltpu.CompilerParams(vmem_limit_bytes=36 * 1024 * 1024),
        name="wave",
    )(
        corner,
        me,
        *rims,
        own,
        probe,
        measured,
        jnp.asarray(right_table),
        jnp.asarray(left_table),
    )


def sum_kernel(
    me_ref, parts_ref, light_ref, own_ref, right_ref, below_ref, diag_ref, marks_ref, sem
):
    me = me_ref[0]
    copy = pltpu.make_async_copy(parts_ref.at[:, 20, pl.ds(0, 1)], marks_ref, sem)
    copy.start()
    targets = (own_ref, right_ref, below_ref, diag_ref)
    sums = [[jnp.zeros(ref.shape[1:], f32) for ref in targets] for _ in range(6)]
    sub = lax.broadcasted_iota(jnp.int32, (2, 8, SIDE), 1)
    side = lax.broadcasted_iota(jnp.int32, (2, 8, SIDE), 0)
    cols = lax.broadcasted_iota(jnp.int32, (2, 8, SIDE), 2)
    rows = HALF * side + 8 * me + sub
    copy.wait()
    for j in range(SCANS):
        r = marks_ref[j, 0, 0].astype(jnp.int32)
        c = marks_ref[j, 0, 1].astype(jnp.int32)
        lights = []
        for h in range(2):
            start = lax.rem(HALF * h + 8 * me + SIDE - r, SIDE)
            base = pl.multiple_of((start // 8) * 8, 8)
            block = light_ref[pl.ds(base, 16), :]
            block = pltpu.roll(block, lax.rem(16 - (start - base), 16), 0)[:8]
            lights.append(pltpu.roll(block, c, 1)[None])
        light = jnp.concatenate(lights, axis=0)
        inside_row, inside_col = rows >= r, cols >= c
        for k in range(6):
            value = light
            if k < 5:
                halves = [parts_ref[j, 4 * k + 2 * h : 4 * k + 2 * h + 2] for h in range(2)]
                value = jnp.concatenate(halves, axis=2)
            here = jnp.where(inside_row, value, 0.0)
            there = (value - here)[0]
            sums[k][0] += jnp.where(inside_col, here, 0.0)
            sums[k][1] += jnp.where(inside_col, 0.0, here)[:, :, :HALF]
            sums[k][2] += jnp.where(inside_col[0], there, 0.0)
            sums[k][3] += jnp.where(inside_col[0], 0.0, there)[:, :HALF]
    for k in range(6):
        for ref, value in zip(targets, sums[k]):
            ref[k] = value


def run_sum(me, parts, light):
    smem = pl.BlockSpec(memory_space=pltpu.SMEM)
    vmem = pl.BlockSpec(memory_space=pltpu.VMEM)
    return pl.pallas_call(
        sum_kernel,
        out_shape=(
            jax.ShapeDtypeStruct((6, 2, 8, SIDE), f32),
            jax.ShapeDtypeStruct((6, 2, 8, HALF), f32),
            jax.ShapeDtypeStruct((6, 8, SIDE), f32),
            jax.ShapeDtypeStruct((6, 8, HALF), f32),
        ),
        in_specs=[smem, vmem, vmem],
        out_specs=(vmem,) * 4,
        scratch_shapes=[pltpu.SMEM((SCANS, 1, HALF), f32), pltpu.SemaphoreType.DMA],
        compiler_params=pltpu.CompilerParams(vmem_limit_bytes=8 * 1024 * 1024),
        name="sum",
    )(me, parts, light)


def update_kernel(me_ref, object_ref, own_ref, right_ref, below_ref, diag_ref, out_ref):
    me = me_ref[0]
    sums = []
    for k in range(6):
        near = own_ref[k, :, :, :HALF] + right_ref[k]
        whole = jnp.concatenate([near, own_ref[k, :, :, HALF:]], axis=2)
        low = jnp.concatenate(
            [below_ref[k, :, :HALF] + diag_ref[k], below_ref[k, :, HALF:]], axis=1
        )
        sums.append([whole[0] + low, whole[1]])
    for s in range(LAYERS):
        base = 3 * (1 - s)
        for h in range(2):
            scale = step_size / (sums[base + 2][h] + 1.0)
            start = pl.multiple_of(HALF * h + 8 * me, 8)
            for p in range(2):
                out_ref[s, p, h] = (
                    object_ref[s, p, pl.ds(start, 8), :] - scale * sums[base + p][h]
                )


def run_update(me, current, own, right, below, diag):
    smem = pl.BlockSpec(memory_space=pltpu.SMEM)
    vmem = pl.BlockSpec(memory_space=pltpu.VMEM)
    return pl.pallas_call(
        update_kernel,
        out_shape=jax.ShapeDtypeStruct((LAYERS, 2, 2, 8, SIDE), f32),
        in_specs=[smem] + [vmem] * 5,
        out_specs=vmem,
        compiler_params=pltpu.CompilerParams(vmem_limit_bytes=4 * 1024 * 1024),
        name="update",
    )(me, current, own, right, below, diag)


def place_kernel(me_ref, *refs):
    blocks, out_ref = refs[:-1], refs[-1]
    me = me_ref[0]
    y, z, core = me // 4, lax.rem(me // 2, 2), lax.rem(me, 2)
    count = 0
    for ref in blocks:
        for b in range(ref.shape[0]):
            dc, dy, dz = count // 8, (count // 2) % 4, count % 2
            i = lax.rem(y + 4 - dy, 4) * 4 + lax.rem(z + dz, 2) * 2 + lax.rem(core + dc, 2)
            for h in range(2):
                start = pl.multiple_of(HALF * h + 8 * i, 8)
                out_ref[:, :, pl.ds(start, 8), :] = ref[b, :, :, h]
            count += 1


def run_place(me, blocks):
    vmem = pl.BlockSpec(memory_space=pltpu.VMEM)
    return pl.pallas_call(
        place_kernel,
        out_shape=jax.ShapeDtypeStruct((LAYERS, 2, SIDE, SIDE), f32),
        in_specs=[pl.BlockSpec(memory_space=pltpu.SMEM)] + [vmem] * len(blocks),
        out_specs=vmem,
        compiler_params=pltpu.CompilerParams(vmem_limit_bytes=8 * 1024 * 1024),
        name="place",
    )(me, *blocks)


def shift(array, axis, by):
    count = lax.axis_size(axis)
    pairs = [(i, i + by) for i in range(count) if 0 <= i + by < count]
    return lax.ppermute(array, axis, pairs)


def shift_both(array, by):
    n_x, n_y = lax.axis_size("tx"), lax.axis_size("ty")
    pairs = [
        (a * n_y + b, (a + by) * n_y + b + by)
        for a in range(n_x)
        for b in range(n_y)
        if 0 <= a + by < n_x and 0 <= b + by < n_y
    ]
    return lax.ppermute(array, ("tx", "ty"), pairs)


def along_scan(array, dy, dz, dc):
    pairs = []
    for i in range(SCANS):
        y, z, core = i // 4, (i // 2) % 2, i % 2
        pairs.append((i, ((y + dy) % 4) * 4 + ((z + dz) % 2) * 2 + (core + dc) % 2))
    return lax.ppermute(array, "scan", pairs)


def on_device(object_slices, probe_modes, corners, measured):
    me = lax.axis_index("scan").astype(jnp.int32).reshape(1)
    corner = corners.reshape(2)
    rims = run_cut(me, object_slices)
    diag = shift_both(rims[2], -1)
    rims = (shift(rims[0], "tx", -1), shift(rims[1], "ty", -1), diag)
    light, expected, halves = run_glow(probe_modes, measured.reshape(SIDE, SIDE))
    rims, light, expected, halves = lax.optimization_barrier((rims, light, expected, halves))
    others = tuple(along_scan(rim, 0, 0, 1) for rim in rims)

    parts = run_wave(
        corner,
        me,
        object_slices,
        rims + others,
        halves,
        expected,
    )
    parts = lax.all_to_all(parts, "scan", 0, 0)
    own, to_right, to_below, to_diag = run_sum(me, parts, light)
    to_right = shift(to_right, "ty", 1)
    to_below = shift(to_below, "tx", 1)
    to_diag = shift_both(to_diag, 1)
    mine = run_update(me, object_slices, own, to_right, to_below, to_diag)[None]
    pair = jnp.concatenate([mine, along_scan(mine, 0, 1, 0)], axis=0)
    ring = [pair] + [along_scan(pair, dy, 0, 0) for dy in (1, 2, 3)]
    return run_place(me, ring + [along_scan(block, 0, 0, 1) for block in ring])


def solution(mesh):
    placed = (
        P(None, None, "tx", "ty"),
        P(),
        P("tx", "ty", "scan", None),
        P("tx", "ty", "scan", None, None),
    )
    return jax.shard_map(
        on_device, mesh=mesh, in_specs=placed, out_specs=P(None, None, "tx", "ty"), check_vma=False
    )
```
